32 devices in a mesh: ctx: 16 (over z, y, core), tp: 2 (over x).
Axes of the slice: x: 2, y: 2, z: 4, core: 2. Of those that a mesh axis runs over, the one named last changes fastest.
Arguments:
- queries: bfloat16 [2048, 8192], P('ctx', 'tp'), may hold values from -8 to 8
- keys: bfloat16 [2048, 1024], P('ctx', 'tp'), may hold values from -4 to 4
- values: bfloat16 [2048, 1024], P('ctx', 'tp'), may hold values from -4 to 4
- attn_out: bfloat16 [2048, 8192], P('ctx', 'tp'), may hold values from -4 to 4, as said below
- out_grad: bfloat16 [2048, 8192], P(('ctx', 'tp')), may hold values from -24 to 24
- logsumexp: float32 [64, 2048], P('tp', 'ctx'), may hold values from -50 to 50, as said below
- position_ids: int32 [3, 2048], P(None, 'ctx'), may hold values from 0 to 2047, as said below
- block_map: int32 [32], replicated, may hold values from 0 to 31, as said below
- span_blocks: int32 [4, 2], replicated, may hold values from 0 to 31, as said below
Outputs:
- grad_q: bfloat16 [2048, 8192], P('ctx', 'tp')
- key_gradient: bfloat16 [2048, 1024], P('ctx', 'tp')
- value_gradient: bfloat16 [2048, 1024], P('ctx', 'tp')
The draws below stay inside these ranges and needn't reach their ends.
Inputs may be any that keep to these rules, and one draw needn't show every extreme that they name: `block_map`: a permutation of the sequence blocks. `span_blocks`: spans ascend in sequence order and do not intersect; each row is a start block and an end block past the span's last; the first span starts at block 0 and the last ends at block 31. `position_ids`: given inputs, not renumbered after spans: text rows carry their sequence position in all three ids; a row of a visual span carries the span's first position plus its frame, grid row and grid column. `attn_out`: the output of the forward pass for these queries, keys and values. `logsumexp`: the log of each row's softmax total over its allowed keys, from the forward pass.
All inputs are finite; a program needn't handle non-finite values.
Results may differ from the reference program's by a relative error of at most 0.011.
Values may be sent and summed in bfloat16 or wider, within the bound.
No kernel may reach another device: no remote copies, remote signals or barrier semaphores. Data moves between devices by JAX's collectives and lax.ppermute only.
A program may use at most 64 MiB of HBM per device.

```python
import math
import jax
import jax.numpy as jnp
from jax import lax

QUERY_HEADS = 64
KEY_VALUE_HEADS = 8
HEAD_SIZE = 128
BLK = 64
NBLK = 32
SEQUENCE_TOKENS = 2048
SPANS = 4


THETA = 1000000.0


def layout_ints(key):
    permuted = jax.random.permutation(jax.random.fold_in(key, 101), NBLK).astype(jnp.int32)
    segment = NBLK // SPANS
    offsets = jax.random.randint(jax.random.fold_in(key, 102), (SPANS,), 0, 4).astype(jnp.int32)
    offsets = offsets.at[0].set(0)
    raw_bits = jax.random.randint(jax.random.fold_in(key, 103), (SPANS,), 0, 1 << 20).astype(jnp.int32)
    room_left = segment - offsets
    lengths = 1 + raw_bits % (room_left - 1)
    lengths = lengths.at[SPANS - 1].set(room_left[SPANS - 1] - 1)
    starts = jnp.arange(SPANS, dtype=jnp.int32) * segment + offsets
    return (permuted, starts, starts + lengths)


def row_info(key):
    permuted, starts, ends = layout_ints(key)
    row_index = jnp.arange(SEQUENCE_TOKENS, dtype=jnp.int32)
    seq_pos = permuted[row_index // BLK] * BLK + row_index % BLK
    seq_block = seq_pos // BLK
    inside = (seq_block[:, None] >= starts[None, :]) & (seq_block[:, None] < ends[None, :])
    numbers = jnp.arange(SPANS, dtype=jnp.int32)[None, :] + 1
    span_ids = jnp.sum(jnp.where(inside, numbers, 0), axis=1).astype(jnp.int32) - 1
    span_start = jnp.sum(jnp.where(inside, starts[None, :], 0), axis=1).astype(jnp.int32)
    return (seq_pos, span_ids, span_start)


def draw_block_map(key, part):
    return layout_ints(key)[0]


def draw_span_blocks(key, part):
    permuted, starts, ends = layout_ints(key)
    return jnp.stack([starts, ends], axis=1)


def draw_position_ids(key, part):
    seq_pos, span_ids, span_start = row_info(key)
    grid_side = 8 if BLK % 8 == 0 else 2
    base_pos = span_start * BLK
    offset = seq_pos - base_pos
    visual = span_ids >= 0
    temporal = jnp.where(visual, base_pos + offset // BLK, seq_pos)
    height = jnp.where(visual, base_pos + offset % BLK // grid_side, seq_pos)
    width_id = jnp.where(visual, base_pos + offset % grid_side, seq_pos)
    return jnp.stack([temporal, height, width_id]).astype(jnp.int32)


def float_portion(key, salt, shape, spread):
    sub_key = jax.random.fold_in(key, salt)
    values_out = jnp.clip(jax.random.normal(sub_key, shape, jnp.float32) * spread, -4.0 * spread, 4.0 * spread)
    return values_out.astype(jnp.bfloat16)


def draw_queries(key, part):
    return float_portion(key, 201, (SEQUENCE_TOKENS, QUERY_HEADS * HEAD_SIZE), 2.0)


def draw_keys(key, part):
    return float_portion(key, 202, (SEQUENCE_TOKENS, KEY_VALUE_HEADS * HEAD_SIZE), 1.0)


def draw_values(key, part):
    return float_portion(key, 203, (SEQUENCE_TOKENS, KEY_VALUE_HEADS * HEAD_SIZE), 1.0)


def rope_tables_drawn(position_ids, width):
    half_width = width // 2
    pair_index = jnp.arange(half_width, dtype=jnp.int32)
    first_cut = width // 8
    second_cut = first_cut + 3 * width // 16
    inverse = jnp.exp(pair_index.astype(jnp.float32) * jnp.float32(-2.0 * math.log(THETA) / width))
    picked = jnp.where(pair_index[None, :] < first_cut, position_ids[0][:, None], jnp.where(pair_index[None, :] < second_cut, position_ids[1][:, None], position_ids[2][:, None]))
    angles = picked.astype(jnp.float32) * inverse[None, :]
    cosine_table = jnp.concatenate([jnp.cos(angles), jnp.cos(angles)], axis=-1)
    sine_lookup = jnp.concatenate([jnp.sin(angles), jnp.sin(angles)], axis=-1)
    return (cosine_table, sine_lookup)


def apply_rotation_sampled(field, cosine_table, sine_lookup):
    half_width = field.shape[-1] // 2
    turned = jnp.concatenate([-field[..., half_width:], field[..., :half_width]], axis=-1)
    return field * cosine_table[:, None, :] + turned * sine_lookup[:, None, :]


def forward_pass(key):
    seq_pos, span_ids, span_start = row_info(key)
    allowed = (seq_pos[None, :] <= seq_pos[:, None]) | (span_ids[:, None] == span_ids[None, :]) & (span_ids[:, None] >= 0)
    cosine_table, sine_lookup = rope_tables_drawn(draw_position_ids(key, 0), HEAD_SIZE)
    q_rot = apply_rotation_sampled(draw_queries(key, 0).astype(jnp.float32).reshape(SEQUENCE_TOKENS, QUERY_HEADS, HEAD_SIZE), cosine_table, sine_lookup).astype(jnp.bfloat16)
    rotated_keys = apply_rotation_sampled(draw_keys(key, 0).astype(jnp.float32).reshape(SEQUENCE_TOKENS, KEY_VALUE_HEADS, HEAD_SIZE), cosine_table, sine_lookup).astype(jnp.bfloat16)
    value_heads = draw_values(key, 0).reshape(SEQUENCE_TOKENS, KEY_VALUE_HEADS, HEAD_SIZE)
    score_scale = 1.0 / math.sqrt(HEAD_SIZE)
    query_group_width = QUERY_HEADS // KEY_VALUE_HEADS

    def one_head(head_index):
        kv_index = head_index // query_group_width
        q_head = lax.dynamic_index_in_dim(q_rot, head_index, 1, False)
        k_group = lax.dynamic_index_in_dim(rotated_keys, kv_index, 1, False)
        v_group = lax.dynamic_index_in_dim(value_heads, kv_index, 1, False)
        scores_h = jnp.dot(q_head, k_group.T, preferred_element_type=jnp.float32) * score_scale
        masked = jnp.where(allowed, scores_h, -jnp.inf)
        lse_head = jax.nn.logsumexp(masked, axis=-1)
        probs_h = jnp.exp(masked - lse_head[:, None])
        out_head = jnp.dot(probs_h.astype(jnp.bfloat16), v_group, preferred_element_type=jnp.float32)
        return (lse_head, out_head)
    lse_all, out_all = lax.map(one_head, jnp.arange(QUERY_HEADS, dtype=jnp.int32))
    return (lse_all, out_all.transpose(1, 0, 2).reshape(SEQUENCE_TOKENS, QUERY_HEADS * HEAD_SIZE))


def draw_attn_out(key, part):
    return forward_pass(key)[1].astype(jnp.bfloat16)


def draw_logsumexp(key, part):
    return forward_pass(key)[0].astype(jnp.float32)


def levels(stream_key, dims, shards, least, high):
    gain = 1.0
    for dim, shards_of in shards:
        heights = jax.random.uniform(jax.random.fold_in(jax.random.fold_in(stream_key, 6), dim), (shards_of,), jnp.float32, least / len(shards), high / len(shards))
        gain = gain * jnp.repeat(jnp.exp(heights), dims[dim] // shards_of).reshape((-1,) + (1,) * (len(dims) - 1 - dim))
    return gain


def scatter_about(key, extent, scale, most, cuts=(), kind=jnp.bfloat16):
    array = scale * jax.random.normal(key, extent, jnp.float32)
    if cuts:
        array = array * levels(key, extent, cuts, -0.22, 0.18)
    return jnp.clip(array, -most, most).astype(kind)


def setup_inputs(seed: int = 0) -> dict:
    streams_of = jax.random.split(jax.random.key(seed), 10)
    return {
        "queries": draw_queries(jax.random.fold_in(streams_of[9], 71), 0),
        "keys": draw_keys(jax.random.fold_in(streams_of[9], 71), 0),
        "values": draw_values(jax.random.fold_in(streams_of[9], 71), 0),
        "attn_out": draw_attn_out(jax.random.fold_in(streams_of[9], 71), 0),
        "out_grad": scatter_about(streams_of[4], (SEQUENCE_TOKENS, QUERY_HEADS * HEAD_SIZE), 4.0, 24.0, ((0, 32),)),
        "logsumexp": draw_logsumexp(jax.random.fold_in(streams_of[9], 71), 0),
        "position_ids": draw_position_ids(jax.random.fold_in(streams_of[9], 71), 0),
        "block_map": draw_block_map(jax.random.fold_in(streams_of[9], 71), 0),
        "span_blocks": draw_span_blocks(jax.random.fold_in(streams_of[9], 71), 0),
    }


THETA = 1000000.0

def rope_tables(position_ids, width):
    half_width = width // 2
    pair_index = jnp.arange(half_width, dtype=jnp.int32)
    first_cut = width // 8
    second_cut = first_cut + 3 * width // 16
    inverse = jnp.exp(pair_index.astype(jnp.float32) * jnp.float32(-2.0 * math.log(THETA) / width))
    picked = jnp.where(pair_index[None, :] < first_cut, position_ids[0][:, None], jnp.where(pair_index[None, :] < second_cut, position_ids[1][:, None], position_ids[2][:, None]))
    angles = picked.astype(jnp.float32) * inverse[None, :]
    cosine_table = jnp.concatenate([jnp.cos(angles), jnp.cos(angles)], axis=-1)
    sine_lookup = jnp.concatenate([jnp.sin(angles), jnp.sin(angles)], axis=-1)
    return (cosine_table, sine_lookup)

def apply_rotation(field, cosine_table, sine_lookup):
    half_width = field.shape[-1] // 2
    turned = jnp.concatenate([-field[..., half_width:], field[..., :half_width]], axis=-1)
    return field * cosine_table[:, None, :] + turned * sine_lookup[:, None, :]

def reverse_rotation(field, cosine_table, sine_lookup):
    half_width = field.shape[-1] // 2
    scaled = field * sine_lookup[:, None, :]
    turned = jnp.concatenate([scaled[..., half_width:], -scaled[..., :half_width]], axis=-1)
    return field * cosine_table[:, None, :] + turned

def row_tables(block_map, span_blocks, row_total_count, block_len):
    row_index = jnp.arange(row_total_count, dtype=jnp.int32)
    seq_pos = (jnp.take(block_map, row_index // block_len) * block_len + row_index % block_len).astype(jnp.int32)
    seq_block = seq_pos // block_len
    inside = (seq_block[:, None] >= span_blocks[None, :, 0]) & (seq_block[:, None] < span_blocks[None, :, 1])
    numbers = jnp.arange(span_blocks.shape[0], dtype=jnp.int32)[None, :] + 1
    span_ids = (lax.optimization_barrier(jnp.sum(jnp.where(inside, numbers, 0), axis=1)) - 1).astype(jnp.int32)
    return (seq_pos, span_ids)

def reference(queries, keys, values, attn_out, out_grad, logsumexp, position_ids, block_map, span_blocks):
    row_total_count = queries.shape[0]
    score_scale = 1.0 / math.sqrt(HEAD_SIZE)
    query_group_width = QUERY_HEADS // KEY_VALUE_HEADS
    seq_pos, span_ids = row_tables(block_map, span_blocks, row_total_count, BLK)
    allowed = (seq_pos[None, :] <= seq_pos[:, None]) | (span_ids[:, None] == span_ids[None, :]) & (span_ids[:, None] >= 0)
    cosine_table, sine_lookup = rope_tables(position_ids, HEAD_SIZE)
    q_rot = apply_rotation(queries.astype(jnp.float32).reshape(row_total_count, QUERY_HEADS, HEAD_SIZE), cosine_table, sine_lookup).astype(jnp.bfloat16)
    rotated_keys = apply_rotation(keys.astype(jnp.float32).reshape(row_total_count, KEY_VALUE_HEADS, HEAD_SIZE), cosine_table, sine_lookup).astype(jnp.bfloat16)
    value_heads = values.reshape(row_total_count, KEY_VALUE_HEADS, HEAD_SIZE)
    grad_heads = out_grad.reshape(row_total_count, QUERY_HEADS, HEAD_SIZE)
    delta_rows = lax.optimization_barrier(jnp.sum(out_grad.astype(jnp.float32).reshape(row_total_count, QUERY_HEADS, HEAD_SIZE) * attn_out.astype(jnp.float32).reshape(row_total_count, QUERY_HEADS, HEAD_SIZE), axis=-1))

    def single_key_value(kv_index):
        k_group = lax.dynamic_index_in_dim(rotated_keys, kv_index, 1, False)
        v_group = lax.dynamic_index_in_dim(value_heads, kv_index, 1, False)

        def one_q(loop_state, member):
            head_index = kv_index * query_group_width + member
            q_head = lax.dynamic_index_in_dim(q_rot, head_index, 1, False)
            do_head = lax.dynamic_index_in_dim(grad_heads, head_index, 1, False)
            lse_head = lax.dynamic_index_in_dim(logsumexp, head_index, 0, False)
            delta_head = lax.dynamic_index_in_dim(delta_rows, head_index, 1, False)
            scores_h = jnp.dot(q_head, k_group.T, preferred_element_type=jnp.float32) * score_scale
            probs_h = jnp.exp(jnp.where(allowed, scores_h - lse_head[:, None], -jnp.inf))
            dv_part = jnp.dot(probs_h.astype(jnp.bfloat16).T, do_head, preferred_element_type=jnp.float32)
            grad_p = jnp.dot(do_head, v_group.T, preferred_element_type=jnp.float32)
            grad_s = (probs_h * (grad_p - delta_head[:, None])).astype(jnp.bfloat16)
            dq_head = jnp.dot(grad_s, k_group, preferred_element_type=jnp.float32) * score_scale
            dk_part = jnp.dot(grad_s.T, q_head, preferred_element_type=jnp.float32)
            return ((loop_state[0] + dk_part, loop_state[1] + dv_part), dq_head)
        empty = jnp.zeros((row_total_count, HEAD_SIZE), jnp.float32)
        (dk_group, dv_group), dq_group = lax.scan(one_q, (empty, empty), jnp.arange(query_group_width, dtype=jnp.int32))
        return (dq_group, dk_group * score_scale, dv_group)
    query_gradient_full, key_gradient_full, value_gradient_full = lax.map(single_key_value, jnp.arange(KEY_VALUE_HEADS, dtype=jnp.int32))
    dq_rot = query_gradient_full.reshape(QUERY_HEADS, row_total_count, HEAD_SIZE).transpose(1, 0, 2)
    grad_q = reverse_rotation(dq_rot, cosine_table, sine_lookup).astype(jnp.bfloat16).reshape(row_total_count, QUERY_HEADS * HEAD_SIZE)
    rotated_key_gradient = key_gradient_full.transpose(1, 0, 2)
    key_gradient = reverse_rotation(rotated_key_gradient, cosine_table, sine_lookup).astype(jnp.bfloat16).reshape(row_total_count, KEY_VALUE_HEADS * HEAD_SIZE)
    value_gradient = value_gradient_full.transpose(1, 0, 2).astype(jnp.bfloat16).reshape(row_total_count, KEY_VALUE_HEADS * HEAD_SIZE)
    return (grad_q, key_gradient, value_gradient)
```

```python
import functools
import math

import jax
import jax.numpy as jnp
from jax import lax
from jax.experimental import pallas as pl
from jax.experimental.pallas import tpu as pltpu
from jax.sharding import Mesh
from jax.sharding import PartitionSpec as P

HEAD_SIZE = 128
BLOCKS_DEV = 2
THETA = 1000000.0
CHUNK = 256
SCORE_SCALE = 1.0 / math.sqrt(HEAD_SIZE)
LOG2E = math.log2(math.e)
SWAP = [(0, 1), (1, 0)]


def turned_tables(ids, width):
    half = width // 2
    rows = ids.shape[1]
    pair = lax.broadcasted_iota(jnp.int32, (half, rows), 0)
    first_cut = width // 8
    second_cut = first_cut + 3 * width // 16
    inverse = jnp.exp(pair.astype(jnp.float32) * jnp.float32(-2.0 * math.log(THETA) / width))
    ids = ids.astype(jnp.float32)
    picked = jnp.where(
        pair < first_cut, ids[0:1, :], jnp.where(pair < second_cut, ids[1:2, :], ids[2:3, :])
    )
    angles = picked * inverse
    cosine = jnp.cos(angles)
    sine = jnp.sin(angles)
    return (
        jnp.concatenate([cosine, cosine], axis=0).T,
        jnp.concatenate([sine, sine], axis=0).T,
    )


def half_sign():
    lane = lax.broadcasted_iota(jnp.int32, (1, HEAD_SIZE), 1)
    return jnp.where(lane < HEAD_SIZE // 2, -1.0, 1.0).astype(jnp.float32)


def prep_kernel(
    split, heads, where_ref, ids_own, ids_other, k_own, k_other, v_own, v_other,
    kv_ref, cos_ref, sin_ref,
):
    core = where_ref[0]
    rows = k_own.shape[0]
    sign = half_sign()
    sources = [(ids_own, k_own, v_own, core)]
    if split == 2:
        sources.append((ids_other, k_other, v_other, 1 - core))
    else:
        sources = [(ids_own, k_own, v_own, 0)]
    for number, (ids, k_ref, v_ref, place) in enumerate(sources):
        cosine, sine = turned_tables(ids[...], HEAD_SIZE)
        cos_ref[pl.ds(number * rows, rows), :] = cosine
        sin_ref[pl.ds(number * rows, rows), :] = sine
        at = pl.multiple_of(place * rows, rows)
        for head in range(heads):
            columns = pl.ds(head * HEAD_SIZE, HEAD_SIZE)
            keys = k_ref[:, columns].astype(jnp.float32)
            turned = pltpu.roll(keys, HEAD_SIZE // 2, 1) * sign
            kv_ref[head, 0, pl.ds(at, rows), :] = (keys * cosine + turned * sine).astype(
                jnp.bfloat16
            )
            kv_ref[head, 1, pl.ds(at, rows), :] = v_ref[:, columns]


def row_vector(lse, upper, block_len):
    group, width = lse.shape
    rolled = pltpu.roll(lse, block_len, 1)
    low = jnp.where(upper == 0, lse, rolled)
    high = jnp.where(upper == 0, rolled, lse)
    lane = lax.broadcasted_iota(jnp.int32, (1, width), 1)
    pieces = [
        jnp.where(lane < block_len, low[h : h + 1, :], high[h + 1 : h + 2, :])
        for h in range(0, group, 2)
    ]
    return jnp.concatenate(pieces, axis=1)


def attend_kernel(split, group, block_len, where_ref, map_ref, span_ref, *refs):
    refs = list(refs)
    kv_ref = refs.pop(0)
    cos_ref = refs.pop(0)
    sin_ref = refs.pop(0)
    q_refs = [refs.pop(0) for _ in range(split)]
    a_refs = [refs.pop(0) for _ in range(split)]
    l_refs = [refs.pop(0) for _ in range(split)]
    g_refs = [refs.pop(0) for _ in range(4 if split == 2 else 1)]
    dq_refs = [refs.pop(0) for _ in range(split)]
    part_ref = refs.pop(0)
    k_sort, v_sort, k_turn, q_all, g_all, l_all, d_all, dk_sum, dv_sum, dq_sum = refs
    core, tp_index, device = where_ref[0], where_ref[1], where_ref[2]
    rows = q_refs[0].shape[0]
    units, _, unit_rows, _ = kv_ref.shape
    unit_blocks = unit_rows // block_len
    blocks = units * unit_blocks
    spans = span_ref.shape[0] // 2
    columns = group * block_len
    sign = half_sign()

    @pl.loop(0, blocks)
    def _(stored):
        unit = stored // unit_blocks
        at = pl.multiple_of((stored % unit_blocks) * block_len, block_len)
        to = pl.multiple_of(map_ref[stored] * block_len, block_len)
        k_sort[pl.ds(to, block_len), :] = kv_ref[unit, 0, pl.ds(at, block_len), :]
        v_sort[pl.ds(to, block_len), :] = kv_ref[unit, 1, pl.ds(at, block_len), :]

    @pl.loop(0, k_turn.shape[0])
    def _(chunk):
        at = pl.multiple_of(chunk * CHUNK, CHUNK)
        k_turn[chunk] = k_sort[pl.ds(at, CHUNK), :].T
        dk_sum[pl.ds(at, CHUNK), :] = jnp.zeros((CHUNK, HEAD_SIZE), jnp.float32)
        dv_sum[pl.ds(at, CHUNK), :] = jnp.zeros((CHUNK, HEAD_SIZE), jnp.float32)

    places = []
    for number in range(split):
        owner = device if number == 0 else device + 1 - 2 * core
        for step in range(BLOCKS_DEV):
            if split == 2:
                upper = tp_index if step == 0 else 1 - tp_index
                g_ref, g_row = g_refs[number * BLOCKS_DEV + step], 0
            else:
                upper = step
                g_ref, g_row = g_refs[0], step * block_len
            places.append((number, owner * BLOCKS_DEV + upper, upper, g_ref, g_row))

    for place, (number, stored, upper, g_ref, g_row) in enumerate(places):
        row = upper * block_len
        if not isinstance(row, int):
            row = pl.multiple_of(row, block_len)
        table_row = row + number * rows
        if not isinstance(table_row, int):
            table_row = pl.multiple_of(table_row, block_len)
        cosine = cos_ref[pl.ds(table_row, block_len), :]
        sine = sin_ref[pl.ds(table_row, block_len), :] * sign
        products = []
        for head in range(group):
            lanes = pl.ds(head * HEAD_SIZE, HEAD_SIZE)
            field = q_refs[number][pl.ds(row, block_len), lanes].astype(jnp.float32)
            turned = pltpu.roll(field, HEAD_SIZE // 2, 1)
            q_all[place, pl.ds(head * block_len, block_len), :] = (
                field * cosine + turned * sine
            ).astype(jnp.bfloat16)
            grad = g_ref[pl.ds(g_row, block_len), lanes]
            g_all[place, pl.ds(head * block_len, block_len), :] = grad
            products.append(
                grad.astype(jnp.float32)
                * a_refs[number][pl.ds(row, block_len), lanes].astype(jnp.float32)
            )
        product = jnp.concatenate(products, axis=0)
        d_all[place] = jnp.sum(product.T, axis=0, keepdims=True)
        l_all[place] = row_vector(l_refs[number][...], upper, block_len) * LOG2E

    lane = lax.broadcasted_iota(jnp.int32, (1, columns), 1)
    within = lax.rem(lane, block_len)
    key_row = lax.broadcasted_iota(jnp.int32, (CHUNK, 1), 0)

    for place, (number, stored, upper, g_ref, g_row) in enumerate(places):
        block = map_ref[stored]
        end = jnp.int32(0)
        for span in range(spans):
            inside = (block >= span_ref[2 * span]) & (block < span_ref[2 * span + 1])
            end = jnp.where(inside, span_ref[2 * span + 1], end)
        limit = jnp.where(end > 0, end * block_len, block * block_len + within + 1)
        last = jnp.maximum(end, block + 1) * block_len
        chunks = (last + CHUNK - 1) // CHUNK
        queries = q_all[place]
        grads = g_all[place]
        lse = l_all[place]
        delta = d_all[place]
        dq_sum[...] = jnp.zeros_like(dq_sum)

        @pl.loop(0, chunks)
        def _(chunk):
            at = pl.multiple_of(chunk * CHUNK, CHUNK)
            keys = k_sort[pl.ds(at, CHUNK), :]
            values = v_sort[pl.ds(at, CHUNK), :]
            scores = lax.dot_general(
                keys, queries, (((1,), (1,)), ((), ())), preferred_element_type=jnp.float32
            )
            raised = scores * (SCORE_SCALE * LOG2E) - lse
            raised = jnp.where(key_row + at < limit, raised, -jnp.inf)
            probs = jnp.exp2(raised)
            grad_p = lax.dot_general(
                values, grads, (((1,), (1,)), ((), ())), preferred_element_type=jnp.float32
            )
            grad_s = (probs * (grad_p - delta)).astype(jnp.bfloat16)
            dv_sum[pl.ds(at, CHUNK), :] += jnp.dot(
                probs.astype(jnp.bfloat16), grads, preferred_element_type=jnp.float32
            )
            dk_sum[pl.ds(at, CHUNK), :] += jnp.dot(
                grad_s, queries, preferred_element_type=jnp.float32
            )
            dq_sum[...] += jnp.dot(k_turn[chunk], grad_s, preferred_element_type=jnp.float32)

        row = upper * block_len
        if not isinstance(row, int):
            row = pl.multiple_of(row, block_len)
        table_row = row + number * rows
        if not isinstance(table_row, int):
            table_row = pl.multiple_of(table_row, block_len)
        cosine = cos_ref[pl.ds(table_row, block_len), :]
        sine = sin_ref[pl.ds(table_row, block_len), :]
        dq_rot = dq_sum[...].T * SCORE_SCALE
        for head in range(group):
            field = dq_rot[head * block_len : (head + 1) * block_len, :]
            turned = pltpu.roll(field * sine, HEAD_SIZE // 2, 1) * sign
            dq_refs[number][pl.ds(row, block_len), pl.ds(head * HEAD_SIZE, HEAD_SIZE)] = (
                field * cosine - turned
            ).astype(jnp.bfloat16)

    @pl.loop(0, blocks)
    def _(stored):
        unit = stored // unit_blocks
        to = pl.multiple_of((stored % unit_blocks) * block_len, block_len)
        at = pl.multiple_of(map_ref[stored] * block_len, block_len)
        part_ref[unit, 0, pl.ds(to, block_len), :] = (
            dk_sum[pl.ds(at, block_len), :] * SCORE_SCALE
        ).astype(part_ref.dtype)
        part_ref[unit, 1, pl.ds(to, block_len), :] = dv_sum[pl.ds(at, block_len), :].astype(
            part_ref.dtype
        )


def reverse_rotation(field, cosine, sine):
    half = field.shape[-1] // 2
    scaled = field * sine
    turned = jnp.concatenate([scaled[..., half:], -scaled[..., :half]], axis=-1)
    return field * cosine + turned


def whole(shape):
    return pl.BlockSpec(shape, lambda *_: (0,) * len(shape))


def shards(
    queries, keys, values, attn_out, out_grad, logsumexp, position_ids, block_map, span_blocks
):
    rows = queries.shape[0]
    kv_heads = keys.shape[1] // HEAD_SIZE
    q_heads = queries.shape[1] // HEAD_SIZE
    group = q_heads // kv_heads
    block_len = rows // BLOCKS_DEV
    tp_size = lax.axis_size("tp")
    split = 2 if kv_heads % 2 == 0 and tp_size == 2 else 1
    heads = kv_heads // split
    core = lax.axis_index("core")
    tp_index = lax.axis_index("tp")
    ring = lax.axis_size("z") * lax.axis_size("y")
    units = ring * 2 // split
    unit_rows = rows * split
    gather_axes = ("z", "y") if split == 2 else ("z", "y", "core")
    device = (lax.axis_index("z") * lax.axis_size("y") + lax.axis_index("y")) * 2 + core
    place = jnp.stack([core, tp_index, device]).astype(jnp.int32)
    spans = span_blocks.reshape(-1)
    width = group * HEAD_SIZE

    def other_half(array, axis):
        size = array.shape[axis] // 2
        return lax.dynamic_slice_in_dim(array, (1 - core) * size, size, axis)

    def own_half(array, axis):
        size = array.shape[axis] // 2
        return lax.dynamic_slice_in_dim(array, core * size, size, axis)

    def swap(array):
        return lax.ppermute(array, "core", SWAP)

    if split == 2:
        ids_other = swap(position_ids)
        k_other = swap(other_half(keys, 1))
        v_other = swap(other_half(values, 1))
        k_mine, v_mine = own_half(keys, 1), own_half(values, 1)
        lse_other = swap(other_half(logsumexp, 0))
    else:
        ids_other, k_other, v_other = position_ids, keys, values
        k_mine, v_mine = keys, values

    kv_block, cosine, sine = pl.pallas_call(
        functools.partial(prep_kernel, split, heads),
        grid_spec=pltpu.PrefetchScalarGridSpec(
            num_scalar_prefetch=1,
            grid=(1,),
            in_specs=[
                whole(a.shape)
                for a in (position_ids, ids_other, k_mine, k_other, v_mine, v_other)
            ],
            out_specs=[
                whole((heads, 2, unit_rows, HEAD_SIZE)),
                whole((unit_rows, HEAD_SIZE)),
                whole((unit_rows, HEAD_SIZE)),
            ],
        ),
        out_shape=[
            jax.ShapeDtypeStruct((heads, 2, unit_rows, HEAD_SIZE), jnp.bfloat16),
            jax.ShapeDtypeStruct((unit_rows, HEAD_SIZE), jnp.float32),
            jax.ShapeDtypeStruct((unit_rows, HEAD_SIZE), jnp.float32),
        ],
        name="prep",
    )(place, position_ids, ids_other, k_mine, k_other, v_mine, v_other)

    gathered = [
        lax.all_gather(kv_block[head], gather_axes, axis=0, tiled=False)
        for head in range(heads)
    ]

    if split == 1:
        grads_in = lax.all_to_all(out_grad, "tp", split_axis=1, concat_axis=0, tiled=True)

    tokens = units * unit_rows
    dq_parts = []
    finished = []
    for head in range(heads):
        own_column = core * heads + head if split == 2 else head

        def picked(array, block_rows):
            return pl.BlockSpec(
                (block_rows, width),
                lambda i, where, *_: (0, (where[0] * heads if split == 2 else 0) + head),
            )

        q_in, a_in, l_in = [queries], [attn_out], [logsumexp]
        q_spec, a_spec = [picked(queries, rows)], [picked(attn_out, rows)]
        l_spec = [
            pl.BlockSpec(
                (group, rows),
                lambda i, where, *_: ((where[0] * heads if split == 2 else 0) + head, 0),
            )
        ]
        if split == 2:
            away = ((1 - core) * heads + head) * width
            q_in.append(swap(lax.dynamic_slice_in_dim(queries, away, width, 1)))
            a_in.append(swap(lax.dynamic_slice_in_dim(attn_out, away, width, 1)))
            l_in.append(lse_other)
            q_spec.append(whole((rows, width)))
            a_spec.append(whole((rows, width)))
            l_spec.append(pl.BlockSpec((group, rows), lambda i, *_: (head, 0)))

            def grad_piece(to_tp, to_core):
                column = ((to_tp * 2 + to_core) * heads + head) * width
                return lax.dynamic_slice_in_dim(out_grad, column, width, 1)

            pairs = [(c, t) for c in range(2) for t in range(2)]

            def sent(piece, flip_core, flip_tp):
                route = [
                    (c * 2 + t, (c ^ flip_core) * 2 + (t ^ flip_tp)) for c, t in pairs
                ]
                return lax.ppermute(piece, ("core", "tp"), route)

            g_in = [
                grad_piece(tp_index, core),
                sent(grad_piece(1 - tp_index, core), 0, 1),
                sent(grad_piece(tp_index, 1 - core), 1, 0),
                sent(grad_piece(1 - tp_index, 1 - core), 1, 1),
            ]
            g_spec = [whole((block_len, width))] * 4
        else:
            g_in = [grads_in]
            g_spec = [picked(grads_in, rows)]

        inputs = [gathered[head], cosine, sine]
        specs = [whole(a.shape) for a in inputs]
        columns = group * block_len
        results = pl.pallas_call(
            functools.partial(attend_kernel, split, group, block_len),
            grid_spec=pltpu.PrefetchScalarGridSpec(
                num_scalar_prefetch=3,
                grid=(1,),
                in_specs=specs + q_spec + a_spec + l_spec + g_spec,
                out_specs=[whole((rows, width))] * split
                + [whole((units, 2, unit_rows, HEAD_SIZE))],
                scratch_shapes=[
                    pltpu.VMEM((tokens, HEAD_SIZE), jnp.bfloat16),
                    pltpu.VMEM((tokens, HEAD_SIZE), jnp.bfloat16),
                    pltpu.VMEM((tokens // CHUNK, HEAD_SIZE, CHUNK), jnp.bfloat16),
                    pltpu.VMEM((split * BLOCKS_DEV, columns, HEAD_SIZE), jnp.bfloat16),
                    pltpu.VMEM((split * BLOCKS_DEV, columns, HEAD_SIZE), jnp.bfloat16),
                    pltpu.VMEM((split * BLOCKS_DEV, 1, columns), jnp.float32),
                    pltpu.VMEM((split * BLOCKS_DEV, 1, columns), jnp.float32),
                    pltpu.VMEM((tokens, HEAD_SIZE), jnp.float32),
                    pltpu.VMEM((tokens, HEAD_SIZE), jnp.float32),
                    pltpu.VMEM((HEAD_SIZE, columns), jnp.float32),
                ],
            ),
            out_shape=[jax.ShapeDtypeStruct((rows, width), jnp.bfloat16)] * split
            + [jax.ShapeDtypeStruct((units, 2, unit_rows, HEAD_SIZE), jnp.bfloat16)],
            compiler_params=pltpu.CompilerParams(vmem_limit_bytes=40 * 1024 * 1024),
            cost_estimate=pl.CostEstimate(
                flops=6 * group * unit_rows * tokens * HEAD_SIZE,
                bytes_accessed=4 * 1024 * 1024,
                transcendentals=group * unit_rows * tokens // 2,
            ),
            name="attend",
        )(place, block_map, spans, *inputs, *q_in, *a_in, *l_in, *g_in)
        part = results[-1]
        total = lax.psum_scatter(part, gather_axes, scatter_dimension=0, tiled=True)[0]
        if split == 2:
            dq_parts.append((results[0], swap(results[1])))
            mine = own_half(total, 1)
            theirs = swap(other_half(total, 1))
            finished.append((mine, theirs))
        else:
            dq_parts.append((results[0],))
            finished.append((total,))

    def in_order(pairs):
        if split == 1:
            return jnp.concatenate([p[0] for p in pairs], axis=-1)
        mine = jnp.concatenate([p[0] for p in pairs], axis=-1)
        theirs = jnp.concatenate([p[1] for p in pairs], axis=-1)
        return jnp.where(
            core == 0,
            jnp.concatenate([mine, theirs], axis=-1),
            jnp.concatenate([theirs, mine], axis=-1),
        )

    grad_q = in_order(dq_parts)
    key_sums = in_order([tuple(p[0] for p in f) for f in finished]).astype(jnp.float32)
    key_gradient = (
        reverse_rotation(
            key_sums.reshape(rows, kv_heads, HEAD_SIZE),
            cosine[:rows, None, :],
            sine[:rows, None, :],
        )
        .astype(jnp.bfloat16)
        .reshape(rows, kv_heads * HEAD_SIZE)
    )
    value_gradient = in_order([tuple(p[1] for p in f) for f in finished])
    return (grad_q, key_gradient, value_gradient)


def solution(mesh):
    ctx, tp = mesh.shape["ctx"], mesh.shape["tp"]
    fine = Mesh(mesh.devices.reshape(ctx // 4, 2, 2, tp), ("z", "y", "core", "tp"))
    ctx_axes = ("z", "y", "core")
    return jax.shard_map(
        shards,
        mesh=fine,
        in_specs=(
            P(ctx_axes, "tp"),
            P(ctx_axes, "tp"),
            P(ctx_axes, "tp"),
            P(ctx_axes, "tp"),
            P((*ctx_axes, "tp"), None),
            P("tp", ctx_axes),
            P(None, ctx_axes),
            P(),
            P(),
        ),
        out_specs=(P(ctx_axes, "tp"), P(ctx_axes, "tp"), P(ctx_axes, "tp")),
        check_vma=False,
    )
```

```python
import functools
import math

import jax
import jax.numpy as jnp
from jax import lax
from jax.experimental import pallas as pl
from jax.experimental.pallas import tpu as pltpu
from jax.sharding import Mesh
from jax.sharding import PartitionSpec as P

HEAD_SIZE = 128
BLOCKS_DEV = 2
THETA = 1000000.0
CHUNK = 256
SCORE_SCALE = 1.0 / math.sqrt(HEAD_SIZE)
LOG2E = math.log2(math.e)
MEMORY = 56 * 1024 * 1024


def turned_tables(ids, width):
    half = width // 2
    rows = ids.shape[1]
    pair = lax.broadcasted_iota(jnp.int32, (half, rows), 0)
    first_cut = width // 8
    second_cut = first_cut + 3 * width // 16
    inverse = jnp.exp(pair.astype(jnp.float32) * jnp.float32(-2.0 * math.log(THETA) / width))
    ids = ids.astype(jnp.float32)
    picked = jnp.where(
        pair < first_cut, ids[0:1, :], jnp.where(pair < second_cut, ids[1:2, :], ids[2:3, :])
    )
    angles = picked * inverse
    cosine = jnp.cos(angles)
    sine = jnp.sin(angles)
    return (
        jnp.concatenate([cosine, cosine], axis=0).T,
        jnp.concatenate([sine, sine], axis=0).T,
    )


def half_sign():
    lane = lax.broadcasted_iota(jnp.int32, (1, HEAD_SIZE), 1)
    return jnp.where(lane < HEAD_SIZE // 2, -1.0, 1.0).astype(jnp.float32)


def head_lanes(member, flip, heads, head):
    first = ((member ^ flip) * heads + head) * HEAD_SIZE
    return pl.ds(pl.multiple_of(first, HEAD_SIZE), HEAD_SIZE)


def first_kernel(members, with_piece, where_ref, ids_ref, k_ref, v_ref, *refs):
    refs = list(refs)
    if with_piece:
        grad_ref = refs.pop(0)
        copy_sem = refs.pop()
        piece_ref = refs.pop()
        width = piece_ref.shape[1]
        start = pl.multiple_of((1 - where_ref[1]) * width, width)
        copy = pltpu.make_async_copy(grad_ref.at[:, pl.ds(start, width)], piece_ref, copy_sem)
        copy.start()
    cos_ref, sin_ref = refs.pop(0), refs.pop(0)
    member = where_ref[0]
    cosine, sine = turned_tables(ids_ref[...], HEAD_SIZE)
    cos_ref[...] = cosine
    sin_ref[...] = sine
    signed = sine * half_sign()
    for flip in range(members):
        lanes = head_lanes(member, flip, 1, 0)
        keys = k_ref[:, lanes].astype(jnp.float32)
        refs[flip][0] = (keys * cosine + pltpu.roll(keys, HEAD_SIZE // 2, 1) * signed).astype(
            jnp.bfloat16
        )
        refs[flip][1] = v_ref[:, lanes]
    if with_piece:
        copy.wait()


def query_kernel(members, group, where_ref, cos_ref, sin_ref, q_ref, *out_refs):
    member = where_ref[0]
    cosine = cos_ref[...]
    signed = sin_ref[...] * half_sign()
    for flip in range(members):
        for head in range(group):
            field = q_ref[:, head_lanes(member, flip, group, head)].astype(jnp.float32)
            turned = pltpu.roll(field, HEAD_SIZE // 2, 1)
            out_refs[flip][:, head * HEAD_SIZE : (head + 1) * HEAD_SIZE] = (
                field * cosine + turned * signed
            ).astype(jnp.bfloat16)


def delta_kernel(members, group, where_ref, a_ref, l_ref, *refs):
    refs = list(refs)
    own_ref = refs.pop(0)
    other_ref = refs.pop(0) if members > 1 else None
    grad_refs, stat_refs = refs[:members], refs[members:]
    member, tp_index = where_ref[0], where_ref[1]
    rows = a_ref.shape[0]
    for flip in range(members):
        g_ref = grad_refs[flip]
        sums = []
        for head in range(group):
            lanes = head_lanes(member, flip, group, head)
            here = slice(head * HEAD_SIZE, (head + 1) * HEAD_SIZE)
            if members > 1:
                half = rows // 2
                mine = pl.multiple_of(tp_index * half, half)
                theirs = pl.multiple_of((1 - tp_index) * half, half)
                g_ref[pl.ds(mine, half), here] = own_ref[:, lanes]
                g_ref[pl.ds(theirs, half), here] = other_ref[:, lanes]
            else:
                g_ref[:, here] = own_ref[:, lanes]
            product = g_ref[:, here].astype(jnp.float32) * a_ref[:, lanes].astype(jnp.float32)
            sums.append(jnp.sum(product.T, axis=0, keepdims=True))
        first = pl.multiple_of((member ^ flip) * group, group)
        stat_refs[flip][0:group, :] = l_ref[pl.ds(first, group), :] * LOG2E
        stat_refs[flip][group : 2 * group, :] = jnp.concatenate(sums, axis=0)


def row_vector(table, upper, block_len):
    group, width = table.shape
    rolled = pltpu.roll(table, block_len, 1)
    low, high = (table, rolled) if upper == 0 else (rolled, table)
    lane = lax.broadcasted_iota(jnp.int32, (1, width), 1)
    pieces = [
        jnp.where(lane < block_len, low[h : h + 1, :], high[h + 1 : h + 2, :])
        for h in range(0, group, 2)
    ]
    return jnp.concatenate(pieces, axis=1)


def attend_kernel(members, group, block_len, slabs, where_ref, map_ref, span_ref, *refs):
    refs = list(refs)
    kv_refs = [refs.pop(0) for _ in range(slabs)]
    q_refs = [refs.pop(0) for _ in range(members)]
    g_refs = [refs.pop(0) for _ in range(members)]
    s_refs = [refs.pop(0) for _ in range(members)]
    dq_refs = [refs.pop(0) for _ in range(members)]
    part_refs = [refs.pop(0) for _ in range(slabs)]
    k_sort, v_sort, k_turn, q_all, g_all, l_all, d_all, dk_sum, dv_sum, dq_sum = refs
    member, layer, layers, device = where_ref[0], where_ref[2], where_ref[3], where_ref[4]
    rows = q_refs[0].shape[0]
    units = kv_refs[0].shape[0]
    spans = span_ref.shape[0] // 2
    columns = group * block_len

    def sequence_block(slab, unit, step):
        if members > 1:
            owner = lax.rem(layer - slab + layers, layers) * members + (member ^ unit)
        else:
            owner = unit
        return map_ref[owner * BLOCKS_DEV + step]

    def each_block(body):
        for slab in range(slabs):

            @pl.loop(0, units)
            def _(unit):
                for step in range(BLOCKS_DEV):
                    at = pl.multiple_of(sequence_block(slab, unit, step) * block_len, block_len)
                    body(slab, unit, step * block_len, pl.ds(at, block_len))

    def sort(slab, unit, row, to):
        k_sort[to, :] = kv_refs[slab][unit, 0, pl.ds(row, block_len), :]
        v_sort[to, :] = kv_refs[slab][unit, 1, pl.ds(row, block_len), :]

    each_block(sort)

    @pl.loop(0, k_turn.shape[0])
    def _(chunk):
        at = pl.multiple_of(chunk * CHUNK, CHUNK)
        k_turn[chunk] = k_sort[pl.ds(at, CHUNK), :].T
        dk_sum[pl.ds(at, CHUNK), :] = jnp.zeros((CHUNK, HEAD_SIZE), jnp.float32)
        dv_sum[pl.ds(at, CHUNK), :] = jnp.zeros((CHUNK, HEAD_SIZE), jnp.float32)

    for flip in range(members):
        lse, delta = s_refs[flip][0:group, :], s_refs[flip][group : 2 * group, :]
        for step in range(BLOCKS_DEV):
            place = flip * BLOCKS_DEV + step
            from_rows = slice(step * block_len, (step + 1) * block_len)
            for head in range(group):
                lanes = slice(head * HEAD_SIZE, (head + 1) * HEAD_SIZE)
                to_rows = slice(head * block_len, (head + 1) * block_len)
                q_all[place, to_rows, :] = q_refs[flip][from_rows, lanes]
                g_all[place, to_rows, :] = g_refs[flip][from_rows, lanes]
            l_all[place] = row_vector(lse, step, block_len)
            d_all[place] = row_vector(delta, step, block_len)

    lane = lax.broadcasted_iota(jnp.int32, (1, columns), 1)
    within = lax.rem(lane, block_len)
    key_row = lax.broadcasted_iota(jnp.int32, (CHUNK, 1), 0)

    for flip in range(members):
        for step in range(BLOCKS_DEV):
            place = flip * BLOCKS_DEV + step
            owner = device if members == 1 else layer * members + (member ^ flip)
            block = map_ref[owner * BLOCKS_DEV + step]
            end = jnp.int32(0)
            for span in range(spans):
                inside = (block >= span_ref[2 * span]) & (block < span_ref[2 * span + 1])
                end = jnp.where(inside, span_ref[2 * span + 1], end)
            limit = jnp.where(end > 0, end * block_len, block * block_len + within + 1)
            last = jnp.maximum(end, block + 1) * block_len
            chunks = (last + CHUNK - 1) // CHUNK
            queries = q_all[place]
            grads = g_all[place]
            lse = l_all[place]
            delta = d_all[place]
            dq_sum[...] = jnp.zeros_like(dq_sum)

            @pl.loop(0, chunks)
            def _(chunk):
                at = pl.multiple_of(chunk * CHUNK, CHUNK)
                keys = k_sort[pl.ds(at, CHUNK), :]
                values = v_sort[pl.ds(at, CHUNK), :]
                scores = lax.dot_general(
                    keys, queries, (((1,), (1,)), ((), ())), preferred_element_type=jnp.float32
                )
                raised = scores * (SCORE_SCALE * LOG2E) - lse
                raised = jnp.where(key_row + at < limit, raised, -jnp.inf)
                probs = jnp.exp2(raised)
                grad_p = lax.dot_general(
                    values, grads, (((1,), (1,)), ((), ())), preferred_element_type=jnp.float32
                )
                grad_s = (probs * (grad_p - delta)).astype(jnp.bfloat16)
                dv_sum[pl.ds(at, CHUNK), :] += jnp.dot(
                    probs.astype(jnp.bfloat16), grads, preferred_element_type=jnp.float32
                )
                dk_sum[pl.ds(at, CHUNK), :] += jnp.dot(
                    grad_s, queries, preferred_element_type=jnp.float32
                )
                dq_sum[...] += jnp.dot(k_turn[chunk], grad_s, preferred_element_type=jnp.float32)

            dq_rot = (dq_sum[...].T * SCORE_SCALE).astype(jnp.bfloat16)
            for head in range(group):
                dq_refs[flip][
                    step * block_len : (step + 1) * block_len,
                    head * HEAD_SIZE : (head + 1) * HEAD_SIZE,
                ] = dq_rot[head * block_len : (head + 1) * block_len, :]

    def unsort(slab, unit, row, at):
        kind = part_refs[slab].dtype
        here = pl.ds(row, block_len)
        part_refs[slab][unit, 0, here, :] = (dk_sum[at, :] * SCORE_SCALE).astype(kind)
        part_refs[slab][unit, 1, here, :] = dv_sum[at, :].astype(kind)

    each_block(unsort)


def turned_back(field, cosine, signed):
    return field * cosine - pltpu.roll(field, HEAD_SIZE // 2, 1) * signed


def query_gradient_kernel(members, group, where_ref, cos_ref, sin_ref, *refs):
    member = where_ref[0]
    cosine = cos_ref[...]
    signed = sin_ref[...] * half_sign()
    for flip in range(members):
        for head in range(group):
            field = refs[flip][:, head * HEAD_SIZE : (head + 1) * HEAD_SIZE].astype(jnp.float32)
            refs[members][:, head_lanes(member, flip, group, head)] = turned_back(
                field, cosine, signed
            ).astype(jnp.bfloat16)


def last_kernel(members, where_ref, cos_ref, sin_ref, *refs):
    member = where_ref[0]
    dk_ref, dv_ref = refs[members], refs[members + 1]
    cosine = cos_ref[...]
    signed = sin_ref[...] * half_sign()
    for flip in range(members):
        lanes = head_lanes(member, flip, 1, 0)
        field = refs[flip][0].astype(jnp.float32)
        dk_ref[:, lanes] = turned_back(field, cosine, signed).astype(jnp.bfloat16)
        dv_ref[:, lanes] = refs[flip][1].astype(jnp.bfloat16)


def whole(shape):
    return pl.BlockSpec(shape, lambda *_: (0,) * len(shape))


def call(kernel, name, scalars, inputs, outputs, in_specs=None, out_specs=None, scratch=(), cost=None):
    return pl.pallas_call(
        kernel,
        grid_spec=pltpu.PrefetchScalarGridSpec(
            num_scalar_prefetch=len(scalars),
            grid=(1,),
            in_specs=in_specs or [whole(a.shape) for a in inputs],
            out_specs=out_specs or [whole(shape) for shape, _ in outputs],
            scratch_shapes=list(scratch),
        ),
        out_shape=[jax.ShapeDtypeStruct(shape, kind) for shape, kind in outputs],
        compiler_params=pltpu.CompilerParams(vmem_limit_bytes=MEMORY),
        cost_estimate=cost,
        name=name,
    )(*scalars, *inputs)


def shards(
    queries, keys, values, attn_out, out_grad, logsumexp, position_ids, block_map, span_blocks
):
    rows = queries.shape[0]
    kv_heads = keys.shape[1] // HEAD_SIZE
    group = queries.shape[1] // keys.shape[1]
    block_len = rows // BLOCKS_DEV
    layers = lax.axis_size("z")
    members = 4 if kv_heads == 4 and lax.axis_size("tp") == 2 else 1
    tp_index = lax.axis_index("tp")
    layer = lax.axis_index("z")
    in_slab = lax.axis_index("y") * 2 + lax.axis_index("core")
    device = layer * 4 + in_slab
    member = in_slab if members > 1 else jnp.zeros_like(in_slab)
    place = jnp.stack([member, tp_index, layer, jnp.full_like(layer, layers), device])
    place = place.astype(jnp.int32)
    width = group * HEAD_SIZE
    bf16, f32 = jnp.bfloat16, jnp.float32

    def flipped(array, flip):
        if flip == 0:
            return array
        return lax.ppermute(array, ("y", "core"), [(i, i ^ flip) for i in range(4)])

    def climbed(array, steps):
        route = [(i, (i + steps) % layers) for i in range(layers)]
        return lax.ppermute(array, "z", route)

    every = range(members)
    table = ((rows, HEAD_SIZE), f32)
    pair = (2, rows, HEAD_SIZE)

    inputs = [position_ids, keys, values]
    outputs = [table, table] + [(pair, bf16)] * members
    in_specs = [whole(a.shape) for a in inputs]
    out_specs = [whole(shape) for shape, _ in outputs]
    scratch = []
    if members > 1:
        inputs.append(out_grad)
        in_specs.append(pl.BlockSpec(memory_space=pl.ANY))
        outputs.append(((out_grad.shape[0], members * width), bf16))
        out_specs.append(pl.BlockSpec(memory_space=pl.ANY))
        scratch = [pltpu.SemaphoreType.DMA]
    results = call(
        functools.partial(first_kernel, members, members > 1),
        "first", [place], inputs, outputs, in_specs, out_specs, scratch,
    )
    cosine, sine = results[:2]
    kv_pieces = results[2 : 2 + members]
    if members > 1:
        slab = jnp.stack([flipped(kv_pieces[f], f) for f in every])
        grads_other = lax.ppermute(results[-1], "tp", [(0, 1), (1, 0)])
        kv = [slab] + [climbed(slab, k) for k in range(1, layers)]
        slabs = layers
    else:
        kv = [lax.all_gather(kv_pieces[0], ("z", "y", "core"), axis=0, tiled=False)]
        slabs = 1
        grads_own = lax.all_to_all(out_grad, "tp", split_axis=1, concat_axis=0, tiled=True)

    q_pieces = call(
        functools.partial(query_kernel, members, group),
        "rotate", [place], [cosine, sine, queries], [((rows, width), bf16)] * members,
    )
    q_in = [flipped(q_pieces[f], f) for f in every]

    inputs = [attn_out, logsumexp]
    in_specs = [whole(a.shape) for a in inputs]
    if members > 1:
        inputs += [out_grad, grads_other]
        in_specs += [
            pl.BlockSpec(grads_other.shape, lambda i, where: (0, where[1])),
            whole(grads_other.shape),
        ]
    else:
        inputs += [grads_own]
        in_specs += [whole(grads_own.shape)]
    results = call(
        functools.partial(delta_kernel, members, group),
        "delta", [place], inputs,
        [((rows, width), bf16)] * members + [((2 * group, rows), f32)] * members,
        in_specs,
    )
    g_in = [flipped(results[f], f) for f in every]
    s_in = [flipped(results[members + f], f) for f in every]

    units = kv[0].shape[0]
    tokens = slabs * units * rows
    columns = group * block_len
    blocks = members * BLOCKS_DEV
    part = (units, 2, rows, HEAD_SIZE)
    kinds = [f32] + [bf16] * (slabs - 1) if members > 1 else [bf16]
    results = call(
        functools.partial(attend_kernel, members, group, block_len, slabs),
        "attend", [place, block_map, span_blocks.reshape(-1)],
        [*kv, *q_in, *g_in, *s_in],
        [((rows, width), bf16)] * members + [(part, kind) for kind in kinds],
        scratch=[
            pltpu.VMEM((tokens, HEAD_SIZE), bf16),
            pltpu.VMEM((tokens, HEAD_SIZE), bf16),
            pltpu.VMEM((tokens // CHUNK, HEAD_SIZE, CHUNK), bf16),
            pltpu.VMEM((blocks, columns, HEAD_SIZE), bf16),
            pltpu.VMEM((blocks, columns, HEAD_SIZE), bf16),
            pltpu.VMEM((blocks, 1, columns), f32),
            pltpu.VMEM((blocks, 1, columns), f32),
            pltpu.VMEM((tokens, HEAD_SIZE), f32),
            pltpu.VMEM((tokens, HEAD_SIZE), f32),
            pltpu.VMEM((HEAD_SIZE, columns), f32),
        ],
        cost=pl.CostEstimate(
            flops=6 * group * members * rows * tokens * HEAD_SIZE,
            bytes_accessed=6 * 1024 * 1024,
            transcendentals=group * members * rows * tokens // 2,
        ),
    )
    dq_pieces, parts = results[:members], results[members:]
    if members > 1:
        total = parts[0]
        for k in range(1, layers):
            total = total + climbed(parts[k], layers - k).astype(f32)
        sums = [flipped(total[f].astype(bf16), f) for f in every]
    else:
        sums = [
            lax.psum_scatter(parts[0], ("z", "y", "core"), scatter_dimension=0, tiled=True)[0]
        ]
    (grad_q,) = call(
        functools.partial(query_gradient_kernel, members, group),
        "turn_back", [place],
        [cosine, sine] + [flipped(dq_pieces[f], f) for f in every],
        [(queries.shape, bf16)],
    )
    key_gradient, value_gradient = call(
        functools.partial(last_kernel, members),
        "last", [place], [cosine, sine, *sums],
        [(keys.shape, bf16), (values.shape, bf16)],
    )
    return (grad_q, key_gradient, value_gradient)


def solution(mesh):
    ctx, tp = mesh.shape["ctx"], mesh.shape["tp"]
    fine = Mesh(mesh.devices.reshape(ctx // 4, 2, 2, tp), ("z", "y", "core", "tp"))
    ctx_axes = ("z", "y", "core")
    return jax.shard_map(
        shards,
        mesh=fine,
        in_specs=(
            P(ctx_axes, "tp"),
            P(ctx_axes, "tp"),
            P(ctx_axes, "tp"),
            P(ctx_axes, "tp"),
            P((*ctx_axes, "tp"), None),
            P("tp", ctx_axes),
            P(None, ctx_axes),
            P(),
            P(),
        ),
        out_specs=(P(ctx_axes, "tp"), P(ctx_axes, "tp"), P(ctx_axes, "tp")),
        check_vma=False,
    )
```

```python
import functools
import math

import jax
import jax.numpy as jnp
from jax import lax
from jax.experimental import pallas as pl
from jax.experimental.pallas import tpu as pltpu
from jax.sharding import Mesh
from jax.sharding import PartitionSpec as P

HEAD_SIZE = 128
BLOCKS_DEV = 2
THETA = 1000000.0
CHUNK = 256
SCORE_SCALE = 1.0 / math.sqrt(HEAD_SIZE)
LOG2E = math.log2(math.e)
MEMORY = 56 * 1024 * 1024


def turned_tables(ids, width):
    half = width // 2
    rows = ids.shape[1]
    pair = lax.broadcasted_iota(jnp.int32, (half, rows), 0)
    first_cut = width // 8
    second_cut = first_cut + 3 * width // 16
    inverse = jnp.exp(pair.astype(jnp.float32) * jnp.float32(-2.0 * math.log(THETA) / width))
    ids = ids.astype(jnp.float32)
    picked = jnp.where(
        pair < first_cut, ids[0:1, :], jnp.where(pair < second_cut, ids[1:2, :], ids[2:3, :])
    )
    angles = picked * inverse
    cosine = jnp.cos(angles)
    sine = jnp.sin(angles)
    return (
        jnp.concatenate([cosine, cosine], axis=0).T,
        jnp.concatenate([sine, sine], axis=0).T,
    )


def half_sign():
    lane = lax.broadcasted_iota(jnp.int32, (1, HEAD_SIZE), 1)
    return jnp.where(lane < HEAD_SIZE // 2, -1.0, 1.0).astype(jnp.float32)


def head_lanes(member, flip, heads, head):
    first = ((member ^ flip) * heads + head) * HEAD_SIZE
    return pl.ds(pl.multiple_of(first, HEAD_SIZE), HEAD_SIZE)


def first_kernel(members, with_piece, where_ref, ids_ref, k_ref, v_ref, *refs):
    refs = list(refs)
    if with_piece:
        grad_ref = refs.pop(0)
        refs.pop()[...] = grad_ref[...]
    cos_ref, sin_ref = refs.pop(0), refs.pop(0)
    member = where_ref[0]
    cosine, sine = turned_tables(ids_ref[...], HEAD_SIZE)
    cos_ref[...] = cosine
    sin_ref[...] = sine
    signed = sine * half_sign()
    for flip in range(members):
        lanes = head_lanes(member, flip, 1, 0)
        keys = k_ref[:, lanes].astype(jnp.float32)
        refs[flip][0] = (keys * cosine + pltpu.roll(keys, HEAD_SIZE // 2, 1) * signed).astype(
            jnp.bfloat16
        )
        refs[flip][1] = v_ref[:, lanes]


def stacked(head, block_len):
    return slice(head * block_len, (head + 1) * block_len)


def query_kernel(members, group, where_ref, cos_ref, sin_ref, q_ref, *out_refs):
    member = where_ref[0]
    cosine = cos_ref[...]
    signed = sin_ref[...] * half_sign()
    block_len = q_ref.shape[0] // BLOCKS_DEV
    for flip in range(members):
        for head in range(group):
            field = q_ref[:, head_lanes(member, flip, group, head)].astype(jnp.float32)
            turned = pltpu.roll(field, HEAD_SIZE // 2, 1)
            field = (field * cosine + turned * signed).astype(jnp.bfloat16)
            for step in range(BLOCKS_DEV):
                out_refs[flip][step, stacked(head, block_len), :] = field[
                    step * block_len : (step + 1) * block_len, :
                ]


def delta_kernel(members, group, where_ref, a_ref, l_ref, *refs):
    refs = list(refs)
    own_ref = refs.pop(0)
    other_ref = refs.pop(0) if members > 1 else None
    grad_refs, stat_refs = refs[:members], refs[members:]
    member, tp_index = where_ref[0], where_ref[1]
    block_len = a_ref.shape[0] // BLOCKS_DEV
    for flip in range(members):
        g_ref = grad_refs[flip]
        for head in range(group):
            lanes = head_lanes(member, flip, group, head)
            here = stacked(head, block_len)
            if members > 1:
                g_ref[tp_index, here, :] = own_ref[:, lanes]
                g_ref[1 - tp_index, here, :] = other_ref[:, lanes]
            else:
                for step in range(BLOCKS_DEV):
                    g_ref[step, here, :] = own_ref[stacked(step, block_len), lanes]
        first = pl.multiple_of((member ^ flip) * group, group)
        lse = l_ref[pl.ds(first, group), :] * LOG2E
        for step in range(BLOCKS_DEV):
            sums = []
            for head in range(group):
                lanes = head_lanes(member, flip, group, head)
                product = g_ref[step, stacked(head, block_len), :].astype(jnp.float32) * a_ref[
                    stacked(step, block_len), lanes
                ].astype(jnp.float32)
                sums.append(product)
            total = jnp.sum(jnp.concatenate(sums, axis=0).T, axis=0, keepdims=True)
            stat_refs[flip][2 * step : 2 * step + 1, :] = row_vector(lse, step, block_len)
            stat_refs[flip][2 * step + 1 : 2 * step + 2, :] = total


def row_vector(table, upper, block_len):
    group, width = table.shape
    rolled = pltpu.roll(table, block_len, 1)
    low, high = (table, rolled) if upper == 0 else (rolled, table)
    lane = lax.broadcasted_iota(jnp.int32, (1, width), 1)
    pieces = [
        jnp.where(lane < block_len, low[h : h + 1, :], high[h + 1 : h + 2, :])
        for h in range(0, group, 2)
    ]
    return jnp.concatenate(pieces, axis=1)


def attend_kernel(
    members, group, block_len, slabs, carried, carries, where_ref, map_ref, span_ref, *refs
):
    refs = list(refs)
    count = len(slabs)
    kv_refs = [refs.pop(0) for _ in range(count)]
    q_refs = [refs.pop(0) for _ in range(members)]
    g_refs = [refs.pop(0) for _ in range(members)]
    s_refs = [refs.pop(0) for _ in range(members)]
    in_ref = refs.pop(0) if carried else None
    dq_refs = [refs.pop(0) for _ in range(1 if carries else members)]
    part_refs = [refs.pop(0) for _ in range(count)]
    k_sort, v_sort, k_turn, q_all, g_all, l_all, d_all, dk_sum, dv_sum, dq_sum = refs[:10]
    dq_all, ranks, ordered = refs[10:]
    member, layer, layers, device = where_ref[0], where_ref[2], where_ref[3], where_ref[4]
    units = kv_refs[0].shape[0]
    spans = span_ref.shape[0] // 2
    columns = group * block_len
    blocks = count * units * BLOCKS_DEV
    complete = blocks == map_ref.shape[0]

    def sequence_block(slab, unit, step):
        if members > 1:
            owner = lax.rem(layer - slab + layers, layers) * members + (member ^ unit)
        else:
            owner = unit
        return map_ref[owner * BLOCKS_DEV + step]

    if complete:

        @pl.loop(0, blocks)
        def _(block):
            ordered[block] = block
            ranks[block] = map_ref[block]

        def blocks_before(bound):
            return bound
    else:
        present = [
            sequence_block(slab, unit, step)
            for slab in slabs
            for unit in range(units)
            for step in range(BLOCKS_DEV)
        ]

        def blocks_before(bound):
            return functools.reduce(jnp.add, [(b < bound).astype(jnp.int32) for b in present])

        for number, block in enumerate(present):
            rank = blocks_before(block)
            ranks[number] = rank
            ordered[rank] = block

    def each_block(body):
        for place in range(count):

            @pl.loop(0, units)
            def _(unit):
                for step in range(BLOCKS_DEV):
                    rank = ranks[(place * units + unit) * BLOCKS_DEV + step]
                    at = pl.multiple_of(rank * block_len, block_len)
                    body(place, unit, pl.ds(step * block_len, block_len), pl.ds(at, block_len))

    def sort(place, unit, row, to):
        k_sort[to, :] = kv_refs[place][unit, 0, row, :]
        v_sort[to, :] = kv_refs[place][unit, 1, row, :]

    each_block(sort)

    @pl.loop(0, k_turn.shape[0])
    def _(chunk):
        at = pl.multiple_of(chunk * CHUNK, CHUNK)
        k_turn[chunk] = k_sort[pl.ds(at, CHUNK), :].T
        dk_sum[pl.ds(at, CHUNK), :] = jnp.zeros((CHUNK, HEAD_SIZE), jnp.float32)
        dv_sum[pl.ds(at, CHUNK), :] = jnp.zeros((CHUNK, HEAD_SIZE), jnp.float32)

    for flip in range(members):
        for step in range(BLOCKS_DEV):
            place = flip * BLOCKS_DEV + step
            q_all[place] = q_refs[flip][step]
            g_all[place] = g_refs[flip][step]
            l_all[place] = s_refs[flip][2 * step : 2 * step + 1, :]
            d_all[place] = s_refs[flip][2 * step + 1 : 2 * step + 2, :]

    lane = lax.broadcasted_iota(jnp.int32, (1, columns), 1)
    within = lax.rem(lane, block_len)
    key_row = lax.broadcasted_iota(jnp.int32, (block_len, 1), 0)
    chunk_blocks = CHUNK // block_len

    @pl.loop(0, members * BLOCKS_DEV)
    def _(place):
        flip, step = place // BLOCKS_DEV, lax.rem(place, BLOCKS_DEV)
        owner = device if members == 1 else layer * members + (member ^ flip)
        block = map_ref[owner * BLOCKS_DEV + step]
        end = jnp.int32(0)
        for span in range(spans):
            inside = (block >= span_ref[2 * span]) & (block < span_ref[2 * span + 1])
            end = jnp.where(inside, span_ref[2 * span + 1], end)
        limit = jnp.where(end > 0, end * block_len, block * block_len + within + 1)
        full = blocks_before(jnp.where(end > 0, end, block)) // chunk_blocks
        seen = (blocks_before(jnp.maximum(end, block + 1)) + chunk_blocks - 1) // chunk_blocks
        dq_sum[...] = in_ref[place] if carried else jnp.zeros_like(dq_sum)

        def visit(chunk, masked):
            queries = q_all[place]
            grads = g_all[place]
            at = pl.multiple_of(chunk * CHUNK, CHUNK)
            keys = k_sort[pl.ds(at, CHUNK), :]
            values = v_sort[pl.ds(at, CHUNK), :]
            scores = lax.dot_general(
                keys, queries, (((1,), (1,)), ((), ())), preferred_element_type=jnp.float32
            )
            raised = scores * (SCORE_SCALE * LOG2E) - l_all[place]
            if masked:
                positions = jnp.concatenate(
                    [
                        key_row + ordered[chunk * chunk_blocks + i] * block_len
                        for i in range(chunk_blocks)
                    ],
                    axis=0,
                )
                raised = jnp.where(positions < limit, raised, -jnp.inf)
            probs = jnp.exp2(raised)
            grad_p = lax.dot_general(
                values, grads, (((1,), (1,)), ((), ())), preferred_element_type=jnp.float32
            )
            grad_s = (probs * (grad_p - d_all[place])).astype(jnp.bfloat16)
            dv_sum[pl.ds(at, CHUNK), :] += jnp.dot(
                probs.astype(jnp.bfloat16), grads, preferred_element_type=jnp.float32
            )
            dk_sum[pl.ds(at, CHUNK), :] += jnp.dot(
                grad_s, queries, preferred_element_type=jnp.float32
            )
            dq_sum[...] += jnp.dot(k_turn[chunk], grad_s, preferred_element_type=jnp.float32)

        pl.loop(0, full)(lambda chunk: visit(chunk, False))
        pl.loop(full, seen)(lambda chunk: visit(chunk, True))

        if carries:
            dq_refs[0][place] = dq_sum[...]
        else:
            dq_all[place] = (dq_sum[...].T * SCORE_SCALE).astype(jnp.bfloat16)

    if not carries:
        for flip in range(members):
            for step in range(BLOCKS_DEV):
                dq_refs[flip][step] = dq_all[flip * BLOCKS_DEV + step]

    def unsort(place, unit, here, at):
        kind = part_refs[place].dtype
        part_refs[place][unit, 0, here, :] = (dk_sum[at, :] * SCORE_SCALE).astype(kind)
        part_refs[place][unit, 1, here, :] = dv_sum[at, :].astype(kind)

    each_block(unsort)


def turned_back(field, cosine, signed):
    return field * cosine - pltpu.roll(field, HEAD_SIZE // 2, 1) * signed


def query_gradient_kernel(members, group, where_ref, cos_ref, sin_ref, *refs):
    member = where_ref[0]
    block_len = cos_ref.shape[0] // BLOCKS_DEV
    for step in range(BLOCKS_DEV):
        here = slice(step * block_len, (step + 1) * block_len)
        cosine = cos_ref[here, :]
        signed = sin_ref[here, :] * half_sign()
        for flip in range(members):
            for head in range(group):
                field = refs[flip][step, stacked(head, block_len), :].astype(jnp.float32)
                refs[members][here, head_lanes(member, flip, group, head)] = turned_back(
                    field, cosine, signed
                ).astype(jnp.bfloat16)


def last_kernel(members, where_ref, cos_ref, sin_ref, *refs):
    member = where_ref[0]
    dk_ref, dv_ref = refs[members], refs[members + 1]
    cosine = cos_ref[...]
    signed = sin_ref[...] * half_sign()
    for flip in range(members):
        lanes = head_lanes(member, flip, 1, 0)
        field = refs[flip][0].astype(jnp.float32)
        dk_ref[:, lanes] = turned_back(field, cosine, signed).astype(jnp.bfloat16)
        dv_ref[:, lanes] = refs[flip][1].astype(jnp.bfloat16)


def whole(shape):
    return pl.BlockSpec(shape, lambda *_: (0,) * len(shape))


def call(kernel, name, scalars, inputs, outputs, in_specs=None, out_specs=None, scratch=(), cost=None):
    return pl.pallas_call(
        kernel,
        grid_spec=pltpu.PrefetchScalarGridSpec(
            num_scalar_prefetch=len(scalars),
            grid=(1,),
            in_specs=in_specs or [whole(a.shape) for a in inputs],
            out_specs=out_specs or [whole(shape) for shape, _ in outputs],
            scratch_shapes=list(scratch),
        ),
        out_shape=[jax.ShapeDtypeStruct(shape, kind) for shape, kind in outputs],
        compiler_params=pltpu.CompilerParams(vmem_limit_bytes=MEMORY),
        cost_estimate=cost,
        name=name,
    )(*scalars, *inputs)


def shards(
    queries, keys, values, attn_out, out_grad, logsumexp, position_ids, block_map, span_blocks
):
    rows = queries.shape[0]
    kv_heads = keys.shape[1] // HEAD_SIZE
    group = queries.shape[1] // keys.shape[1]
    block_len = rows // BLOCKS_DEV
    layers = lax.axis_size("z")
    members = 4 if kv_heads == 4 and lax.axis_size("tp") == 2 else 1
    tp_index = lax.axis_index("tp")
    layer = lax.axis_index("z")
    in_slab = lax.axis_index("y") * 2 + lax.axis_index("core")
    device = layer * 4 + in_slab
    member = in_slab if members > 1 else jnp.zeros_like(in_slab)
    place = jnp.stack([member, tp_index, layer, jnp.full_like(layer, layers), device])
    place = place.astype(jnp.int32)
    width = group * HEAD_SIZE
    bf16, f32 = jnp.bfloat16, jnp.float32

    def flipped(array, flip):
        if flip == 0:
            return array
        return lax.ppermute(array, ("y", "core"), [(i, i ^ flip) for i in range(4)])

    def climbed(array, steps):
        route = [(i, (i + steps) % layers) for i in range(layers)]
        return lax.ppermute(array, "z", route)

    every = range(members)
    table = ((rows, HEAD_SIZE), f32)
    pair = (2, rows, HEAD_SIZE)

    inputs = [position_ids, keys, values]
    outputs = [table, table] + [(pair, bf16)] * members
    in_specs = [whole(a.shape) for a in inputs]
    if members > 1:
        other = (out_grad.shape[0], members * width)
        inputs.append(out_grad)
        in_specs.append(pl.BlockSpec(other, lambda i, where: (0, 1 - where[1])))
        outputs.append((other, bf16))
    results = call(
        functools.partial(first_kernel, members, members > 1),
        "first", [place], inputs, outputs, in_specs,
    )
    cosine, sine = results[:2]
    kv_pieces = results[2 : 2 + members]
    columns = group * block_len
    stack = (BLOCKS_DEV, columns, HEAD_SIZE)
    q_pieces = call(
        functools.partial(query_kernel, members, group),
        "rotate", [place], [cosine, sine, queries], [(stack, bf16)] * members,
    )
    if members > 1:
        slab = jnp.stack([flipped(kv_pieces[f], f) for f in every])
        grads_other = lax.ppermute(results[-1], "tp", [(0, 1), (1, 0)])
        far = sorted(range(1, layers), key=lambda k: abs(2 * k - layers))
        rounds = [far[: layers // 2], far[layers // 2 :] + [0]]
        slab, *q_pieces = lax.optimization_barrier((slab, *q_pieces))
        kv = {0: slab}
        for k in far:
            kv[k] = climbed(slab, k)
    else:
        kv = {0: lax.all_gather(kv_pieces[0], ("z", "y", "core"), axis=0, tiled=False)}
        rounds = [[0]]
        grads_own = lax.all_to_all(out_grad, "tp", split_axis=1, concat_axis=0, tiled=True)
    q_in = [flipped(q_pieces[f], f) for f in every]

    inputs = [attn_out, logsumexp]
    in_specs = [whole(a.shape) for a in inputs]
    if members > 1:
        inputs += [out_grad, grads_other]
        in_specs += [
            pl.BlockSpec(grads_other.shape, lambda i, where: (0, where[1])),
            whole(grads_other.shape),
        ]
    else:
        inputs += [grads_own]
        in_specs += [whole(grads_own.shape)]
    results = call(
        functools.partial(delta_kernel, members, group),
        "delta", [place], inputs,
        [(stack, bf16)] * members + [((2 * BLOCKS_DEV, columns), f32)] * members,
        in_specs,
    )
    g_in = [flipped(results[f], f) for f in every]
    s_in = [flipped(results[members + f], f) for f in every]

    units = kv[0].shape[0]
    blocks = members * BLOCKS_DEV
    part = (units, 2, rows, HEAD_SIZE)
    sums = (blocks, HEAD_SIZE, columns)
    parts = {}
    carry = []
    for number, slabs in enumerate(rounds):
        tokens = len(slabs) * units * rows
        carries = number < len(rounds) - 1
        results = call(
            functools.partial(
                attend_kernel, members, group, block_len, slabs, number > 0, carries
            ),
            "attend", [place, block_map, span_blocks.reshape(-1)],
            [*[kv[k] for k in slabs], *q_in, *g_in, *s_in, *carry],
            ([(sums, f32)] if carries else [(stack, bf16)] * members)
            + [(part, f32 if k == 0 and members > 1 else bf16) for k in slabs],
            scratch=[
                pltpu.VMEM((tokens, HEAD_SIZE), bf16),
                pltpu.VMEM((tokens, HEAD_SIZE), bf16),
                pltpu.VMEM((tokens // CHUNK, HEAD_SIZE, CHUNK), bf16),
                pltpu.VMEM((blocks, columns, HEAD_SIZE), bf16),
                pltpu.VMEM((blocks, columns, HEAD_SIZE), bf16),
                pltpu.VMEM((blocks, 1, columns), f32),
                pltpu.VMEM((blocks, 1, columns), f32),
                pltpu.VMEM((tokens, HEAD_SIZE), f32),
                pltpu.VMEM((tokens, HEAD_SIZE), f32),
                pltpu.VMEM((HEAD_SIZE, columns), f32),
                pltpu.VMEM((blocks, columns, HEAD_SIZE), bf16),
                pltpu.SMEM((tokens // block_len,), jnp.int32),
                pltpu.SMEM((tokens // block_len,), jnp.int32),
            ],
            cost=pl.CostEstimate(
                flops=6 * group * members * rows * tokens * HEAD_SIZE,
                bytes_accessed=6 * 1024 * 1024,
                transcendentals=group * members * rows * tokens // 2,
            ),
        )
        outs = 1 if carries else members
        carry = results[:outs]
        parts.update(zip(slabs, results[outs:]))
    dq_pieces = carry
    if members > 1:
        total = parts[0]
        for k in far:
            total = total + climbed(parts[k], layers - k).astype(f32)
        sums = [flipped(total[f].astype(bf16), f) for f in every]
    else:
        sums = [
            lax.psum_scatter(parts[0], ("z", "y", "core"), scatter_dimension=0, tiled=True)[0]
        ]
    (grad_q,) = call(
        functools.partial(query_gradient_kernel, members, group),
        "turn_back", [place],
        [cosine, sine] + [flipped(dq_pieces[f], f) for f in every],
        [(queries.shape, bf16)],
    )
    key_gradient, value_gradient = call(
        functools.partial(last_kernel, members),
        "last", [place], [cosine, sine, *sums],
        [(keys.shape, bf16), (values.shape, bf16)],
    )
    return (grad_q, key_gradient, value_gradient)


def solution(mesh):
    ctx, tp = mesh.shape["ctx"], mesh.shape["tp"]
    fine = Mesh(mesh.devices.reshape(ctx // 4, 2, 2, tp), ("z", "y", "core", "tp"))
    ctx_axes = ("z", "y", "core")
    return jax.shard_map(
        shards,
        mesh=fine,
        in_specs=(
            P(ctx_axes, "tp"),
            P(ctx_axes, "tp"),
            P(ctx_axes, "tp"),
            P(ctx_axes, "tp"),
            P((*ctx_axes, "tp"), None),
            P("tp", ctx_axes),
            P(None, ctx_axes),
            P(),
            P(),
        ),
        out_specs=(P(ctx_axes, "tp"), P(ctx_axes, "tp"), P(ctx_axes, "tp")),
        check_vma=False,
    )
```

```python
import functools
import math

import jax
import jax.numpy as jnp
from jax import lax
from jax.experimental import pallas as pl
from jax.experimental.pallas import tpu as pltpu
from jax.sharding import Mesh
from jax.sharding import PartitionSpec as P

HEAD_SIZE = 128
BLOCKS_DEV = 2
THETA = 1000000.0
CHUNK = 256
WIDE = 512
STAT_ROWS = 32
SCORE_SCALE = 1.0 / math.sqrt(HEAD_SIZE)
LOG2E = math.log2(math.e)
MEMORY = 56 * 1024 * 1024


def turned_tables(ids, width):
    half = width // 2
    rows = ids.shape[1]
    pair = lax.broadcasted_iota(jnp.int32, (half, rows), 0)
    first_cut = width // 8
    second_cut = first_cut + 3 * width // 16
    inverse = jnp.exp(pair.astype(jnp.float32) * jnp.float32(-2.0 * math.log(THETA) / width))
    ids = ids.astype(jnp.float32)
    picked = jnp.where(
        pair < first_cut, ids[0:1, :], jnp.where(pair < second_cut, ids[1:2, :], ids[2:3, :])
    )
    angles = picked * inverse
    cosine = jnp.cos(angles)
    sine = jnp.sin(angles)
    return (
        jnp.concatenate([cosine, cosine], axis=0).T,
        jnp.concatenate([sine, sine], axis=0).T,
    )


def half_sign():
    lane = lax.broadcasted_iota(jnp.int32, (1, HEAD_SIZE), 1)
    return jnp.where(lane < HEAD_SIZE // 2, -1.0, 1.0).astype(jnp.float32)


def head_lanes(member, flip, heads, head):
    first = ((member ^ flip) * heads + head) * HEAD_SIZE
    return pl.ds(pl.multiple_of(first, HEAD_SIZE), HEAD_SIZE)


def first_kernel(members, with_piece, where_ref, ids_ref, k_ref, v_ref, *refs):
    refs = list(refs)
    if with_piece:
        grad_ref = refs.pop(0)
        refs.pop()[...] = grad_ref[...]
    cos_ref, sin_ref = refs.pop(0), refs.pop(0)
    member = where_ref[0]
    cosine, sine = turned_tables(ids_ref[...], HEAD_SIZE)
    cos_ref[...] = cosine
    sin_ref[...] = sine
    signed = sine * half_sign()
    for flip in range(members):
        lanes = head_lanes(member, flip, 1, 0)
        keys = k_ref[:, lanes].astype(jnp.float32)
        refs[flip][0] = (keys * cosine + pltpu.roll(keys, HEAD_SIZE // 2, 1) * signed).astype(
            jnp.bfloat16
        )
        refs[flip][1] = v_ref[:, lanes]


def stacked(head, block_len):
    return slice(head * block_len, (head + 1) * block_len)


def query_kernel(members, group, cos_ref, sin_ref, q_ref, out_ref):
    cosine = cos_ref[...]
    signed = sin_ref[...] * half_sign()
    block_len = q_ref.shape[0] // BLOCKS_DEV
    for member in range(members):
        for head in range(group):
            first = (member * group + head) * HEAD_SIZE
            field = q_ref[:, first : first + HEAD_SIZE].astype(jnp.float32)
            turned = pltpu.roll(field, HEAD_SIZE // 2, 1)
            field = (field * cosine + turned * signed).astype(jnp.bfloat16)
            for step in range(BLOCKS_DEV):
                out_ref[member, step, stacked(head, block_len), :] = field[
                    step * block_len : (step + 1) * block_len, :
                ]


def split_rows(vector):
    pieces = []
    for _ in range(3):
        addend = vector.astype(jnp.bfloat16).astype(jnp.float32)
        vector = vector - addend
        pieces += [
            addend[:, i : i + HEAD_SIZE] for i in range(0, addend.shape[1], HEAD_SIZE)
        ]
    return pieces


def joined_row(rows):
    count = rows.shape[0] // 3
    total = rows[:count] + rows[count : 2 * count] + rows[2 * count :]
    return jnp.concatenate([total[i : i + 1] for i in range(count)], axis=1)


def delta_kernel(members, group, where_ref, a_ref, l_ref, *refs):
    refs = list(refs)
    own_ref = refs.pop(0)
    other_ref = refs.pop(0) if members > 1 else None
    grad_refs = refs
    member, tp_index = where_ref[0], where_ref[1]
    block_len = a_ref.shape[0] // BLOCKS_DEV
    for flip in range(members):
        g_ref = grad_refs[flip]
        for head in range(group):
            lanes = head_lanes(member, flip, group, head)
            here = stacked(head, block_len)
            if members > 1:
                g_ref[tp_index, here, :] = own_ref[:, lanes]
                g_ref[1 - tp_index, here, :] = other_ref[:, lanes]
            else:
                for step in range(BLOCKS_DEV):
                    g_ref[step, here, :] = own_ref[stacked(step, block_len), lanes]
        first = pl.multiple_of((member ^ flip) * group, group)
        lse = l_ref[pl.ds(first, group), :] * LOG2E
        for step in range(BLOCKS_DEV):
            sums = []
            for head in range(group):
                lanes = head_lanes(member, flip, group, head)
                product = g_ref[step, stacked(head, block_len), :].astype(jnp.float32) * a_ref[
                    stacked(step, block_len), lanes
                ].astype(jnp.float32)
                sums.append(product)
            total = jnp.sum(jnp.concatenate(sums, axis=0).T, axis=0, keepdims=True)
            pieces = split_rows(row_vector(lse, step, block_len)) + split_rows(total)
            pieces.append(jnp.zeros((STAT_ROWS - len(pieces), HEAD_SIZE), jnp.float32))
            below = group * block_len
            g_ref[step, below : below + STAT_ROWS, :] = jnp.concatenate(pieces, axis=0).astype(
                jnp.bfloat16
            )


def row_vector(table, upper, block_len):
    group, width = table.shape
    rolled = pltpu.roll(table, block_len, 1)
    low, high = (table, rolled) if upper == 0 else (rolled, table)
    lane = lax.broadcasted_iota(jnp.int32, (1, width), 1)
    pieces = [
        jnp.where(lane < block_len, low[h : h + 1, :], high[h + 1 : h + 2, :])
        for h in range(0, group, 2)
    ]
    return jnp.concatenate(pieces, axis=1)


def attend_kernel(
    members, group, block_len, slabs, carried, carries, where_ref, map_ref, span_ref, *refs
):
    refs = list(refs)
    count = len(slabs)
    kv_refs = [refs.pop(0) for _ in range(count)]
    q_ref = refs.pop(0)
    g_refs = [refs.pop(0) for _ in range(members)]
    in_ref = refs.pop(0) if carried else None
    dq_refs = [refs.pop(0) for _ in range(1 if carries else members)]
    part_refs = [refs.pop(0) for _ in range(count)]
    k_sort, v_sort, k_turn, q_all, g_all, l_all, d_all, dk_sum, dv_sum, dq_sum = refs[:10]
    dq_all, ranks, ordered = refs[10:]
    member, layer, layers, device = where_ref[0], where_ref[2], where_ref[3], where_ref[4]
    units = kv_refs[0].shape[0]
    spans = span_ref.shape[0] // 2
    columns = group * block_len
    blocks = count * units * BLOCKS_DEV
    complete = blocks == map_ref.shape[0]

    def sequence_block(slab, unit, step):
        if members > 1:
            owner = lax.rem(layer - slab + layers, layers) * members + (member ^ unit)
        else:
            owner = unit
        return map_ref[owner * BLOCKS_DEV + step]

    if complete:

        @pl.loop(0, blocks)
        def _(block):
            ordered[block] = block
            ranks[block] = map_ref[block]

        def blocks_before(bound):
            return bound
    else:
        present = [
            sequence_block(slab, unit, step)
            for slab in slabs
            for unit in range(units)
            for step in range(BLOCKS_DEV)
        ]

        def blocks_before(bound):
            return functools.reduce(jnp.add, [(b < bound).astype(jnp.int32) for b in present])

        for number, block in enumerate(present):
            rank = blocks_before(block)
            ranks[number] = rank
            ordered[rank] = block

    def each_block(body):
        for place in range(count):

            @pl.loop(0, units)
            def _(unit):
                for step in range(BLOCKS_DEV):
                    rank = ranks[(place * units + unit) * BLOCKS_DEV + step]
                    at = pl.multiple_of(rank * block_len, block_len)
                    body(place, unit, pl.ds(step * block_len, block_len), pl.ds(at, block_len))

    def sort(place, unit, row, to):
        k_sort[to, :] = kv_refs[place][unit, 0, row, :]
        v_sort[to, :] = kv_refs[place][unit, 1, row, :]

    each_block(sort)

    @pl.loop(0, k_turn.shape[0])
    def _(chunk):
        at = pl.multiple_of(chunk * CHUNK, CHUNK)
        k_turn[chunk] = k_sort[pl.ds(at, CHUNK), :].T
        dk_sum[pl.ds(at, CHUNK), :] = jnp.zeros((CHUNK, HEAD_SIZE), jnp.float32)
        dv_sum[pl.ds(at, CHUNK), :] = jnp.zeros((CHUNK, HEAD_SIZE), jnp.float32)

    for flip in range(members):
        for step in range(BLOCKS_DEV):
            place = flip * BLOCKS_DEV + step
            q_all[place] = q_ref[member ^ flip, step]
            g_all[place] = g_refs[flip][step, :columns, :]
            stats = g_refs[flip][step, columns:, :].astype(jnp.float32)
            half = 3 * columns // HEAD_SIZE
            l_all[place] = joined_row(stats[:half])
            d_all[place] = joined_row(stats[half : 2 * half])

    lane = lax.broadcasted_iota(jnp.int32, (1, columns), 1)
    within = lax.rem(lane, block_len)
    key_row = lax.broadcasted_iota(jnp.int32, (block_len, 1), 0)
    chunk_blocks = CHUNK // block_len

    @pl.loop(0, members * BLOCKS_DEV)
    def _(place):
        flip, step = place // BLOCKS_DEV, lax.rem(place, BLOCKS_DEV)
        owner = device if members == 1 else layer * members + (member ^ flip)
        block = map_ref[owner * BLOCKS_DEV + step]
        end = jnp.int32(0)
        for span in range(spans):
            inside = (block >= span_ref[2 * span]) & (block < span_ref[2 * span + 1])
            end = jnp.where(inside, span_ref[2 * span + 1], end)
        limit = jnp.where(end > 0, end * block_len, block * block_len + within + 1)
        full = blocks_before(jnp.where(end > 0, end, block)) // chunk_blocks
        seen = (blocks_before(jnp.maximum(end, block + 1)) + chunk_blocks - 1) // chunk_blocks
        dq_sum[...] = in_ref[place] if carried else jnp.zeros_like(dq_sum)

        def visit(chunk, size, masked):
            queries = q_all[place]
            grads = g_all[place]
            at = pl.multiple_of(chunk * CHUNK, CHUNK)
            keys = k_sort[pl.ds(at, size), :]
            values = v_sort[pl.ds(at, size), :]
            scores = lax.dot_general(
                keys, queries, (((1,), (1,)), ((), ())), preferred_element_type=jnp.float32
            )
            raised = scores * (SCORE_SCALE * LOG2E) - l_all[place]
            if masked:
                positions = jnp.concatenate(
                    [
                        key_row + ordered[chunk * chunk_blocks + i] * block_len
                        for i in range(chunk_blocks)
                    ],
                    axis=0,
                )
                raised = jnp.where(positions < limit, raised, -jnp.inf)
            probs = jnp.exp2(raised)
            grad_p = lax.dot_general(
                values, grads, (((1,), (1,)), ((), ())), preferred_element_type=jnp.float32
            )
            grad_s = (probs * (grad_p - d_all[place])).astype(jnp.bfloat16)
            dv_sum[pl.ds(at, size), :] += jnp.dot(
                probs.astype(jnp.bfloat16), grads, preferred_element_type=jnp.float32
            )
            dk_sum[pl.ds(at, size), :] += jnp.dot(
                grad_s, queries, preferred_element_type=jnp.float32
            )
            turned = [k_turn[chunk + i] for i in range(size // CHUNK)]
            dq_sum[...] += jnp.dot(
                jnp.concatenate(turned, axis=1), grad_s, preferred_element_type=jnp.float32
            )

        pairs = full // 2
        pl.loop(0, pairs)(lambda pair: visit(2 * pair, WIDE, False))
        pl.loop(2 * pairs, full)(lambda chunk: visit(chunk, CHUNK, False))
        pl.loop(full, seen)(lambda chunk: visit(chunk, CHUNK, True))

        if carries:
            dq_refs[0][place] = dq_sum[...]
        else:
            dq_all[place] = (dq_sum[...].T * SCORE_SCALE).astype(jnp.bfloat16)

    if not carries:
        for flip in range(members):
            for step in range(BLOCKS_DEV):
                dq_refs[flip][step] = dq_all[flip * BLOCKS_DEV + step]

    def unsort(place, unit, here, at):
        kind = part_refs[place].dtype
        part_refs[place][unit, 0, here, :] = (dk_sum[at, :] * SCORE_SCALE).astype(kind)
        part_refs[place][unit, 1, here, :] = dv_sum[at, :].astype(kind)

    each_block(unsort)


def turned_back(field, cosine, signed):
    return field * cosine - pltpu.roll(field, HEAD_SIZE // 2, 1) * signed


def query_gradient_kernel(members, group, where_ref, cos_ref, sin_ref, *refs):
    member = where_ref[0]
    block_len = cos_ref.shape[0] // BLOCKS_DEV
    for step in range(BLOCKS_DEV):
        here = slice(step * block_len, (step + 1) * block_len)
        cosine = cos_ref[here, :]
        signed = sin_ref[here, :] * half_sign()
        for flip in range(members):
            for head in range(group):
                field = refs[flip][step, stacked(head, block_len), :].astype(jnp.float32)
                refs[members][here, head_lanes(member, flip, group, head)] = turned_back(
                    field, cosine, signed
                ).astype(jnp.bfloat16)


def last_kernel(members, where_ref, cos_ref, sin_ref, *refs):
    member = where_ref[0]
    dk_ref, dv_ref = refs[members], refs[members + 1]
    cosine = cos_ref[...]
    signed = sin_ref[...] * half_sign()
    for flip in range(members):
        lanes = head_lanes(member, flip, 1, 0)
        field = refs[flip][0].astype(jnp.float32)
        dk_ref[:, lanes] = turned_back(field, cosine, signed).astype(jnp.bfloat16)
        dv_ref[:, lanes] = refs[flip][1].astype(jnp.bfloat16)


def whole(shape):
    return pl.BlockSpec(shape, lambda *_: (0,) * len(shape))


def call(kernel, name, scalars, inputs, outputs, in_specs=None, out_specs=None, scratch=(), cost=None):
    return pl.pallas_call(
        kernel,
        grid_spec=pltpu.PrefetchScalarGridSpec(
            num_scalar_prefetch=len(scalars),
            grid=(1,),
            in_specs=in_specs or [whole(a.shape) for a in inputs],
            out_specs=out_specs or [whole(shape) for shape, _ in outputs],
            scratch_shapes=list(scratch),
        ),
        out_shape=[jax.ShapeDtypeStruct(shape, kind) for shape, kind in outputs],
        compiler_params=pltpu.CompilerParams(vmem_limit_bytes=MEMORY),
        cost_estimate=cost,
        name=name,
    )(*scalars, *inputs)


def shards(
    queries, keys, values, attn_out, out_grad, logsumexp, position_ids, block_map, span_blocks
):
    rows = queries.shape[0]
    kv_heads = keys.shape[1] // HEAD_SIZE
    group = queries.shape[1] // keys.shape[1]
    block_len = rows // BLOCKS_DEV
    layers = lax.axis_size("z")
    members = 4 if kv_heads == 4 and lax.axis_size("tp") == 2 else 1
    tp_index = lax.axis_index("tp")
    layer = lax.axis_index("z")
    in_slab = lax.axis_index("y") * 2 + lax.axis_index("core")
    device = layer * 4 + in_slab
    member = in_slab if members > 1 else jnp.zeros_like(in_slab)
    place = jnp.stack([member, tp_index, layer, jnp.full_like(layer, layers), device])
    place = place.astype(jnp.int32)
    width = group * HEAD_SIZE
    bf16, f32 = jnp.bfloat16, jnp.float32

    def flipped(array, flip):
        if flip == 0:
            return array
        return lax.ppermute(array, ("y", "core"), [(i, i ^ flip) for i in range(4)])

    def climbed(array, steps):
        route = [(i, (i + steps) % layers) for i in range(layers)]
        return lax.ppermute(array, "z", route)

    every = range(members)
    table = ((rows, HEAD_SIZE), f32)
    pair = (2, rows, HEAD_SIZE)

    inputs = [position_ids, keys, values]
    outputs = [table, table] + [(pair, bf16)] * members
    in_specs = [whole(a.shape) for a in inputs]
    if members > 1:
        other = (out_grad.shape[0], members * width)
        inputs.append(out_grad)
        in_specs.append(pl.BlockSpec(other, lambda i, where: (0, 1 - where[1])))
        outputs.append((other, bf16))
    results = call(
        functools.partial(first_kernel, members, members > 1),
        "first", [place], inputs, outputs, in_specs,
    )
    cosine, sine = results[:2]
    kv_pieces = results[2 : 2 + members]
    columns = group * block_len
    stack = (BLOCKS_DEV, columns, HEAD_SIZE)
    (q_stack,) = call(
        functools.partial(query_kernel, members, group),
        "rotate", [], [cosine, sine, queries], [((members, *stack), bf16)],
    )
    if members > 1:
        slab = jnp.stack([flipped(kv_pieces[f], f) for f in every])
        grads_other = lax.ppermute(results[-1], "tp", [(0, 1), (1, 0)])
        far = sorted(range(1, layers), key=lambda k: abs(2 * k - layers))
        rounds = [far[: layers // 2], far[layers // 2 :] + [0]]
        q_stack = lax.all_to_all(q_stack, ("y", "core"), 0, 0, tiled=True)
        kv = {0: slab}
        for k in far:
            kv[k] = climbed(slab, k)
    else:
        kv = {0: lax.all_gather(kv_pieces[0], ("z", "y", "core"), axis=0, tiled=False)}
        rounds = [[0]]
        grads_own = lax.all_to_all(out_grad, "tp", split_axis=1, concat_axis=0, tiled=True)

    inputs = [attn_out, logsumexp]
    in_specs = [whole(a.shape) for a in inputs]
    if members > 1:
        inputs += [out_grad, grads_other]
        in_specs += [
            pl.BlockSpec(grads_other.shape, lambda i, where: (0, where[1])),
            whole(grads_other.shape),
        ]
    else:
        inputs += [grads_own]
        in_specs += [whole(grads_own.shape)]
    results = call(
        functools.partial(delta_kernel, members, group),
        "delta", [place], inputs,
        [((BLOCKS_DEV, columns + STAT_ROWS, HEAD_SIZE), bf16)] * members,
        in_specs,
    )
    g_in = [flipped(results[f], f) for f in every]

    units = kv[0].shape[0]
    blocks = members * BLOCKS_DEV
    part = (units, 2, rows, HEAD_SIZE)
    sums = (blocks, HEAD_SIZE, columns)
    parts = {}
    carry = []
    for number, slabs in enumerate(rounds):
        tokens = len(slabs) * units * rows
        carries = number < len(rounds) - 1
        results = call(
            functools.partial(
                attend_kernel, members, group, block_len, slabs, number > 0, carries
            ),
            "attend", [place, block_map, span_blocks.reshape(-1)],
            [*[kv[k] for k in slabs], q_stack, *g_in, *carry],
            ([(sums, f32)] if carries else [(stack, bf16)] * members)
            + [(part, f32 if k == 0 and members > 1 else bf16) for k in slabs],
            scratch=[
                pltpu.VMEM((tokens, HEAD_SIZE), bf16),
                pltpu.VMEM((tokens, HEAD_SIZE), bf16),
                pltpu.VMEM((tokens // CHUNK, HEAD_SIZE, CHUNK), bf16),
                pltpu.VMEM((blocks, columns, HEAD_SIZE), bf16),
                pltpu.VMEM((blocks, columns, HEAD_SIZE), bf16),
                pltpu.VMEM((blocks, 1, columns), f32),
                pltpu.VMEM((blocks, 1, columns), f32),
                pltpu.VMEM((tokens, HEAD_SIZE), f32),
                pltpu.VMEM((tokens, HEAD_SIZE), f32),
                pltpu.VMEM((HEAD_SIZE, columns), f32),
                pltpu.VMEM((blocks, columns, HEAD_SIZE), bf16),
                pltpu.SMEM((tokens // block_len,), jnp.int32),
                pltpu.SMEM((tokens // block_len,), jnp.int32),
            ],
            cost=pl.CostEstimate(
                flops=6 * group * members * rows * tokens * HEAD_SIZE,
                bytes_accessed=6 * 1024 * 1024,
                transcendentals=group * members * rows * tokens // 2,
            ),
        )
        outs = 1 if carries else members
        carry = results[:outs]
        parts.update(zip(slabs, results[outs:]))
        if carries:
            home = {k: climbed(parts[k], layers - k) for k in slabs}
    dq_pieces = carry
    if members > 1:
        carry, home, late = lax.optimization_barrier(
            (carry, home, {k: parts[k] for k in rounds[-1]})
        )
        dq_pieces, total = carry, late.pop(0)
        home.update({k: climbed(late[k], layers - k) for k in late})
        for k in far:
            total = total + home[k].astype(f32)
        sums = [flipped(total[f].astype(bf16), f) for f in every]
    else:
        sums = [
            lax.psum_scatter(parts[0], ("z", "y", "core"), scatter_dimension=0, tiled=True)[0]
        ]
    (grad_q,) = call(
        functools.partial(query_gradient_kernel, members, group),
        "turn_back", [place],
        [cosine, sine] + [flipped(dq_pieces[f], f) for f in every],
        [(queries.shape, bf16)],
    )
    key_gradient, value_gradient = call(
        functools.partial(last_kernel, members),
        "last", [place], [cosine, sine, *sums],
        [(keys.shape, bf16), (values.shape, bf16)],
    )
    return (grad_q, key_gradient, value_gradient)


def solution(mesh):
    ctx, tp = mesh.shape["ctx"], mesh.shape["tp"]
    fine = Mesh(mesh.devices.reshape(ctx // 4, 2, 2, tp), ("z", "y", "core", "tp"))
    ctx_axes = ("z", "y", "core")
    return jax.shard_map(
        shards,
        mesh=fine,
        in_specs=(
            P(ctx_axes, "tp"),
            P(ctx_axes, "tp"),
            P(ctx_axes, "tp"),
            P(ctx_axes, "tp"),
            P((*ctx_axes, "tp"), None),
            P("tp", ctx_axes),
            P(None, ctx_axes),
            P(),
            P(),
        ),
        out_specs=(P(ctx_axes, "tp"), P(ctx_axes, "tp"), P(ctx_axes, "tp")),
        check_vma=False,
    )
```

```python
import functools
import math

import jax
import jax.numpy as jnp
from jax import lax
from jax.experimental import pallas as pl
from jax.experimental.pallas import tpu as pltpu
from jax.sharding import Mesh
from jax.sharding import PartitionSpec as P

HEAD_SIZE = 128
BLOCKS_DEV = 2
THETA = 1000000.0
CHUNK = 256
WIDE = 512
STAT_ROWS = 32
SCORE_SCALE = 1.0 / math.sqrt(HEAD_SIZE)
LOG2E = math.log2(math.e)
MEMORY = 56 * 1024 * 1024


def turned_tables(ids, width):
    half = width // 2
    rows = ids.shape[1]
    pair = lax.broadcasted_iota(jnp.int32, (half, rows), 0)
    first_cut = width // 8
    second_cut = first_cut + 3 * width // 16
    inverse = jnp.exp(pair.astype(jnp.float32) * jnp.float32(-2.0 * math.log(THETA) / width))
    ids = ids.astype(jnp.float32)
    picked = jnp.where(
        pair < first_cut, ids[0:1, :], jnp.where(pair < second_cut, ids[1:2, :], ids[2:3, :])
    )
    angles = picked * inverse
    cosine = jnp.cos(angles)
    sine = jnp.sin(angles)
    return (
        jnp.concatenate([cosine, cosine], axis=0).T,
        jnp.concatenate([sine, sine], axis=0).T,
    )


def half_sign():
    lane = lax.broadcasted_iota(jnp.int32, (1, HEAD_SIZE), 1)
    return jnp.where(lane < HEAD_SIZE // 2, -1.0, 1.0).astype(jnp.float32)


def head_lanes(member, flip, heads, head):
    first = ((member ^ flip) * heads + head) * HEAD_SIZE
    return pl.ds(pl.multiple_of(first, HEAD_SIZE), HEAD_SIZE)


def first_kernel(members, group, where_ref, ids_ref, k_ref, v_ref, q_ref, *refs):
    refs = list(refs)
    if members > 1:
        own_ref, other_ref = refs.pop(0), refs.pop(0)
        refs.pop()[...] = other_ref[...]
    pack_ref = refs.pop()
    cos_ref, sin_ref = refs.pop(0), refs.pop(0)
    this = where_ref[0]
    cosine, sine = turned_tables(ids_ref[...], HEAD_SIZE)
    cos_ref[...] = cosine
    sin_ref[...] = sine
    signed = sine * half_sign()
    block_len = q_ref.shape[0] // BLOCKS_DEV
    for flip in range(members):
        lanes = head_lanes(this, flip, 1, 0)
        keys = k_ref[:, lanes].astype(jnp.float32)
        refs[flip][0] = (keys * cosine + pltpu.roll(keys, HEAD_SIZE // 2, 1) * signed).astype(
            jnp.bfloat16
        )
        refs[flip][1] = v_ref[:, lanes]
    for member in range(members):
        for head in range(group):
            start = (member * group + head) * HEAD_SIZE
            lanes = slice(start, start + HEAD_SIZE)
            field = q_ref[:, lanes].astype(jnp.float32)
            turned = pltpu.roll(field, HEAD_SIZE // 2, 1)
            field = (field * cosine + turned * signed).astype(jnp.bfloat16)
            for step in range(BLOCKS_DEV):
                pack_ref[member, step, stacked(head, block_len), :] = field[
                    step * block_len : (step + 1) * block_len, :
                ]
            if members > 1:
                pack_ref[member, BLOCKS_DEV, stacked(head, block_len), :] = own_ref[:, lanes]


def stacked(head, block_len):
    return slice(head * block_len, (head + 1) * block_len)


def split_rows(vector):
    pieces = []
    for _ in range(3):
        addend = vector.astype(jnp.bfloat16).astype(jnp.float32)
        vector = vector - addend
        pieces += [
            addend[:, i : i + HEAD_SIZE] for i in range(0, addend.shape[1], HEAD_SIZE)
        ]
    return pieces


def joined_row(rows):
    count = rows.shape[0] // 3
    total = rows[:count] + rows[count : 2 * count] + rows[2 * count :]
    return jnp.concatenate([total[i : i + 1] for i in range(count)], axis=1)


def delta_kernel(members, group, where_ref, a_ref, l_ref, *refs):
    late_ref = refs[-1]
    block_len = a_ref.shape[0] // BLOCKS_DEV
    columns = group * block_len
    for member in range(members):
        for number in range(BLOCKS_DEV):
            if members > 1:
                step = where_ref[1] if number == 0 else 1 - where_ref[1]
                source, from_rows = refs[number], slice(None)
            else:
                step = number
                source, from_rows = refs[0], stacked(step, block_len)
            row = step * block_len
            if members > 1:
                row = pl.multiple_of(row, block_len)
            products = []
            for head in range(group):
                start = (member * group + head) * HEAD_SIZE
                lanes = slice(start, start + HEAD_SIZE)
                grad = source[from_rows, lanes]
                if members == 1:
                    late_ref[0, stacked(step * group + head, block_len), :] = grad
                elif number == 1:
                    late_ref[member, stacked(head, block_len), :] = grad
                products.append(
                    grad.astype(jnp.float32)
                    * a_ref[pl.ds(row, block_len), lanes].astype(jnp.float32)
                )
            total = jnp.sum(jnp.concatenate(products, axis=0).T, axis=0, keepdims=True)
            lse = l_ref[member * group : (member + 1) * group, :] * LOG2E
            pieces = split_rows(row_vector(lse, step, block_len)) + split_rows(total)
            pieces.append(jnp.zeros((STAT_ROWS - len(pieces), HEAD_SIZE), jnp.float32))
            below = late_ref.shape[1] - BLOCKS_DEV * STAT_ROWS + step * STAT_ROWS
            if members > 1:
                below = pl.multiple_of(below, STAT_ROWS)
            late_ref[member, pl.ds(below, STAT_ROWS), :] = jnp.concatenate(
                pieces, axis=0
            ).astype(jnp.bfloat16)


def row_vector(table, upper, block_len):
    group, width = table.shape
    rolled = pltpu.roll(table, block_len, 1)
    low = jnp.where(upper == 0, table, rolled)
    high = jnp.where(upper == 0, rolled, table)
    lane = lax.broadcasted_iota(jnp.int32, (1, width), 1)
    pieces = [
        jnp.where(lane < block_len, low[h : h + 1, :], high[h + 1 : h + 2, :])
        for h in range(0, group, 2)
    ]
    return jnp.concatenate(pieces, axis=1)


def attend_kernel(
    members, group, block_len, slabs, carried, carries, where_ref, map_ref, span_ref, *refs
):
    refs = list(refs)
    count = len(slabs)
    kv_refs = [refs.pop(0) for _ in range(count)]
    pack_ref, late_ref = refs.pop(0), refs.pop(0)
    in_ref = refs.pop(0) if carried else None
    dq_refs = [refs.pop(0) for _ in range(1 if carries else members)]
    part_refs = [refs.pop(0) for _ in range(count)]
    k_sort, v_sort, k_turn, q_all, g_all, l_all, d_all, dk_sum, dv_sum, dq_sum = refs[:10]
    dq_all, ranks, ordered = refs[10:]
    member, layer, layers, device = where_ref[0], where_ref[2], where_ref[3], where_ref[4]
    units = kv_refs[0].shape[0]
    spans = span_ref.shape[0] // 2
    columns = group * block_len
    blocks = count * units * BLOCKS_DEV
    complete = blocks == map_ref.shape[0]

    def sequence_block(slab, unit, step):
        if members > 1:
            owner = lax.rem(layer - slab + layers, layers) * members + (member ^ unit)
        else:
            owner = unit
        return map_ref[owner * BLOCKS_DEV + step]

    if complete:

        @pl.loop(0, blocks)
        def _(block):
            ordered[block] = block
            ranks[block] = map_ref[block]

        def blocks_before(bound):
            return bound
    else:
        present = [
            sequence_block(slab, unit, step)
            for slab in slabs
            for unit in range(units)
            for step in range(BLOCKS_DEV)
        ]

        def blocks_before(bound):
            return functools.reduce(jnp.add, [(b < bound).astype(jnp.int32) for b in present])

        for number, block in enumerate(present):
            rank = blocks_before(block)
            ranks[number] = rank
            ordered[rank] = block

    def each_block(body):
        for place in range(count):

            @pl.loop(0, units)
            def _(unit):
                for step in range(BLOCKS_DEV):
                    rank = ranks[(place * units + unit) * BLOCKS_DEV + step]
                    at = pl.multiple_of(rank * block_len, block_len)
                    body(place, unit, pl.ds(step * block_len, block_len), pl.ds(at, block_len))

    def sort(place, unit, row, to):
        k_sort[to, :] = kv_refs[place][unit, 0, row, :]
        v_sort[to, :] = kv_refs[place][unit, 1, row, :]

    each_block(sort)

    @pl.loop(0, k_turn.shape[0])
    def _(chunk):
        at = pl.multiple_of(chunk * CHUNK, CHUNK)
        k_turn[chunk] = k_sort[pl.ds(at, CHUNK), :].T
        dk_sum[pl.ds(at, CHUNK), :] = jnp.zeros((CHUNK, HEAD_SIZE), jnp.float32)
        dv_sum[pl.ds(at, CHUNK), :] = jnp.zeros((CHUNK, HEAD_SIZE), jnp.float32)

    for flip in range(members):
        for step in range(BLOCKS_DEV):
            place = flip * BLOCKS_DEV + step
            source = member ^ flip
            q_all[place] = pack_ref[source, step]
            if members == 1:
                g_all[place] = late_ref[0, step * columns : (step + 1) * columns, :]
            elif step == 0:
                tp_index = where_ref[1]
                g_all[flip * BLOCKS_DEV + tp_index] = pack_ref[source, BLOCKS_DEV]
                g_all[flip * BLOCKS_DEV + 1 - tp_index] = late_ref[source, :columns, :]
            half = 3 * columns // HEAD_SIZE
            below = late_ref.shape[1] - (BLOCKS_DEV - step) * STAT_ROWS
            stats = late_ref[source, below : below + STAT_ROWS, :].astype(jnp.float32)
            l_all[place] = joined_row(stats[:half])
            d_all[place] = joined_row(stats[half : 2 * half])

    lane = lax.broadcasted_iota(jnp.int32, (1, columns), 1)
    within = lax.rem(lane, block_len)
    key_row = lax.broadcasted_iota(jnp.int32, (block_len, 1), 0)
    chunk_blocks = CHUNK // block_len

    @pl.loop(0, members * BLOCKS_DEV)
    def _(place):
        flip, step = place // BLOCKS_DEV, lax.rem(place, BLOCKS_DEV)
        owner = device if members == 1 else layer * members + (member ^ flip)
        block = map_ref[owner * BLOCKS_DEV + step]
        end = jnp.int32(0)
        for span in range(spans):
            inside = (block >= span_ref[2 * span]) & (block < span_ref[2 * span + 1])
            end = jnp.where(inside, span_ref[2 * span + 1], end)
        limit = jnp.where(end > 0, end * block_len, block * block_len + within + 1)
        full = blocks_before(jnp.where(end > 0, end, block)) // chunk_blocks
        seen = (blocks_before(jnp.maximum(end, block + 1)) + chunk_blocks - 1) // chunk_blocks
        dq_sum[...] = in_ref[place] if carried else jnp.zeros_like(dq_sum)

        def visit(chunk, size, masked):
            queries = q_all[place]
            grads = g_all[place]
            at = pl.multiple_of(chunk * CHUNK, CHUNK)
            keys = k_sort[pl.ds(at, size), :]
            values = v_sort[pl.ds(at, size), :]
            scores = lax.dot_general(
                keys, queries, (((1,), (1,)), ((), ())), preferred_element_type=jnp.float32
            )
            raised = scores * (SCORE_SCALE * LOG2E) - l_all[place]
            if masked:
                positions = jnp.concatenate(
                    [
                        key_row + ordered[chunk * chunk_blocks + i] * block_len
                        for i in range(chunk_blocks)
                    ],
                    axis=0,
                )
                raised = jnp.where(positions < limit, raised, -jnp.inf)
            probs = jnp.exp2(raised)
            grad_p = lax.dot_general(
                values, grads, (((1,), (1,)), ((), ())), preferred_element_type=jnp.float32
            )
            grad_s = (probs * (grad_p - d_all[place])).astype(jnp.bfloat16)
            dv_sum[pl.ds(at, size), :] += jnp.dot(
                probs.astype(jnp.bfloat16), grads, preferred_element_type=jnp.float32
            )
            dk_sum[pl.ds(at, size), :] += jnp.dot(
                grad_s, queries, preferred_element_type=jnp.float32
            )
            turned = [k_turn[chunk + i] for i in range(size // CHUNK)]
            dq_sum[...] += jnp.dot(
                jnp.concatenate(turned, axis=1), grad_s, preferred_element_type=jnp.float32
            )

        pairs = full // 2
        pl.loop(0, pairs)(lambda pair: visit(2 * pair, WIDE, False))
        pl.loop(2 * pairs, full)(lambda chunk: visit(chunk, CHUNK, False))
        pl.loop(full, seen)(lambda chunk: visit(chunk, CHUNK, True))

        if carries:
            dq_refs[0][place] = dq_sum[...]
        else:
            dq_all[place] = (dq_sum[...].T * SCORE_SCALE).astype(jnp.bfloat16)

    if not carries:
        for flip in range(members):
            for step in range(BLOCKS_DEV):
                dq_refs[flip][step] = dq_all[flip * BLOCKS_DEV + step]

    def unsort(place, unit, here, at):
        kind = part_refs[place].dtype
        part_refs[place][unit, 0, here, :] = (dk_sum[at, :] * SCORE_SCALE).astype(kind)
        part_refs[place][unit, 1, here, :] = dv_sum[at, :].astype(kind)

    each_block(unsort)


def turned_back(field, cosine, signed):
    return field * cosine - pltpu.roll(field, HEAD_SIZE // 2, 1) * signed


def last_kernel(members, group, where_ref, cos_ref, sin_ref, *refs):
    dq_refs, sum_refs = refs[:members], refs[members : 2 * members]
    grad_ref, dk_ref, dv_ref = refs[2 * members :]
    member = where_ref[0]
    block_len = cos_ref.shape[0] // BLOCKS_DEV
    for step in range(BLOCKS_DEV):
        here = slice(step * block_len, (step + 1) * block_len)
        cosine = cos_ref[here, :]
        signed = sin_ref[here, :] * half_sign()
        for flip in range(members):
            lanes = head_lanes(member, flip, 1, 0)
            field = sum_refs[flip][0, here, :].astype(jnp.float32)
            dk_ref[here, lanes] = turned_back(field, cosine, signed).astype(jnp.bfloat16)
            dv_ref[here, lanes] = sum_refs[flip][1, here, :].astype(jnp.bfloat16)
            for head in range(group):
                field = dq_refs[flip][step, stacked(head, block_len), :].astype(jnp.float32)
                grad_ref[here, head_lanes(member, flip, group, head)] = turned_back(
                    field, cosine, signed
                ).astype(jnp.bfloat16)


def whole(shape):
    return pl.BlockSpec(shape, lambda *_: (0,) * len(shape))


def call(kernel, name, scalars, inputs, outputs, in_specs=None, out_specs=None, scratch=(), cost=None):
    return pl.pallas_call(
        kernel,
        grid_spec=pltpu.PrefetchScalarGridSpec(
            num_scalar_prefetch=len(scalars),
            grid=(1,),
            in_specs=in_specs or [whole(a.shape) for a in inputs],
            out_specs=out_specs or [whole(shape) for shape, _ in outputs],
            scratch_shapes=list(scratch),
        ),
        out_shape=[jax.ShapeDtypeStruct(shape, kind) for shape, kind in outputs],
        compiler_params=pltpu.CompilerParams(vmem_limit_bytes=MEMORY),
        cost_estimate=cost,
        name=name,
    )(*scalars, *inputs)


def shards(
    queries, keys, values, attn_out, out_grad, logsumexp, position_ids, block_map, span_blocks
):
    rows = queries.shape[0]
    kv_heads = keys.shape[1] // HEAD_SIZE
    group = queries.shape[1] // keys.shape[1]
    block_len = rows // BLOCKS_DEV
    layers = lax.axis_size("z")
    members = 4 if kv_heads == 4 and lax.axis_size("tp") == 2 else 1
    tp_index = lax.axis_index("tp")
    layer = lax.axis_index("z")
    in_slab = lax.axis_index("y") * 2 + lax.axis_index("core")
    device = layer * 4 + in_slab
    member = in_slab if members > 1 else jnp.zeros_like(in_slab)
    place = jnp.stack([member, tp_index, layer, jnp.full_like(layer, layers), device])
    place = place.astype(jnp.int32)
    width = group * HEAD_SIZE
    bf16, f32 = jnp.bfloat16, jnp.float32

    def flipped(array, flip):
        if flip == 0:
            return array
        return lax.ppermute(array, ("y", "core"), [(i, i ^ flip) for i in range(4)])

    def climbed(array, steps):
        route = [(i, (i + steps) % layers) for i in range(layers)]
        return lax.ppermute(array, "z", route)

    every = range(members)
    table = ((rows, HEAD_SIZE), f32)
    pair = (2, rows, HEAD_SIZE)

    columns = group * block_len
    stack = (BLOCKS_DEV, columns, HEAD_SIZE)
    inputs = [position_ids, keys, values, queries]
    in_specs = [whole(a.shape) for a in inputs]
    outputs = [table, table] + [(pair, bf16)] * members
    late_rows = columns + BLOCKS_DEV * STAT_ROWS
    if members > 1:
        half = (out_grad.shape[0], members * width)
        own_half = pl.BlockSpec(half, lambda i, where: (0, where[1]))
        inputs += [out_grad, out_grad]
        in_specs += [own_half, pl.BlockSpec(half, lambda i, where: (0, 1 - where[1]))]
        outputs += [((members, BLOCKS_DEV + 1, columns, HEAD_SIZE), bf16), (half, bf16)]
    else:
        outputs.append(((members, *stack), bf16))
        late_rows += columns
    results = call(
        functools.partial(first_kernel, members, group),
        "first", [place], inputs, outputs, in_specs,
    )
    cosine, sine = results[:2]
    kv_pieces, pack = results[2 : 2 + members], results[2 + members]

    def shared(array):
        if members == 1:
            return array
        return lax.all_to_all(array, ("y", "core"), 0, 0, tiled=True)

    if members > 1:
        grads_other = lax.ppermute(results[-1], "tp", [(0, 1), (1, 0)])
        slab = jnp.stack([flipped(kv_pieces[f], f) for f in every])
        far = sorted(range(1, layers), key=lambda k: abs(2 * k - layers))
        rounds = [far[: layers // 2], far[layers // 2 :] + [0]]
        slab, grads_other = lax.optimization_barrier((slab, grads_other))
        kv = {0: slab}
        for k in far:
            kv[k] = climbed(slab, k)
    else:
        kv = {0: lax.all_gather(kv_pieces[0], ("z", "y", "core"), axis=0, tiled=False)}
        rounds = [[0]]
        grads_own = lax.all_to_all(out_grad, "tp", split_axis=1, concat_axis=0, tiled=True)
    pack = shared(pack)

    inputs = [attn_out, logsumexp]
    in_specs = [whole(a.shape) for a in inputs]
    if members > 1:
        inputs += [out_grad, grads_other]
        in_specs += [own_half, whole(grads_other.shape)]
    else:
        inputs += [grads_own]
        in_specs += [whole(grads_own.shape)]
    (late,) = call(
        functools.partial(delta_kernel, members, group),
        "delta", [place], inputs, [((members, late_rows, HEAD_SIZE), bf16)], in_specs,
    )
    late = shared(late)

    units = kv[0].shape[0]
    blocks = members * BLOCKS_DEV
    part = (units, 2, rows, HEAD_SIZE)
    sums = (blocks, HEAD_SIZE, columns)
    parts = {}
    carry = []
    for number, slabs in enumerate(rounds):
        tokens = len(slabs) * units * rows
        carries = number < len(rounds) - 1
        results = call(
            functools.partial(
                attend_kernel, members, group, block_len, slabs, number > 0, carries
            ),
            "attend", [place, block_map, span_blocks.reshape(-1)],
            [*[kv[k] for k in slabs], pack, late, *carry],
            ([(sums, f32)] if carries else [(stack, bf16)] * members)
            + [(part, f32 if k == 0 and members > 1 else bf16) for k in slabs],
            scratch=[
                pltpu.VMEM((tokens, HEAD_SIZE), bf16),
                pltpu.VMEM((tokens, HEAD_SIZE), bf16),
                pltpu.VMEM((tokens // CHUNK, HEAD_SIZE, CHUNK), bf16),
                pltpu.VMEM((blocks, columns, HEAD_SIZE), bf16),
                pltpu.VMEM((blocks, columns, HEAD_SIZE), bf16),
                pltpu.VMEM((blocks, 1, columns), f32),
                pltpu.VMEM((blocks, 1, columns), f32),
                pltpu.VMEM((tokens, HEAD_SIZE), f32),
                pltpu.VMEM((tokens, HEAD_SIZE), f32),
                pltpu.VMEM((HEAD_SIZE, columns), f32),
                pltpu.VMEM((blocks, columns, HEAD_SIZE), bf16),
                pltpu.SMEM((tokens // block_len,), jnp.int32),
                pltpu.SMEM((tokens // block_len,), jnp.int32),
            ],
            cost=pl.CostEstimate(
                flops=6 * group * members * rows * tokens * HEAD_SIZE,
                bytes_accessed=6 * 1024 * 1024,
                transcendentals=group * members * rows * tokens // 2,
            ),
        )
        outs = 1 if carries else members
        carry = results[:outs]
        parts.update(zip(slabs, results[outs:]))
        if carries:
            home = {k: climbed(parts[k], layers - k) for k in slabs}
    dq_pieces = carry
    if members > 1:
        carry, home, late = lax.optimization_barrier(
            (carry, home, {k: parts[k] for k in rounds[-1]})
        )
        dq_pieces, total = carry, late.pop(0)
        home.update({k: climbed(late[k], layers - k) for k in late})
        for k in far:
            total = total + home[k].astype(f32)
        sums = [flipped(total[f].astype(bf16), f) for f in every]
    else:
        sums = [
            lax.psum_scatter(parts[0], ("z", "y", "core"), scatter_dimension=0, tiled=True)[0]
        ]
    return tuple(
        call(
            functools.partial(last_kernel, members, group),
            "last", [place],
            [cosine, sine, *[flipped(dq_pieces[f], f) for f in every], *sums],
            [(queries.shape, bf16), (keys.shape, bf16), (values.shape, bf16)],
        )
    )


def solution(mesh):
    ctx, tp = mesh.shape["ctx"], mesh.shape["tp"]
    fine = Mesh(mesh.devices.reshape(ctx // 4, 2, 2, tp), ("z", "y", "core", "tp"))
    ctx_axes = ("z", "y", "core")
    return jax.shard_map(
        shards,
        mesh=fine,
        in_specs=(
            P(ctx_axes, "tp"),
            P(ctx_axes, "tp"),
            P(ctx_axes, "tp"),
            P(ctx_axes, "tp"),
            P((*ctx_axes, "tp"), None),
            P("tp", ctx_axes),
            P(None, ctx_axes),
            P(),
            P(),
        ),
        out_specs=(P(ctx_axes, "tp"), P(ctx_axes, "tp"), P(ctx_axes, "tp")),
        check_vma=False,
    )
```

```python
import functools
import math

import jax
import jax.numpy as jnp
from jax import lax
from jax.experimental import pallas as pl
from jax.experimental.pallas import tpu as pltpu
from jax.sharding import Mesh
from jax.sharding import PartitionSpec as P

HEAD_SIZE = 128
BLOCKS_DEV = 2
THETA = 1000000.0
CHUNK = 256
WIDE = 512
STAT_ROWS = 32
SCORE_SCALE = 1.0 / math.sqrt(HEAD_SIZE)
LOG2E = math.log2(math.e)
MEMORY = 56 * 1024 * 1024


def turned_tables(ids, width):
    half = width // 2
    rows = ids.shape[1]
    pair = lax.broadcasted_iota(jnp.int32, (half, rows), 0)
    first_cut = width // 8
    second_cut = first_cut + 3 * width // 16
    inverse = jnp.exp(pair.astype(jnp.float32) * jnp.float32(-2.0 * math.log(THETA) / width))
    ids = ids.astype(jnp.float32)
    picked = jnp.where(
        pair < first_cut, ids[0:1, :], jnp.where(pair < second_cut, ids[1:2, :], ids[2:3, :])
    )
    angles = picked * inverse
    cosine = jnp.cos(angles)
    sine = jnp.sin(angles)
    return (
        jnp.concatenate([cosine, cosine], axis=0).T,
        jnp.concatenate([sine, sine], axis=0).T,
    )


def half_sign():
    lane = lax.broadcasted_iota(jnp.int32, (1, HEAD_SIZE), 1)
    return jnp.where(lane < HEAD_SIZE // 2, -1.0, 1.0).astype(jnp.float32)


def head_lanes(member, flip, heads, head):
    first = ((member ^ flip) * heads + head) * HEAD_SIZE
    return pl.ds(pl.multiple_of(first, HEAD_SIZE), HEAD_SIZE)


def first_kernel(members, with_piece, where_ref, ids_ref, k_ref, v_ref, *refs):
    refs = list(refs)
    if with_piece:
        grad_ref = refs.pop(0)
        refs.pop()[...] = grad_ref[...]
    cos_ref, sin_ref = refs.pop(0), refs.pop(0)
    member = where_ref[0]
    cosine, sine = turned_tables(ids_ref[...], HEAD_SIZE)
    cos_ref[...] = cosine
    sin_ref[...] = sine
    signed = sine * half_sign()
    for flip in range(members):
        lanes = head_lanes(member, flip, 1, 0)
        keys = k_ref[:, lanes].astype(jnp.float32)
        refs[flip][0] = (keys * cosine + pltpu.roll(keys, HEAD_SIZE // 2, 1) * signed).astype(
            jnp.bfloat16
        )
        refs[flip][1] = v_ref[:, lanes]


def stacked(head, block_len):
    return slice(head * block_len, (head + 1) * block_len)


def query_kernel(members, group, where_ref, cos_ref, sin_ref, q_ref, *out_refs):
    member = where_ref[0]
    cosine = cos_ref[...]
    signed = sin_ref[...] * half_sign()
    block_len = q_ref.shape[0] // BLOCKS_DEV
    for flip in range(members):
        for head in range(group):
            field = q_ref[:, head_lanes(member, flip, group, head)].astype(jnp.float32)
            turned = pltpu.roll(field, HEAD_SIZE // 2, 1)
            field = (field * cosine + turned * signed).astype(jnp.bfloat16)
            for step in range(BLOCKS_DEV):
                out_refs[flip][step, stacked(head, block_len), :] = field[
                    step * block_len : (step + 1) * block_len, :
                ]


def split_rows(vector):
    pieces = []
    for _ in range(3):
        addend = vector.astype(jnp.bfloat16).astype(jnp.float32)
        vector = vector - addend
        pieces += [
            addend[:, i : i + HEAD_SIZE] for i in range(0, addend.shape[1], HEAD_SIZE)
        ]
    return pieces


def joined_row(rows):
    count = rows.shape[0] // 3
    total = rows[:count] + rows[count : 2 * count] + rows[2 * count :]
    return jnp.concatenate([total[i : i + 1] for i in range(count)], axis=1)


def block_half(members, number, where):
    if members == 1:
        return number
    return where[1] if number == 0 else 1 - where[1]


def delta_kernel(members, group, number, where_ref, a_ref, l_ref, source_ref, *grad_refs):
    member = where_ref[0]
    upper = block_half(members, number, where_ref)
    block_len = a_ref.shape[0]
    columns = group * block_len
    for flip in range(members):
        products = []
        for head in range(group):
            lanes = head_lanes(member, flip, group, head)
            grad = source_ref[:, lanes]
            grad_refs[flip][stacked(head, block_len), :] = grad
            products.append(grad.astype(jnp.float32) * a_ref[:, lanes].astype(jnp.float32))
        total = jnp.sum(jnp.concatenate(products, axis=0).T, axis=0, keepdims=True)
        first = pl.multiple_of((member ^ flip) * group, group)
        lse = l_ref[pl.ds(first, group), :] * LOG2E
        pieces = split_rows(row_vector(lse, upper, block_len)) + split_rows(total)
        pieces.append(jnp.zeros((STAT_ROWS - len(pieces), HEAD_SIZE), jnp.float32))
        grad_refs[flip][columns : columns + STAT_ROWS, :] = jnp.concatenate(
            pieces, axis=0
        ).astype(jnp.bfloat16)


def row_vector(table, upper, block_len):
    group, width = table.shape
    rolled = pltpu.roll(table, block_len, 1)
    low = jnp.where(upper == 0, table, rolled)
    high = jnp.where(upper == 0, rolled, table)
    lane = lax.broadcasted_iota(jnp.int32, (1, width), 1)
    pieces = [
        jnp.where(lane < block_len, low[h : h + 1, :], high[h + 1 : h + 2, :])
        for h in range(0, group, 2)
    ]
    return jnp.concatenate(pieces, axis=1)


def attend_kernel(
    members, group, block_len, slabs, carried, carries, where_ref, map_ref, span_ref, *refs
):
    refs = list(refs)
    count = len(slabs)
    kv_refs = [refs.pop(0) for _ in range(count)]
    q_refs = [refs.pop(0) for _ in range(members)]
    g_refs = [[refs.pop(0) for _ in range(members)] for _ in range(BLOCKS_DEV)]
    in_ref = refs.pop(0) if carried else None
    dq_refs = [refs.pop(0) for _ in range(1 if carries else members)]
    part_refs = [refs.pop(0) for _ in range(count)]
    k_sort, v_sort, k_turn, q_all, g_all, l_all, d_all, dk_sum, dv_sum, dq_sum = refs[:10]
    dq_all, ranks, ordered = refs[10:]
    member, layer, layers, device = where_ref[0], where_ref[2], where_ref[3], where_ref[4]
    units = kv_refs[0].shape[0]
    spans = span_ref.shape[0] // 2
    columns = group * block_len
    blocks = count * units * BLOCKS_DEV
    complete = blocks == map_ref.shape[0]

    def sequence_block(slab, unit, step):
        if members > 1:
            owner = lax.rem(layer - slab + layers, layers) * members + (member ^ unit)
        else:
            owner = unit
        return map_ref[owner * BLOCKS_DEV + step]

    if complete:

        @pl.loop(0, blocks)
        def _(block):
            ordered[block] = block
            ranks[block] = map_ref[block]

        def blocks_before(bound):
            return bound
    else:
        present = [
            sequence_block(slab, unit, step)
            for slab in slabs
            for unit in range(units)
            for step in range(BLOCKS_DEV)
        ]

        def blocks_before(bound):
            return functools.reduce(jnp.add, [(b < bound).astype(jnp.int32) for b in present])

        for number, block in enumerate(present):
            rank = blocks_before(block)
            ranks[number] = rank
            ordered[rank] = block

    def each_block(body):
        for place in range(count):

            @pl.loop(0, units)
            def _(unit):
                for step in range(BLOCKS_DEV):
                    rank = ranks[(place * units + unit) * BLOCKS_DEV + step]
                    at = pl.multiple_of(rank * block_len, block_len)
                    body(place, unit, pl.ds(step * block_len, block_len), pl.ds(at, block_len))

    def sort(place, unit, row, to):
        k_sort[to, :] = kv_refs[place][unit, 0, row, :]
        v_sort[to, :] = kv_refs[place][unit, 1, row, :]

    each_block(sort)

    @pl.loop(0, k_turn.shape[0])
    def _(chunk):
        at = pl.multiple_of(chunk * CHUNK, CHUNK)
        k_turn[chunk] = k_sort[pl.ds(at, CHUNK), :].T
        dk_sum[pl.ds(at, CHUNK), :] = jnp.zeros((CHUNK, HEAD_SIZE), jnp.float32)
        dv_sum[pl.ds(at, CHUNK), :] = jnp.zeros((CHUNK, HEAD_SIZE), jnp.float32)

    for flip in range(members):
        for step in range(BLOCKS_DEV):
            place = flip * BLOCKS_DEV + step
            q_all[place] = q_refs[flip][step]
            place = flip * BLOCKS_DEV + block_half(members, step, where_ref)
            g_all[place] = g_refs[step][flip][:columns, :]
            stats = g_refs[step][flip][columns:, :].astype(jnp.float32)
            half = 3 * columns // HEAD_SIZE
            l_all[place] = joined_row(stats[:half])
            d_all[place] = joined_row(stats[half : 2 * half])

    lane = lax.broadcasted_iota(jnp.int32, (1, columns), 1)
    within = lax.rem(lane, block_len)
    key_row = lax.broadcasted_iota(jnp.int32, (block_len, 1), 0)
    chunk_blocks = CHUNK // block_len

    @pl.loop(0, members * BLOCKS_DEV)
    def _(place):
        flip, step = place // BLOCKS_DEV, lax.rem(place, BLOCKS_DEV)
        owner = device if members == 1 else layer * members + (member ^ flip)
        block = map_ref[owner * BLOCKS_DEV + step]
        end = jnp.int32(0)
        for span in range(spans):
            inside = (block >= span_ref[2 * span]) & (block < span_ref[2 * span + 1])
            end = jnp.where(inside, span_ref[2 * span + 1], end)
        limit = jnp.where(end > 0, end * block_len, block * block_len + within + 1)
        full = blocks_before(jnp.where(end > 0, end, block)) // chunk_blocks
        seen = (blocks_before(jnp.maximum(end, block + 1)) + chunk_blocks - 1) // chunk_blocks
        dq_sum[...] = in_ref[place] if carried else jnp.zeros_like(dq_sum)

        def visit(chunk, size, masked):
            queries = q_all[place]
            grads = g_all[place]
            at = pl.multiple_of(chunk * CHUNK, CHUNK)
            keys = k_sort[pl.ds(at, size), :]
            values = v_sort[pl.ds(at, size), :]
            scores = lax.dot_general(
                keys, queries, (((1,), (1,)), ((), ())), preferred_element_type=jnp.float32
            )
            raised = scores * (SCORE_SCALE * LOG2E) - l_all[place]
            if masked:
                positions = jnp.concatenate(
                    [
                        key_row + ordered[chunk * chunk_blocks + i] * block_len
                        for i in range(chunk_blocks)
                    ],
                    axis=0,
                )
                raised = jnp.where(positions < limit, raised, -jnp.inf)
            probs = jnp.exp2(raised)
            grad_p = lax.dot_general(
                values, grads, (((1,), (1,)), ((), ())), preferred_element_type=jnp.float32
            )
            grad_s = (probs * (grad_p - d_all[place])).astype(jnp.bfloat16)
            dv_sum[pl.ds(at, size), :] += jnp.dot(
                probs.astype(jnp.bfloat16), grads, preferred_element_type=jnp.float32
            )
            dk_sum[pl.ds(at, size), :] += jnp.dot(
                grad_s, queries, preferred_element_type=jnp.float32
            )
            turned = [k_turn[chunk + i] for i in range(size // CHUNK)]
            dq_sum[...] += jnp.dot(
                jnp.concatenate(turned, axis=1), grad_s, preferred_element_type=jnp.float32
            )

        pairs = full // 2
        pl.loop(0, pairs)(lambda pair: visit(2 * pair, WIDE, False))
        pl.loop(2 * pairs, full)(lambda chunk: visit(chunk, CHUNK, False))
        pl.loop(full, seen)(lambda chunk: visit(chunk, CHUNK, True))

        if carries:
            dq_refs[0][place] = dq_sum[...]
        else:
            dq_all[place] = (dq_sum[...].T * SCORE_SCALE).astype(jnp.bfloat16)

    if not carries:
        for flip in range(members):
            for step in range(BLOCKS_DEV):
                dq_refs[flip][step] = dq_all[flip * BLOCKS_DEV + step]

    def unsort(place, unit, here, at):
        kind = part_refs[place].dtype
        part_refs[place][unit, 0, here, :] = (dk_sum[at, :] * SCORE_SCALE).astype(kind)
        part_refs[place][unit, 1, here, :] = dv_sum[at, :].astype(kind)

    each_block(unsort)


def turned_back(field, cosine, signed):
    return field * cosine - pltpu.roll(field, HEAD_SIZE // 2, 1) * signed


def last_kernel(members, group, where_ref, cos_ref, sin_ref, *refs):
    dq_refs, sum_refs = refs[:members], refs[members : 2 * members]
    grad_ref, dk_ref, dv_ref = refs[2 * members :]
    member = where_ref[0]
    block_len = cos_ref.shape[0] // BLOCKS_DEV
    for step in range(BLOCKS_DEV):
        here = slice(step * block_len, (step + 1) * block_len)
        cosine = cos_ref[here, :]
        signed = sin_ref[here, :] * half_sign()
        for flip in range(members):
            lanes = head_lanes(member, flip, 1, 0)
            field = sum_refs[flip][0, here, :].astype(jnp.float32)
            dk_ref[here, lanes] = turned_back(field, cosine, signed).astype(jnp.bfloat16)
            dv_ref[here, lanes] = sum_refs[flip][1, here, :].astype(jnp.bfloat16)
            for head in range(group):
                field = dq_refs[flip][step, stacked(head, block_len), :].astype(jnp.float32)
                grad_ref[here, head_lanes(member, flip, group, head)] = turned_back(
                    field, cosine, signed
                ).astype(jnp.bfloat16)


def whole(shape):
    return pl.BlockSpec(shape, lambda *_: (0,) * len(shape))


def call(kernel, name, scalars, inputs, outputs, in_specs=None, out_specs=None, scratch=(), cost=None):
    return pl.pallas_call(
        kernel,
        grid_spec=pltpu.PrefetchScalarGridSpec(
            num_scalar_prefetch=len(scalars),
            grid=(1,),
            in_specs=in_specs or [whole(a.shape) for a in inputs],
            out_specs=out_specs or [whole(shape) for shape, _ in outputs],
            scratch_shapes=list(scratch),
        ),
        out_shape=[jax.ShapeDtypeStruct(shape, kind) for shape, kind in outputs],
        compiler_params=pltpu.CompilerParams(vmem_limit_bytes=MEMORY),
        cost_estimate=cost,
        name=name,
    )(*scalars, *inputs)


def shards(
    queries, keys, values, attn_out, out_grad, logsumexp, position_ids, block_map, span_blocks
):
    rows = queries.shape[0]
    kv_heads = keys.shape[1] // HEAD_SIZE
    group = queries.shape[1] // keys.shape[1]
    block_len = rows // BLOCKS_DEV
    layers = lax.axis_size("z")
    members = 4 if kv_heads == 4 and lax.axis_size("tp") == 2 else 1
    tp_index = lax.axis_index("tp")
    layer = lax.axis_index("z")
    in_slab = lax.axis_index("y") * 2 + lax.axis_index("core")
    device = layer * 4 + in_slab
    member = in_slab if members > 1 else jnp.zeros_like(in_slab)
    place = jnp.stack([member, tp_index, layer, jnp.full_like(layer, layers), device])
    place = place.astype(jnp.int32)
    width = group * HEAD_SIZE
    bf16, f32 = jnp.bfloat16, jnp.float32

    def flipped(array, flip):
        if flip == 0:
            return array
        return lax.ppermute(array, ("y", "core"), [(i, i ^ flip) for i in range(4)])

    def climbed(array, steps):
        route = [(i, (i + steps) % layers) for i in range(layers)]
        return lax.ppermute(array, "z", route)

    every = range(members)
    table = ((rows, HEAD_SIZE), f32)
    pair = (2, rows, HEAD_SIZE)

    inputs = [position_ids, keys, values]
    outputs = [table, table] + [(pair, bf16)] * members
    in_specs = [whole(a.shape) for a in inputs]
    if members > 1:
        other = (out_grad.shape[0], members * width)
        inputs.append(out_grad)
        in_specs.append(pl.BlockSpec(other, lambda i, where: (0, 1 - where[1])))
        outputs.append((other, bf16))
    results = call(
        functools.partial(first_kernel, members, members > 1),
        "first", [place], inputs, outputs, in_specs,
    )
    cosine, sine = results[:2]
    kv_pieces = results[2 : 2 + members]
    columns = group * block_len
    stack = (BLOCKS_DEV, columns, HEAD_SIZE)
    q_pieces = call(
        functools.partial(query_kernel, members, group),
        "rotate", [place], [cosine, sine, queries], [(stack, bf16)] * members,
    )
    if members > 1:
        slab = jnp.stack([flipped(kv_pieces[f], f) for f in every])
        grads_other = lax.ppermute(results[-1], "tp", [(0, 1), (1, 0)])
        far = sorted(range(1, layers), key=lambda k: abs(2 * k - layers))
        rounds = [far[: layers // 2], far[layers // 2 :] + [0]]
        slab, *q_pieces = lax.optimization_barrier((slab, *q_pieces))
        kv = {0: slab}
        for k in far:
            kv[k] = climbed(slab, k)
    else:
        kv = {0: lax.all_gather(kv_pieces[0], ("z", "y", "core"), axis=0, tiled=False)}
        rounds = [[0]]
        grads_own = lax.all_to_all(out_grad, "tp", split_axis=1, concat_axis=0, tiled=True)
    q_in = [flipped(q_pieces[f], f) for f in every]

    g_in = []
    for number in range(BLOCKS_DEV):

        def half_rows(i, where, number=number):
            return (block_half(members, number, where), 0)

        own_rows = pl.BlockSpec((block_len, members * width), half_rows)
        if members == 1:
            source, spec = grads_own, own_rows
        elif number == 0:
            source = out_grad
            spec = pl.BlockSpec(grads_other.shape, lambda i, where: (0, where[1]))
        else:
            source, spec = grads_other, whole(grads_other.shape)
        pieces = call(
            functools.partial(delta_kernel, members, group, number),
            "delta", [place], [attn_out, logsumexp, source],
            [((columns + STAT_ROWS, HEAD_SIZE), bf16)] * members,
            [own_rows, whole(logsumexp.shape), spec],
        )
        g_in += [flipped(pieces[f], f) for f in every]

    units = kv[0].shape[0]
    blocks = members * BLOCKS_DEV
    part = (units, 2, rows, HEAD_SIZE)
    sums = (blocks, HEAD_SIZE, columns)
    parts = {}
    carry = []
    for number, slabs in enumerate(rounds):
        tokens = len(slabs) * units * rows
        carries = number < len(rounds) - 1
        results = call(
            functools.partial(
                attend_kernel, members, group, block_len, slabs, number > 0, carries
            ),
            "attend", [place, block_map, span_blocks.reshape(-1)],
            [*[kv[k] for k in slabs], *q_in, *g_in, *carry],
            ([(sums, f32)] if carries else [(stack, bf16)] * members)
            + [(part, f32 if k == 0 and members > 1 else bf16) for k in slabs],
            scratch=[
                pltpu.VMEM((tokens, HEAD_SIZE), bf16),
                pltpu.VMEM((tokens, HEAD_SIZE), bf16),
                pltpu.VMEM((tokens // CHUNK, HEAD_SIZE, CHUNK), bf16),
                pltpu.VMEM((blocks, columns, HEAD_SIZE), bf16),
                pltpu.VMEM((blocks, columns, HEAD_SIZE), bf16),
                pltpu.VMEM((blocks, 1, columns), f32),
                pltpu.VMEM((blocks, 1, columns), f32),
                pltpu.VMEM((tokens, HEAD_SIZE), f32),
                pltpu.VMEM((tokens, HEAD_SIZE), f32),
                pltpu.VMEM((HEAD_SIZE, columns), f32),
                pltpu.VMEM((blocks, columns, HEAD_SIZE), bf16),
                pltpu.SMEM((tokens // block_len,), jnp.int32),
                pltpu.SMEM((tokens // block_len,), jnp.int32),
            ],
            cost=pl.CostEstimate(
                flops=6 * group * members * rows * tokens * HEAD_SIZE,
                bytes_accessed=6 * 1024 * 1024,
                transcendentals=group * members * rows * tokens // 2,
            ),
        )
        outs = 1 if carries else members
        carry = results[:outs]
        parts.update(zip(slabs, results[outs:]))
        if carries:
            home = {k: climbed(parts[k], layers - k) for k in slabs}
    dq_pieces = carry
    if members > 1:
        carry, home, late = lax.optimization_barrier(
            (carry, home, {k: parts[k] for k in rounds[-1]})
        )
        dq_pieces, total = carry, late.pop(0)
        home.update({k: climbed(late[k], layers - k) for k in late})
        for k in far:
            total = total + home[k].astype(f32)
        sums = [flipped(total[f].astype(bf16), f) for f in every]
    else:
        sums = [
            lax.psum_scatter(parts[0], ("z", "y", "core"), scatter_dimension=0, tiled=True)[0]
        ]
    return tuple(
        call(
            functools.partial(last_kernel, members, group),
            "last", [place],
            [cosine, sine, *[flipped(dq_pieces[f], f) for f in every], *sums],
            [(queries.shape, bf16), (keys.shape, bf16), (values.shape, bf16)],
        )
    )


def solution(mesh):
    ctx, tp = mesh.shape["ctx"], mesh.shape["tp"]
    fine = Mesh(mesh.devices.reshape(ctx // 4, 2, 2, tp), ("z", "y", "core", "tp"))
    ctx_axes = ("z", "y", "core")
    return jax.shard_map(
        shards,
        mesh=fine,
        in_specs=(
            P(ctx_axes, "tp"),
            P(ctx_axes, "tp"),
            P(ctx_axes, "tp"),
            P(ctx_axes, "tp"),
            P((*ctx_axes, "tp"), None),
            P("tp", ctx_axes),
            P(None, ctx_axes),
            P(),
            P(),
        ),
        out_specs=(P(ctx_axes, "tp"), P(ctx_axes, "tp"), P(ctx_axes, "tp")),
        check_vma=False,
    )
```

```python
import functools
import math

import jax
import jax.numpy as jnp
from jax import lax
from jax.experimental import pallas as pl
from jax.experimental.pallas import tpu as pltpu
from jax.sharding import Mesh
from jax.sharding import PartitionSpec as P

HEAD_SIZE = 128
BLOCKS_DEV = 2
THETA = 1000000.0
CHUNK = 256
WIDE = 512
STAT_ROWS = 32
SCORE_SCALE = 1.0 / math.sqrt(HEAD_SIZE)
LOG2E = math.log2(math.e)
MEMORY = 56 * 1024 * 1024


def turned_tables(ids, width):
    half = width // 2
    rows = ids.shape[1]
    pair = lax.broadcasted_iota(jnp.int32, (half, rows), 0)
    first_cut = width // 8
    second_cut = first_cut + 3 * width // 16
    inverse = jnp.exp(pair.astype(jnp.float32) * jnp.float32(-2.0 * math.log(THETA) / width))
    ids = ids.astype(jnp.float32)
    picked = jnp.where(
        pair < first_cut, ids[0:1, :], jnp.where(pair < second_cut, ids[1:2, :], ids[2:3, :])
    )
    angles = picked * inverse
    cosine = jnp.cos(angles)
    sine = jnp.sin(angles)
    return (
        jnp.concatenate([cosine, cosine], axis=0).T,
        jnp.concatenate([sine, sine], axis=0).T,
    )


def half_sign():
    lane = lax.broadcasted_iota(jnp.int32, (1, HEAD_SIZE), 1)
    return jnp.where(lane < HEAD_SIZE // 2, -1.0, 1.0).astype(jnp.float32)


def head_lanes(member, flip, heads, head):
    first = ((member ^ flip) * heads + head) * HEAD_SIZE
    return pl.ds(pl.multiple_of(first, HEAD_SIZE), HEAD_SIZE)


def first_kernel(members, with_piece, where_ref, ids_ref, k_ref, v_ref, *refs):
    refs = list(refs)
    if with_piece:
        grad_ref = refs.pop(0)
        refs.pop()[...] = grad_ref[...]
    cos_ref, sin_ref = refs.pop(0), refs.pop(0)
    member = where_ref[0]
    cosine, sine = turned_tables(ids_ref[...], HEAD_SIZE)
    cos_ref[...] = cosine
    sin_ref[...] = sine
    signed = sine * half_sign()
    for flip in range(members):
        lanes = head_lanes(member, flip, 1, 0)
        keys = k_ref[:, lanes].astype(jnp.float32)
        refs[flip][0] = (keys * cosine + pltpu.roll(keys, HEAD_SIZE // 2, 1) * signed).astype(
            jnp.bfloat16
        )
        refs[flip][1] = v_ref[:, lanes]


def stacked(head, block_len):
    return slice(head * block_len, (head + 1) * block_len)


def query_kernel(members, group, where_ref, cos_ref, sin_ref, q_ref, *out_refs):
    member = where_ref[0]
    cosine = cos_ref[...]
    signed = sin_ref[...] * half_sign()
    block_len = q_ref.shape[0] // BLOCKS_DEV
    for flip in range(members):
        for head in range(group):
            field = q_ref[:, head_lanes(member, flip, group, head)].astype(jnp.float32)
            turned = pltpu.roll(field, HEAD_SIZE // 2, 1)
            field = (field * cosine + turned * signed).astype(jnp.bfloat16)
            for step in range(BLOCKS_DEV):
                out_refs[flip][step, stacked(head, block_len), :] = field[
                    step * block_len : (step + 1) * block_len, :
                ]


def split_rows(vector):
    pieces = []
    for _ in range(3):
        addend = vector.astype(jnp.bfloat16).astype(jnp.float32)
        vector = vector - addend
        pieces += [
            addend[:, i : i + HEAD_SIZE] for i in range(0, addend.shape[1], HEAD_SIZE)
        ]
    return pieces


def joined_row(rows):
    count = rows.shape[0] // 3
    total = rows[:count] + rows[count : 2 * count] + rows[2 * count :]
    return jnp.concatenate([total[i : i + 1] for i in range(count)], axis=1)


def block_half(members, number, where):
    if members == 1:
        return number
    return where[1] if number == 0 else 1 - where[1]


def delta_kernel(members, group, number, where_ref, a_ref, l_ref, source_ref, *grad_refs):
    member = where_ref[0]
    upper = block_half(members, number, where_ref)
    block_len = a_ref.shape[0]
    columns = group * block_len
    for flip in range(members):
        products = []
        for head in range(group):
            lanes = head_lanes(member, flip, group, head)
            grad = source_ref[:, lanes]
            grad_refs[flip][stacked(head, block_len), :] = grad
            products.append(grad.astype(jnp.float32) * a_ref[:, lanes].astype(jnp.float32))
        total = jnp.sum(jnp.concatenate(products, axis=0).T, axis=0, keepdims=True)
        first = pl.multiple_of((member ^ flip) * group, group)
        lse = l_ref[pl.ds(first, group), :] * LOG2E
        pieces = split_rows(row_vector(lse, upper, block_len)) + split_rows(total)
        pieces.append(jnp.zeros((STAT_ROWS - len(pieces), HEAD_SIZE), jnp.float32))
        grad_refs[flip][columns : columns + STAT_ROWS, :] = jnp.concatenate(
            pieces, axis=0
        ).astype(jnp.bfloat16)


def row_vector(table, upper, block_len):
    group, width = table.shape
    rolled = pltpu.roll(table, block_len, 1)
    low = jnp.where(upper == 0, table, rolled)
    high = jnp.where(upper == 0, rolled, table)
    lane = lax.broadcasted_iota(jnp.int32, (1, width), 1)
    pieces = [
        jnp.where(lane < block_len, low[h : h + 1, :], high[h + 1 : h + 2, :])
        for h in range(0, group, 2)
    ]
    return jnp.concatenate(pieces, axis=1)


def attend_kernel(
    members, group, block_len, slabs, carried, carries, where_ref, map_ref, span_ref, *refs
):
    refs = list(refs)
    count = len(slabs)
    kv_refs = [refs.pop(0) for _ in range(count)]
    q_refs = [refs.pop(0) for _ in range(members)]
    g_refs = [[refs.pop(0) for _ in range(members)] for _ in range(BLOCKS_DEV)]
    in_ref = refs.pop(0) if carried else None
    dq_refs = [refs.pop(0) for _ in range(1 if carries else members)]
    part_refs = [refs.pop(0) for _ in range(count)]
    k_sort, v_sort, k_turn, q_all, g_all, l_all, d_all, dk_sum, dv_sum, dq_sum = refs[:10]
    dq_all, ranks, ordered = refs[10:]
    member, layer, layers, device = where_ref[0], where_ref[2], where_ref[3], where_ref[4]
    units = kv_refs[0].shape[0]
    spans = span_ref.shape[0] // 2
    columns = group * block_len
    blocks = count * units * BLOCKS_DEV
    complete = blocks == map_ref.shape[0]

    def sequence_block(slab, unit, step):
        if members > 1:
            owner = lax.rem(layer - slab + layers, layers) * members + (member ^ unit)
        else:
            owner = unit
        return map_ref[owner * BLOCKS_DEV + step]

    if complete:

        @pl.loop(0, blocks)
        def _(block):
            ordered[block] = block
            ranks[block] = map_ref[block]

        def blocks_before(bound):
            return bound
    else:
        present = [
            sequence_block(slab, unit, step)
            for slab in slabs
            for unit in range(units)
            for step in range(BLOCKS_DEV)
        ]

        def blocks_before(bound):
            return functools.reduce(jnp.add, [(b < bound).astype(jnp.int32) for b in present])

        for number, block in enumerate(present):
            rank = blocks_before(block)
            ranks[number] = rank
            ordered[rank] = block

    def each_block(body):
        for place in range(count):

            @pl.loop(0, units)
            def _(unit):
                for step in range(BLOCKS_DEV):
                    rank = ranks[(place * units + unit) * BLOCKS_DEV + step]
                    at = pl.multiple_of(rank * block_len, block_len)
                    body(place, unit, pl.ds(step * block_len, block_len), pl.ds(at, block_len))

    def sort(place, unit, row, to):
        k_sort[to, :] = kv_refs[place][unit, 0, row, :]
        v_sort[to, :] = kv_refs[place][unit, 1, row, :]

    each_block(sort)

    @pl.loop(0, k_turn.shape[0])
    def _(chunk):
        at = pl.multiple_of(chunk * CHUNK, CHUNK)
        k_turn[chunk] = k_sort[pl.ds(at, CHUNK), :].T
        dk_sum[pl.ds(at, CHUNK), :] = jnp.zeros((CHUNK, HEAD_SIZE), jnp.float32)
        dv_sum[pl.ds(at, CHUNK), :] = jnp.zeros((CHUNK, HEAD_SIZE), jnp.float32)

    for flip in range(members):
        for step in range(BLOCKS_DEV):
            place = flip * BLOCKS_DEV + step
            q_all[place] = q_refs[flip][step]
            place = flip * BLOCKS_DEV + block_half(members, step, where_ref)
            g_all[place] = g_refs[step][flip][:columns, :]
            stats = g_refs[step][flip][columns:, :].astype(jnp.float32)
            half = 3 * columns // HEAD_SIZE
            l_all[place] = joined_row(stats[:half])
            d_all[place] = joined_row(stats[half : 2 * half])

    lane = lax.broadcasted_iota(jnp.int32, (1, columns), 1)
    within = lax.rem(lane, block_len)
    key_row = lax.broadcasted_iota(jnp.int32, (block_len, 1), 0)
    chunk_blocks = CHUNK // block_len

    @pl.loop(0, members * BLOCKS_DEV)
    def _(place):
        flip, step = place // BLOCKS_DEV, lax.rem(place, BLOCKS_DEV)
        owner = device if members == 1 else layer * members + (member ^ flip)
        block = map_ref[owner * BLOCKS_DEV + step]
        end = jnp.int32(0)
        for span in range(spans):
            inside = (block >= span_ref[2 * span]) & (block < span_ref[2 * span + 1])
            end = jnp.where(inside, span_ref[2 * span + 1], end)
        limit = jnp.where(end > 0, end * block_len, block * block_len + within + 1)
        full = blocks_before(jnp.where(end > 0, end, block)) // chunk_blocks
        seen = (blocks_before(jnp.maximum(end, block + 1)) + chunk_blocks - 1) // chunk_blocks
        dq_sum[...] = in_ref[place] if carried else jnp.zeros_like(dq_sum)

        def visit(chunk, size, masked):
            queries = q_all[place]
            grads = g_all[place]
            at = pl.multiple_of(chunk * CHUNK, CHUNK)
            keys = k_sort[pl.ds(at, size), :]
            values = v_sort[pl.ds(at, size), :]
            scores = lax.dot_general(
                keys, queries, (((1,), (1,)), ((), ())), preferred_element_type=jnp.float32
            )
            raised = scores * (SCORE_SCALE * LOG2E) - l_all[place]
            if masked:
                positions = jnp.concatenate(
                    [
                        key_row + ordered[chunk * chunk_blocks + i] * block_len
                        for i in range(chunk_blocks)
                    ],
                    axis=0,
                )
                raised = jnp.where(positions < limit, raised, -jnp.inf)
            probs = jnp.exp2(raised)
            grad_p = lax.dot_general(
                values, grads, (((1,), (1,)), ((), ())), preferred_element_type=jnp.float32
            )
            grad_s = (probs * (grad_p - d_all[place])).astype(jnp.bfloat16)
            dv_sum[pl.ds(at, size), :] += jnp.dot(
                probs.astype(jnp.bfloat16), grads, preferred_element_type=jnp.float32
            )
            dk_sum[pl.ds(at, size), :] += jnp.dot(
                grad_s, queries, preferred_element_type=jnp.float32
            )
            turned = [k_turn[chunk + i] for i in range(size // CHUNK)]
            dq_sum[...] += jnp.dot(
                jnp.concatenate(turned, axis=1), grad_s, preferred_element_type=jnp.float32
            )

        pairs = full // 2
        pl.loop(0, pairs)(lambda pair: visit(2 * pair, WIDE, False))
        pl.loop(2 * pairs, full)(lambda chunk: visit(chunk, CHUNK, False))
        pl.loop(full, seen)(lambda chunk: visit(chunk, CHUNK, True))

        if carries:
            dq_refs[0][place] = dq_sum[...]
        else:
            dq_all[place] = (dq_sum[...].T * SCORE_SCALE).astype(jnp.bfloat16)

    if not carries:
        for flip in range(members):
            for step in range(BLOCKS_DEV):
                dq_refs[flip][step] = dq_all[flip * BLOCKS_DEV + step]

    def unsort(place, unit, here, at):
        kind = part_refs[place].dtype
        part_refs[place][unit, 0, here, :] = (dk_sum[at, :] * SCORE_SCALE).astype(kind)
        part_refs[place][unit, 1, here, :] = dv_sum[at, :].astype(kind)

    each_block(unsort)


def turned_back(field, cosine, signed):
    return field * cosine - pltpu.roll(field, HEAD_SIZE // 2, 1) * signed


def last_kernel(members, group, where_ref, cos_ref, sin_ref, *refs):
    dq_refs, sum_refs = refs[:members], refs[members : 2 * members]
    grad_ref, dk_ref, dv_ref = refs[2 * members :]
    member = where_ref[0]
    block_len = cos_ref.shape[0] // BLOCKS_DEV
    for step in range(BLOCKS_DEV):
        here = slice(step * block_len, (step + 1) * block_len)
        cosine = cos_ref[here, :]
        signed = sin_ref[here, :] * half_sign()
        for flip in range(members):
            lanes = head_lanes(member, flip, 1, 0)
            field = sum_refs[flip][0, here, :].astype(jnp.float32)
            dk_ref[here, lanes] = turned_back(field, cosine, signed).astype(jnp.bfloat16)
            dv_ref[here, lanes] = sum_refs[flip][1, here, :].astype(jnp.bfloat16)
            for head in range(group):
                field = dq_refs[flip][step, stacked(head, block_len), :].astype(jnp.float32)
                grad_ref[here, head_lanes(member, flip, group, head)] = turned_back(
                    field, cosine, signed
                ).astype(jnp.bfloat16)


def whole(shape):
    return pl.BlockSpec(shape, lambda *_: (0,) * len(shape))


def call(kernel, name, scalars, inputs, outputs, in_specs=None, out_specs=None, scratch=(), cost=None):
    return pl.pallas_call(
        kernel,
        grid_spec=pltpu.PrefetchScalarGridSpec(
            num_scalar_prefetch=len(scalars),
            grid=(1,),
            in_specs=in_specs or [whole(a.shape) for a in inputs],
            out_specs=out_specs or [whole(shape) for shape, _ in outputs],
            scratch_shapes=list(scratch),
        ),
        out_shape=[jax.ShapeDtypeStruct(shape, kind) for shape, kind in outputs],
        compiler_params=pltpu.CompilerParams(vmem_limit_bytes=MEMORY),
        cost_estimate=cost,
        name=name,
    )(*scalars, *inputs)


def shards(
    queries, keys, values, attn_out, out_grad, logsumexp, position_ids, block_map, span_blocks
):
    rows = queries.shape[0]
    kv_heads = keys.shape[1] // HEAD_SIZE
    group = queries.shape[1] // keys.shape[1]
    block_len = rows // BLOCKS_DEV
    layers = lax.axis_size("z")
    members = 4 if kv_heads == 4 and lax.axis_size("tp") == 2 else 1
    tp_index = lax.axis_index("tp")
    layer = lax.axis_index("z")
    in_slab = lax.axis_index("y") * 2 + lax.axis_index("core")
    device = layer * 4 + in_slab
    member = in_slab if members > 1 else jnp.zeros_like(in_slab)
    place = jnp.stack([member, tp_index, layer, jnp.full_like(layer, layers), device])
    place = place.astype(jnp.int32)
    width = group * HEAD_SIZE
    bf16, f32 = jnp.bfloat16, jnp.float32

    def flipped(array, flip):
        if flip == 0:
            return array
        return lax.ppermute(array, ("y", "core"), [(i, i ^ flip) for i in range(4)])

    def climbed(array, steps):
        route = [(i, (i + steps) % layers) for i in range(layers)]
        return lax.ppermute(array, "z", route)

    every = range(members)
    table = ((rows, HEAD_SIZE), f32)
    pair = (2, rows, HEAD_SIZE)

    inputs = [position_ids, keys, values]
    outputs = [table, table] + [(pair, bf16)] * members
    in_specs = [whole(a.shape) for a in inputs]
    if members > 1:
        other = (out_grad.shape[0], members * width)
        inputs.append(out_grad)
        in_specs.append(pl.BlockSpec(other, lambda i, where: (0, 1 - where[1])))
        outputs.append((other, bf16))
    results = call(
        functools.partial(first_kernel, members, members > 1),
        "first", [place], inputs, outputs, in_specs,
    )
    cosine, sine = results[:2]
    kv_pieces = results[2 : 2 + members]
    columns = group * block_len
    stack = (BLOCKS_DEV, columns, HEAD_SIZE)
    cosine_now = cosine
    if members > 1:
        slab = jnp.stack([flipped(kv_pieces[f], f) for f in every])
        grads_other = lax.ppermute(results[-1], "tp", [(0, 1), (1, 0)])
        far = sorted(range(1, layers), key=lambda k: abs(2 * k - layers))
        rounds = [far[: layers // 2], far[layers // 2 :] + [0]]
        slab, cosine_now = lax.optimization_barrier((slab, cosine))
        kv = {0: slab}
        for k in far:
            kv[k] = climbed(slab, k)
        kv[far[0]], grads_other = lax.optimization_barrier((kv[far[0]], grads_other))
    else:
        kv = {0: lax.all_gather(kv_pieces[0], ("z", "y", "core"), axis=0, tiled=False)}
        rounds = [[0]]
        grads_own = lax.all_to_all(out_grad, "tp", split_axis=1, concat_axis=0, tiled=True)
    q_pieces = call(
        functools.partial(query_kernel, members, group),
        "rotate", [place], [cosine_now, sine, queries], [(stack, bf16)] * members,
    )
    q_in = [flipped(q_pieces[f], f) for f in every]

    g_in = []
    for number in range(BLOCKS_DEV):

        def half_rows(i, where, number=number):
            return (block_half(members, number, where), 0)

        own_rows = pl.BlockSpec((block_len, members * width), half_rows)
        if members == 1:
            source, spec = grads_own, own_rows
        elif number == 0:
            source = out_grad
            spec = pl.BlockSpec(grads_other.shape, lambda i, where: (0, where[1]))
        else:
            source, spec = grads_other, whole(grads_other.shape)
        pieces = call(
            functools.partial(delta_kernel, members, group, number),
            "delta", [place], [attn_out, logsumexp, source],
            [((columns + STAT_ROWS, HEAD_SIZE), bf16)] * members,
            [own_rows, whole(logsumexp.shape), spec],
        )
        g_in += [flipped(pieces[f], f) for f in every]

    units = kv[0].shape[0]
    blocks = members * BLOCKS_DEV
    part = (units, 2, rows, HEAD_SIZE)
    sums = (blocks, HEAD_SIZE, columns)
    parts = {}
    carry = []
    for number, slabs in enumerate(rounds):
        tokens = len(slabs) * units * rows
        carries = number < len(rounds) - 1
        results = call(
            functools.partial(
                attend_kernel, members, group, block_len, slabs, number > 0, carries
            ),
            "attend", [place, block_map, span_blocks.reshape(-1)],
            [*[kv[k] for k in slabs], *q_in, *g_in, *carry],
            ([(sums, f32)] if carries else [(stack, bf16)] * members)
            + [(part, f32 if k == 0 and members > 1 else bf16) for k in slabs],
            scratch=[
                pltpu.VMEM((tokens, HEAD_SIZE), bf16),
                pltpu.VMEM((tokens, HEAD_SIZE), bf16),
                pltpu.VMEM((tokens // CHUNK, HEAD_SIZE, CHUNK), bf16),
                pltpu.VMEM((blocks, columns, HEAD_SIZE), bf16),
                pltpu.VMEM((blocks, columns, HEAD_SIZE), bf16),
                pltpu.VMEM((blocks, 1, columns), f32),
                pltpu.VMEM((blocks, 1, columns), f32),
                pltpu.VMEM((tokens, HEAD_SIZE), f32),
                pltpu.VMEM((tokens, HEAD_SIZE), f32),
                pltpu.VMEM((HEAD_SIZE, columns), f32),
                pltpu.VMEM((blocks, columns, HEAD_SIZE), bf16),
                pltpu.SMEM((tokens // block_len,), jnp.int32),
                pltpu.SMEM((tokens // block_len,), jnp.int32),
            ],
            cost=pl.CostEstimate(
                flops=6 * group * members * rows * tokens * HEAD_SIZE,
                bytes_accessed=6 * 1024 * 1024,
                transcendentals=group * members * rows * tokens // 2,
            ),
        )
        outs = 1 if carries else members
        carry = results[:outs]
        parts.update(zip(slabs, results[outs:]))
        if carries:
            home = {k: climbed(parts[k], layers - k) for k in slabs}
    dq_pieces = carry
    if members > 1:
        carry, home, late = lax.optimization_barrier(
            (carry, home, {k: parts[k] for k in rounds[-1]})
        )
        dq_pieces, total = carry, late.pop(0)
        home.update({k: climbed(late[k], layers - k) for k in late})
        for k in far:
            total = total + home[k].astype(f32)
        sums = [flipped(total[f].astype(bf16), f) for f in every]
    else:
        sums = [
            lax.psum_scatter(parts[0], ("z", "y", "core"), scatter_dimension=0, tiled=True)[0]
        ]
    return tuple(
        call(
            functools.partial(last_kernel, members, group),
            "last", [place],
            [cosine, sine, *[flipped(dq_pieces[f], f) for f in every], *sums],
            [(queries.shape, bf16), (keys.shape, bf16), (values.shape, bf16)],
        )
    )


def solution(mesh):
    ctx, tp = mesh.shape["ctx"], mesh.shape["tp"]
    fine = Mesh(mesh.devices.reshape(ctx // 4, 2, 2, tp), ("z", "y", "core", "tp"))
    ctx_axes = ("z", "y", "core")
    return jax.shard_map(
        shards,
        mesh=fine,
        in_specs=(
            P(ctx_axes, "tp"),
            P(ctx_axes, "tp"),
            P(ctx_axes, "tp"),
            P(ctx_axes, "tp"),
            P((*ctx_axes, "tp"), None),
            P("tp", ctx_axes),
            P(None, ctx_axes),
            P(),
            P(),
        ),
        out_specs=(P(ctx_axes, "tp"), P(ctx_axes, "tp"), P(ctx_axes, "tp")),
        check_vma=False,
    )
```

```python
import functools
import math

import jax
import jax.numpy as jnp
from jax import lax
from jax.experimental import pallas as pl
from jax.experimental.pallas import tpu as pltpu
from jax.sharding import Mesh
from jax.sharding import PartitionSpec as P

HEAD_SIZE = 128
BLOCKS_DEV = 2
THETA = 1000000.0
CHUNK = 256
WIDE = 512
STAT_ROWS = 32
SCORE_SCALE = 1.0 / math.sqrt(HEAD_SIZE)
LOG2E = math.log2(math.e)
MEMORY = 56 * 1024 * 1024


def turned_tables(ids, width):
    half = width // 2
    rows = ids.shape[1]
    pair = lax.broadcasted_iota(jnp.int32, (half, rows), 0)
    first_cut = width // 8
    second_cut = first_cut + 3 * width // 16
    inverse = jnp.exp(pair.astype(jnp.float32) * jnp.float32(-2.0 * math.log(THETA) / width))
    ids = ids.astype(jnp.float32)
    picked = jnp.where(
        pair < first_cut, ids[0:1, :], jnp.where(pair < second_cut, ids[1:2, :], ids[2:3, :])
    )
    angles = picked * inverse
    cosine = jnp.cos(angles)
    sine = jnp.sin(angles)
    return (
        jnp.concatenate([cosine, cosine], axis=0).T,
        jnp.concatenate([sine, sine], axis=0).T,
    )


def half_sign():
    lane = lax.broadcasted_iota(jnp.int32, (1, HEAD_SIZE), 1)
    return jnp.where(lane < HEAD_SIZE // 2, -1.0, 1.0).astype(jnp.float32)


def head_lanes(member, flip, heads, head):
    first = ((member ^ flip) * heads + head) * HEAD_SIZE
    return pl.ds(pl.multiple_of(first, HEAD_SIZE), HEAD_SIZE)


def first_kernel(members, with_piece, where_ref, ids_ref, k_ref, v_ref, *refs):
    refs = list(refs)
    if with_piece:
        grad_ref = refs.pop(0)
        refs.pop()[...] = grad_ref[...]
    cos_ref, sin_ref = refs.pop(0), refs.pop(0)
    member = where_ref[0]
    cosine, sine = turned_tables(ids_ref[...], HEAD_SIZE)
    cos_ref[...] = cosine
    sin_ref[...] = sine
    signed = sine * half_sign()
    for flip in range(members):
        lanes = head_lanes(member, flip, 1, 0)
        keys = k_ref[:, lanes].astype(jnp.float32)
        refs[flip][0] = (keys * cosine + pltpu.roll(keys, HEAD_SIZE // 2, 1) * signed).astype(
            jnp.bfloat16
        )
        refs[flip][1] = v_ref[:, lanes]


def stacked(head, block_len):
    return slice(head * block_len, (head + 1) * block_len)


def query_kernel(members, group, where_ref, cos_ref, sin_ref, q_ref, *out_refs):
    member = where_ref[0]
    cosine = cos_ref[...]
    signed = sin_ref[...] * half_sign()
    block_len = q_ref.shape[0] // BLOCKS_DEV
    for flip in range(members):
        for head in range(group):
            field = q_ref[:, head_lanes(member, flip, group, head)].astype(jnp.float32)
            turned = pltpu.roll(field, HEAD_SIZE // 2, 1)
            field = (field * cosine + turned * signed).astype(jnp.bfloat16)
            for step in range(BLOCKS_DEV):
                out_refs[flip][step, stacked(head, block_len), :] = field[
                    step * block_len : (step + 1) * block_len, :
                ]


def split_rows(vector):
    pieces = []
    for _ in range(3):
        addend = vector.astype(jnp.bfloat16).astype(jnp.float32)
        vector = vector - addend
        pieces += [
            addend[:, i : i + HEAD_SIZE] for i in range(0, addend.shape[1], HEAD_SIZE)
        ]
    return pieces


def joined_row(rows):
    count = rows.shape[0] // 3
    total = rows[:count] + rows[count : 2 * count] + rows[2 * count :]
    return jnp.concatenate([total[i : i + 1] for i in range(count)], axis=1)


def block_half(members, number, where):
    if members == 1:
        return number
    return where[1] if number == 0 else 1 - where[1]


def delta_kernel(members, group, number, where_ref, a_ref, l_ref, source_ref, *grad_refs):
    member = where_ref[0]
    upper = block_half(members, number, where_ref)
    block_len = a_ref.shape[0]
    columns = group * block_len
    for flip in range(members):
        products = []
        for head in range(group):
            lanes = head_lanes(member, flip, group, head)
            grad = source_ref[:, lanes]
            grad_refs[flip][stacked(head, block_len), :] = grad
            products.append(grad.astype(jnp.float32) * a_ref[:, lanes].astype(jnp.float32))
        total = jnp.sum(jnp.concatenate(products, axis=0).T, axis=0, keepdims=True)
        first = pl.multiple_of((member ^ flip) * group, group)
        lse = l_ref[pl.ds(first, group), :] * LOG2E
        pieces = split_rows(row_vector(lse, upper, block_len)) + split_rows(total)
        pieces.append(jnp.zeros((STAT_ROWS - len(pieces), HEAD_SIZE), jnp.float32))
        grad_refs[flip][columns : columns + STAT_ROWS, :] = jnp.concatenate(
            pieces, axis=0
        ).astype(jnp.bfloat16)


def row_vector(table, upper, block_len):
    group, width = table.shape
    rolled = pltpu.roll(table, block_len, 1)
    low = jnp.where(upper == 0, table, rolled)
    high = jnp.where(upper == 0, rolled, table)
    lane = lax.broadcasted_iota(jnp.int32, (1, width), 1)
    pieces = [
        jnp.where(lane < block_len, low[h : h + 1, :], high[h + 1 : h + 2, :])
        for h in range(0, group, 2)
    ]
    return jnp.concatenate(pieces, axis=1)


def attend_kernel(
    members, group, block_len, slabs, carried, carries, where_ref, map_ref, span_ref, *refs
):
    refs = list(refs)
    count = len(slabs)
    kv_refs = [refs.pop(0) for _ in range(count)]
    q_refs = [refs.pop(0) for _ in range(members)]
    g_refs = [[refs.pop(0) for _ in range(members)] for _ in range(BLOCKS_DEV)]
    in_ref = refs.pop(0) if carried else None
    dq_refs = [refs.pop(0) for _ in range(1 if carries else members)]
    part_refs = [refs.pop(0) for _ in range(count)]
    k_sort, v_sort, k_turn, q_all, g_all, l_all, d_all, dk_sum, dv_sum, dq_sum = refs[:10]
    dq_all, ranks, ordered = refs[10:]
    member, layer, layers, device = where_ref[0], where_ref[2], where_ref[3], where_ref[4]
    units = kv_refs[0].shape[0]
    spans = span_ref.shape[0] // 2
    columns = group * block_len
    blocks = count * units * BLOCKS_DEV
    complete = blocks == map_ref.shape[0]

    def sequence_block(slab, unit, step):
        if members > 1:
            owner = lax.rem(layer - slab + layers, layers) * members + (member ^ unit)
        else:
            owner = unit
        return map_ref[owner * BLOCKS_DEV + step]

    if complete:

        @pl.loop(0, blocks)
        def _(block):
            ordered[block] = block
            ranks[block] = map_ref[block]

        def blocks_before(bound):
            return bound
    else:
        present = [
            sequence_block(slab, unit, step)
            for slab in slabs
            for unit in range(units)
            for step in range(BLOCKS_DEV)
        ]

        def blocks_before(bound):
            return functools.reduce(jnp.add, [(b < bound).astype(jnp.int32) for b in present])

        for number, block in enumerate(present):
            rank = blocks_before(block)
            ranks[number] = rank
            ordered[rank] = block

    def each_block(body):
        for place in range(count):

            @pl.loop(0, units)
            def _(unit):
                for step in range(BLOCKS_DEV):
                    rank = ranks[(place * units + unit) * BLOCKS_DEV + step]
                    at = pl.multiple_of(rank * block_len, block_len)
                    body(place, unit, pl.ds(step * block_len, block_len), pl.ds(at, block_len))

    def sort(place, unit, row, to):
        k_sort[to, :] = kv_refs[place][unit, 0, row, :]
        v_sort[to, :] = kv_refs[place][unit, 1, row, :]

    each_block(sort)

    @pl.loop(0, k_turn.shape[0])
    def _(chunk):
        at = pl.multiple_of(chunk * CHUNK, CHUNK)
        k_turn[chunk] = k_sort[pl.ds(at, CHUNK), :].T
        dk_sum[pl.ds(at, CHUNK), :] = jnp.zeros((CHUNK, HEAD_SIZE), jnp.float32)
        dv_sum[pl.ds(at, CHUNK), :] = jnp.zeros((CHUNK, HEAD_SIZE), jnp.float32)

    for flip in range(members):
        for step in range(BLOCKS_DEV):
            place = flip * BLOCKS_DEV + step
            q_all[place] = q_refs[flip][step]
            place = flip * BLOCKS_DEV + block_half(members, step, where_ref)
            g_all[place] = g_refs[step][flip][:columns, :]
            stats = g_refs[step][flip][columns:, :].astype(jnp.float32)
            half = 3 * columns // HEAD_SIZE
            l_all[place] = joined_row(stats[:half])
            d_all[place] = joined_row(stats[half : 2 * half])

    lane = lax.broadcasted_iota(jnp.int32, (1, columns), 1)
    within = lax.rem(lane, block_len)
    key_row = lax.broadcasted_iota(jnp.int32, (block_len, 1), 0)
    chunk_blocks = CHUNK // block_len

    @pl.loop(0, members * BLOCKS_DEV)
    def _(place):
        flip, step = place // BLOCKS_DEV, lax.rem(place, BLOCKS_DEV)
        owner = device if members == 1 else layer * members + (member ^ flip)
        block = map_ref[owner * BLOCKS_DEV + step]
        end = jnp.int32(0)
        for span in range(spans):
            inside = (block >= span_ref[2 * span]) & (block < span_ref[2 * span + 1])
            end = jnp.where(inside, span_ref[2 * span + 1], end)
        limit = jnp.where(end > 0, end * block_len, block * block_len + within + 1)
        full = blocks_before(jnp.where(end > 0, end, block)) // chunk_blocks
        seen = (blocks_before(jnp.maximum(end, block + 1)) + chunk_blocks - 1) // chunk_blocks
        dq_sum[...] = in_ref[place] if carried else jnp.zeros_like(dq_sum)

        def visit(chunk, size, masked):
            queries = q_all[place]
            grads = g_all[place]
            at = pl.multiple_of(chunk * CHUNK, CHUNK)
            keys = k_sort[pl.ds(at, size), :]
            values = v_sort[pl.ds(at, size), :]
            scores = lax.dot_general(
                keys, queries, (((1,), (1,)), ((), ())), preferred_element_type=jnp.float32
            )
            raised = scores * (SCORE_SCALE * LOG2E) - l_all[place]
            if masked:
                positions = jnp.concatenate(
                    [
                        key_row + ordered[chunk * chunk_blocks + i] * block_len
                        for i in range(chunk_blocks)
                    ],
                    axis=0,
                )
                raised = jnp.where(positions < limit, raised, -jnp.inf)
            probs = jnp.exp2(raised)
            grad_p = lax.dot_general(
                values, grads, (((1,), (1,)), ((), ())), preferred_element_type=jnp.float32
            )
            grad_s = (probs * (grad_p - d_all[place])).astype(jnp.bfloat16)
            dv_sum[pl.ds(at, size), :] += jnp.dot(
                probs.astype(jnp.bfloat16), grads, preferred_element_type=jnp.float32
            )
            dk_sum[pl.ds(at, size), :] += jnp.dot(
                grad_s, queries, preferred_element_type=jnp.float32
            )
            turned = [k_turn[chunk + i] for i in range(size // CHUNK)]
            dq_sum[...] += jnp.dot(
                jnp.concatenate(turned, axis=1), grad_s, preferred_element_type=jnp.float32
            )

        pairs = full // 2
        pl.loop(0, pairs)(lambda pair: visit(2 * pair, WIDE, False))
        pl.loop(2 * pairs, full)(lambda chunk: visit(chunk, CHUNK, False))
        pl.loop(full, seen)(lambda chunk: visit(chunk, CHUNK, True))

        if carries:
            dq_refs[0][place] = dq_sum[...]
        else:
            dq_all[place] = (dq_sum[...].T * SCORE_SCALE).astype(jnp.bfloat16)

    if not carries:
        for flip in range(members):
            for step in range(BLOCKS_DEV):
                dq_refs[flip][step] = dq_all[flip * BLOCKS_DEV + step]

    def unsort(place, unit, here, at):
        kind = part_refs[place].dtype
        part_refs[place][unit, 0, here, :] = (dk_sum[at, :] * SCORE_SCALE).astype(kind)
        part_refs[place][unit, 1, here, :] = dv_sum[at, :].astype(kind)

    each_block(unsort)


def turned_back(field, cosine, signed):
    return field * cosine - pltpu.roll(field, HEAD_SIZE // 2, 1) * signed


def last_kernel(members, group, where_ref, cos_ref, sin_ref, *refs):
    dq_refs, sum_refs = refs[:members], refs[members : 2 * members]
    grad_ref, dk_ref, dv_ref = refs[2 * members :]
    member = where_ref[0]
    block_len = cos_ref.shape[0] // BLOCKS_DEV
    for step in range(BLOCKS_DEV):
        here = slice(step * block_len, (step + 1) * block_len)
        cosine = cos_ref[here, :]
        signed = sin_ref[here, :] * half_sign()
        for flip in range(members):
            lanes = head_lanes(member, flip, 1, 0)
            field = sum_refs[flip][0, here, :].astype(jnp.float32)
            dk_ref[here, lanes] = turned_back(field, cosine, signed).astype(jnp.bfloat16)
            dv_ref[here, lanes] = sum_refs[flip][1, here, :].astype(jnp.bfloat16)
            for head in range(group):
                field = dq_refs[flip][step, stacked(head, block_len), :].astype(jnp.float32)
                grad_ref[here, head_lanes(member, flip, group, head)] = turned_back(
                    field, cosine, signed
                ).astype(jnp.bfloat16)


def whole(shape):
    return pl.BlockSpec(shape, lambda *_: (0,) * len(shape))


def call(kernel, name, scalars, inputs, outputs, in_specs=None, out_specs=None, scratch=(), cost=None):
    return pl.pallas_call(
        kernel,
        grid_spec=pltpu.PrefetchScalarGridSpec(
            num_scalar_prefetch=len(scalars),
            grid=(1,),
            in_specs=in_specs or [whole(a.shape) for a in inputs],
            out_specs=out_specs or [whole(shape) for shape, _ in outputs],
            scratch_shapes=list(scratch),
        ),
        out_shape=[jax.ShapeDtypeStruct(shape, kind) for shape, kind in outputs],
        compiler_params=pltpu.CompilerParams(vmem_limit_bytes=MEMORY),
        cost_estimate=cost,
        name=name,
    )(*scalars, *inputs)


def shards(
    queries, keys, values, attn_out, out_grad, logsumexp, position_ids, block_map, span_blocks
):
    rows = queries.shape[0]
    kv_heads = keys.shape[1] // HEAD_SIZE
    group = queries.shape[1] // keys.shape[1]
    block_len = rows // BLOCKS_DEV
    layers = lax.axis_size("z")
    members = 4 if kv_heads == 4 and lax.axis_size("tp") == 2 else 1
    tp_index = lax.axis_index("tp")
    layer = lax.axis_index("z")
    in_slab = lax.axis_index("y") * 2 + lax.axis_index("core")
    device = layer * 4 + in_slab
    member = in_slab if members > 1 else jnp.zeros_like(in_slab)
    place = jnp.stack([member, tp_index, layer, jnp.full_like(layer, layers), device])
    place = place.astype(jnp.int32)
    width = group * HEAD_SIZE
    bf16, f32 = jnp.bfloat16, jnp.float32

    def flipped(array, flip):
        if flip == 0:
            return array
        return lax.ppermute(array, ("y", "core"), [(i, i ^ flip) for i in range(4)])

    def climbed(array, steps):
        route = [(i, (i + steps) % layers) for i in range(layers)]
        return lax.ppermute(array, "z", route)

    every = range(members)
    table = ((rows, HEAD_SIZE), f32)
    pair = (2, rows, HEAD_SIZE)

    inputs = [position_ids, keys, values]
    outputs = [table, table] + [(pair, bf16)] * members
    in_specs = [whole(a.shape) for a in inputs]
    if members > 1:
        other = (out_grad.shape[0], members * width)
        inputs.append(out_grad)
        in_specs.append(pl.BlockSpec(other, lambda i, where: (0, 1 - where[1])))
        outputs.append((other, bf16))
    results = call(
        functools.partial(first_kernel, members, members > 1),
        "first", [place], inputs, outputs, in_specs,
    )
    cosine, sine = results[:2]
    kv_pieces = results[2 : 2 + members]
    columns = group * block_len
    stack = (BLOCKS_DEV, columns, HEAD_SIZE)
    cosine_now = cosine
    if members > 1:
        slab = jnp.stack([flipped(kv_pieces[f], f) for f in every])
        grads_other = lax.ppermute(results[-1], "tp", [(0, 1), (1, 0)])
        far = sorted(range(1, layers), key=lambda k: abs(2 * k - layers))
        rounds = [far[: layers // 2], far[layers // 2 :] + [0]]
        slab, cosine_now = lax.optimization_barrier((slab, cosine))
        kv = {0: slab}
        for k in far:
            kv[k] = climbed(slab, k)
        kv[far[1]], grads_other = lax.optimization_barrier((kv[far[1]], grads_other))
    else:
        kv = {0: lax.all_gather(kv_pieces[0], ("z", "y", "core"), axis=0, tiled=False)}
        rounds = [[0]]
        grads_own = lax.all_to_all(out_grad, "tp", split_axis=1, concat_axis=0, tiled=True)
    q_pieces = call(
        functools.partial(query_kernel, members, group),
        "rotate", [place], [cosine_now, sine, queries], [(stack, bf16)] * members,
    )
    q_in = [flipped(q_pieces[f], f) for f in every]

    g_in = []
    for number in range(BLOCKS_DEV):

        def half_rows(i, where, number=number):
            return (block_half(members, number, where), 0)

        own_rows = pl.BlockSpec((block_len, members * width), half_rows)
        if members == 1:
            source, spec = grads_own, own_rows
        elif number == 0:
            source = out_grad
            spec = pl.BlockSpec(grads_other.shape, lambda i, where: (0, where[1]))
        else:
            source, spec = grads_other, whole(grads_other.shape)
        pieces = call(
            functools.partial(delta_kernel, members, group, number),
            "delta", [place], [attn_out, logsumexp, source],
            [((columns + STAT_ROWS, HEAD_SIZE), bf16)] * members,
            [own_rows, whole(logsumexp.shape), spec],
        )
        g_in += [flipped(pieces[f], f) for f in every]

    units = kv[0].shape[0]
    blocks = members * BLOCKS_DEV
    part = (units, 2, rows, HEAD_SIZE)
    sums = (blocks, HEAD_SIZE, columns)
    parts = {}
    carry = []
    for number, slabs in enumerate(rounds):
        tokens = len(slabs) * units * rows
        carries = number < len(rounds) - 1
        results = call(
            functools.partial(
                attend_kernel, members, group, block_len, slabs, number > 0, carries
            ),
            "attend", [place, block_map, span_blocks.reshape(-1)],
            [*[kv[k] for k in slabs], *q_in, *g_in, *carry],
            ([(sums, f32)] if carries else [(stack, bf16)] * members)
            + [(part, f32 if k == 0 and members > 1 else bf16) for k in slabs],
            scratch=[
                pltpu.VMEM((tokens, HEAD_SIZE), bf16),
                pltpu.VMEM((tokens, HEAD_SIZE), bf16),
                pltpu.VMEM((tokens // CHUNK, HEAD_SIZE, CHUNK), bf16),
                pltpu.VMEM((blocks, columns, HEAD_SIZE), bf16),
                pltpu.VMEM((blocks, columns, HEAD_SIZE), bf16),
                pltpu.VMEM((blocks, 1, columns), f32),
                pltpu.VMEM((blocks, 1, columns), f32),
                pltpu.VMEM((tokens, HEAD_SIZE), f32),
                pltpu.VMEM((tokens, HEAD_SIZE), f32),
                pltpu.VMEM((HEAD_SIZE, columns), f32),
                pltpu.VMEM((blocks, columns, HEAD_SIZE), bf16),
                pltpu.SMEM((tokens // block_len,), jnp.int32),
                pltpu.SMEM((tokens // block_len,), jnp.int32),
            ],
            cost=pl.CostEstimate(
                flops=6 * group * members * rows * tokens * HEAD_SIZE,
                bytes_accessed=6 * 1024 * 1024,
                transcendentals=group * members * rows * tokens // 2,
            ),
        )
        outs = 1 if carries else members
        carry = results[:outs]
        parts.update(zip(slabs, results[outs:]))
        if carries:
            home = {k: climbed(parts[k], layers - k) for k in slabs}
    dq_pieces = carry
    if members > 1:
        carry, home, late = lax.optimization_barrier(
            (carry, home, {k: parts[k] for k in rounds[-1]})
        )
        dq_pieces, total = carry, late.pop(0)
        home.update({k: climbed(late[k], layers - k) for k in late})
        for k in far:
            total = total + home[k].astype(f32)
        sums = [flipped(total[f].astype(bf16), f) for f in every]
    else:
        sums = [
            lax.psum_scatter(parts[0], ("z", "y", "core"), scatter_dimension=0, tiled=True)[0]
        ]
    return tuple(
        call(
            functools.partial(last_kernel, members, group),
            "last", [place],
            [cosine, sine, *[flipped(dq_pieces[f], f) for f in every], *sums],
            [(queries.shape, bf16), (keys.shape, bf16), (values.shape, bf16)],
        )
    )


def solution(mesh):
    ctx, tp = mesh.shape["ctx"], mesh.shape["tp"]
    fine = Mesh(mesh.devices.reshape(ctx // 4, 2, 2, tp), ("z", "y", "core", "tp"))
    ctx_axes = ("z", "y", "core")
    return jax.shard_map(
        shards,
        mesh=fine,
        in_specs=(
            P(ctx_axes, "tp"),
            P(ctx_axes, "tp"),
            P(ctx_axes, "tp"),
            P(ctx_axes, "tp"),
            P((*ctx_axes, "tp"), None),
            P("tp", ctx_axes),
            P(None, ctx_axes),
            P(),
            P(),
        ),
        out_specs=(P(ctx_axes, "tp"), P(ctx_axes, "tp"), P(ctx_axes, "tp")),
        check_vma=False,
    )
```

```python
import functools
import math

import jax
import jax.numpy as jnp
from jax import lax
from jax.experimental import pallas as pl
from jax.experimental.pallas import tpu as pltpu
from jax.sharding import Mesh
from jax.sharding import PartitionSpec as P

HEAD_SIZE = 128
BLOCKS_DEV = 2
THETA = 1000000.0
CHUNK = 256
WIDE = 512
STAT_ROWS = 32
SCORE_SCALE = 1.0 / math.sqrt(HEAD_SIZE)
LOG2E = math.log2(math.e)
MEMORY = 56 * 1024 * 1024


def turned_tables(ids, width):
    half = width // 2
    rows = ids.shape[1]
    pair = lax.broadcasted_iota(jnp.int32, (half, rows), 0)
    first_cut = width // 8
    second_cut = first_cut + 3 * width // 16
    inverse = jnp.exp(pair.astype(jnp.float32) * jnp.float32(-2.0 * math.log(THETA) / width))
    ids = ids.astype(jnp.float32)
    picked = jnp.where(
        pair < first_cut, ids[0:1, :], jnp.where(pair < second_cut, ids[1:2, :], ids[2:3, :])
    )
    angles = picked * inverse
    cosine = jnp.cos(angles)
    sine = jnp.sin(angles)
    return (
        jnp.concatenate([cosine, cosine], axis=0).T,
        jnp.concatenate([sine, sine], axis=0).T,
    )


def half_sign():
    lane = lax.broadcasted_iota(jnp.int32, (1, HEAD_SIZE), 1)
    return jnp.where(lane < HEAD_SIZE // 2, -1.0, 1.0).astype(jnp.float32)


def head_lanes(member, flip, heads, head):
    first = ((member ^ flip) * heads + head) * HEAD_SIZE
    return pl.ds(pl.multiple_of(first, HEAD_SIZE), HEAD_SIZE)


def first_kernel(members, with_piece, where_ref, ids_ref, k_ref, v_ref, *refs):
    refs = list(refs)
    if with_piece:
        grad_ref = refs.pop(0)
        refs.pop()[...] = grad_ref[...]
    cos_ref, sin_ref = refs.pop(0), refs.pop(0)
    member = where_ref[0]
    cosine, sine = turned_tables(ids_ref[...], HEAD_SIZE)
    cos_ref[...] = cosine
    sin_ref[...] = sine
    signed = sine * half_sign()
    for flip in range(members):
        lanes = head_lanes(member, flip, 1, 0)
        keys = k_ref[:, lanes].astype(jnp.float32)
        refs[flip][0] = (keys * cosine + pltpu.roll(keys, HEAD_SIZE // 2, 1) * signed).astype(
            jnp.bfloat16
        )
        refs[flip][1] = v_ref[:, lanes]


def stacked(head, block_len):
    return slice(head * block_len, (head + 1) * block_len)


def query_kernel(members, group, where_ref, cos_ref, sin_ref, q_ref, *out_refs):
    member = where_ref[0]
    cosine = cos_ref[...]
    signed = sin_ref[...] * half_sign()
    block_len = q_ref.shape[0] // BLOCKS_DEV
    for flip in range(members):
        for head in range(group):
            field = q_ref[:, head_lanes(member, flip, group, head)].astype(jnp.float32)
            turned = pltpu.roll(field, HEAD_SIZE // 2, 1)
            field = (field * cosine + turned * signed).astype(jnp.bfloat16)
            for step in range(BLOCKS_DEV):
                out_refs[flip][step, stacked(head, block_len), :] = field[
                    step * block_len : (step + 1) * block_len, :
                ]


def split_rows(vector):
    pieces = []
    for _ in range(3):
        addend = vector.astype(jnp.bfloat16).astype(jnp.float32)
        vector = vector - addend
        pieces += [
            addend[:, i : i + HEAD_SIZE] for i in range(0, addend.shape[1], HEAD_SIZE)
        ]
    return pieces


def joined_row(rows):
    count = rows.shape[0] // 3
    total = rows[:count] + rows[count : 2 * count] + rows[2 * count :]
    return jnp.concatenate([total[i : i + 1] for i in range(count)], axis=1)


def block_half(members, number, where):
    if members == 1:
        return number
    return where[1] if number == 0 else 1 - where[1]


def delta_kernel(members, group, number, where_ref, a_ref, l_ref, source_ref, *grad_refs):
    member = where_ref[0]
    upper = block_half(members, number, where_ref)
    block_len = a_ref.shape[0]
    columns = group * block_len
    for flip in range(members):
        products = []
        for head in range(group):
            lanes = head_lanes(member, flip, group, head)
            grad = source_ref[:, lanes]
            grad_refs[flip][stacked(head, block_len), :] = grad
            products.append(grad.astype(jnp.float32) * a_ref[:, lanes].astype(jnp.float32))
        total = jnp.sum(jnp.concatenate(products, axis=0).T, axis=0, keepdims=True)
        first = pl.multiple_of((member ^ flip) * group, group)
        lse = l_ref[pl.ds(first, group), :] * LOG2E
        pieces = split_rows(row_vector(lse, upper, block_len)) + split_rows(total)
        pieces.append(jnp.zeros((STAT_ROWS - len(pieces), HEAD_SIZE), jnp.float32))
        grad_refs[flip][columns : columns + STAT_ROWS, :] = jnp.concatenate(
            pieces, axis=0
        ).astype(jnp.bfloat16)


def row_vector(table, upper, block_len):
    group, width = table.shape
    rolled = pltpu.roll(table, block_len, 1)
    low = jnp.where(upper == 0, table, rolled)
    high = jnp.where(upper == 0, rolled, table)
    lane = lax.broadcasted_iota(jnp.int32, (1, width), 1)
    pieces = [
        jnp.where(lane < block_len, low[h : h + 1, :], high[h + 1 : h + 2, :])
        for h in range(0, group, 2)
    ]
    return jnp.concatenate(pieces, axis=1)


def attend_kernel(
    members, group, block_len, slabs, carried, carries, where_ref, map_ref, span_ref, *refs
):
    refs = list(refs)
    count = len(slabs)
    kv_refs = [refs.pop(0) for _ in range(count)]
    q_refs = [refs.pop(0) for _ in range(members)]
    g_refs = [[refs.pop(0) for _ in range(members)] for _ in range(BLOCKS_DEV)]
    in_ref = refs.pop(0) if carried else None
    dq_refs = [refs.pop(0) for _ in range(1 if carries else members)]
    part_refs = [refs.pop(0) for _ in range(count)]
    k_sort, v_sort, k_turn, q_all, g_all, l_all, d_all, dk_sum, dv_sum, dq_sum = refs[:10]
    dq_all, ranks, ordered = refs[10:]
    member, layer, layers, device = where_ref[0], where_ref[2], where_ref[3], where_ref[4]
    units = kv_refs[0].shape[0]
    spans = span_ref.shape[0] // 2
    columns = group * block_len
    blocks = count * units * BLOCKS_DEV
    complete = blocks == map_ref.shape[0]

    def sequence_block(slab, unit, step):
        if members > 1:
            owner = lax.rem(layer - slab + layers, layers) * members + (member ^ unit)
        else:
            owner = unit
        return map_ref[owner * BLOCKS_DEV + step]

    if complete:

        @pl.loop(0, blocks)
        def _(block):
            ordered[block] = block
            ranks[block] = map_ref[block]

        def blocks_before(bound):
            return bound
    else:
        present = [
            sequence_block(slab, unit, step)
            for slab in slabs
            for unit in range(units)
            for step in range(BLOCKS_DEV)
        ]

        def blocks_before(bound):
            return functools.reduce(jnp.add, [(b < bound).astype(jnp.int32) for b in present])

        for number, block in enumerate(present):
            rank = blocks_before(block)
            ranks[number] = rank
            ordered[rank] = block

    def each_block(body):
        for place in range(count):

            @pl.loop(0, units)
            def _(unit):
                for step in range(BLOCKS_DEV):
                    rank = ranks[(place * units + unit) * BLOCKS_DEV + step]
                    at = pl.multiple_of(rank * block_len, block_len)
                    body(place, unit, pl.ds(step * block_len, block_len), pl.ds(at, block_len))

    def sort(place, unit, row, to):
        k_sort[to, :] = kv_refs[place][unit, 0, row, :]
        v_sort[to, :] = kv_refs[place][unit, 1, row, :]

    each_block(sort)

    @pl.loop(0, k_turn.shape[0])
    def _(chunk):
        at = pl.multiple_of(chunk * CHUNK, CHUNK)
        k_turn[chunk] = k_sort[pl.ds(at, CHUNK), :].T
        dk_sum[pl.ds(at, CHUNK), :] = jnp.zeros((CHUNK, HEAD_SIZE), jnp.float32)
        dv_sum[pl.ds(at, CHUNK), :] = jnp.zeros((CHUNK, HEAD_SIZE), jnp.float32)

    for flip in range(members):
        for step in range(BLOCKS_DEV):
            place = flip * BLOCKS_DEV + step
            q_all[place] = q_refs[flip][step]
            place = flip * BLOCKS_DEV + block_half(members, step, where_ref)
            g_all[place] = g_refs[step][flip][:columns, :]
            stats = g_refs[step][flip][columns:, :].astype(jnp.float32)
            half = 3 * columns // HEAD_SIZE
            l_all[place] = joined_row(stats[:half])
            d_all[place] = joined_row(stats[half : 2 * half])

    lane = lax.broadcasted_iota(jnp.int32, (1, columns), 1)
    within = lax.rem(lane, block_len)
    key_row = lax.broadcasted_iota(jnp.int32, (block_len, 1), 0)
    chunk_blocks = CHUNK // block_len

    @pl.loop(0, members * BLOCKS_DEV)
    def _(place):
        flip, step = place // BLOCKS_DEV, lax.rem(place, BLOCKS_DEV)
        owner = device if members == 1 else layer * members + (member ^ flip)
        block = map_ref[owner * BLOCKS_DEV + step]
        end = jnp.int32(0)
        for span in range(spans):
            inside = (block >= span_ref[2 * span]) & (block < span_ref[2 * span + 1])
            end = jnp.where(inside, span_ref[2 * span + 1], end)
        limit = jnp.where(end > 0, end * block_len, block * block_len + within + 1)
        full = blocks_before(jnp.where(end > 0, end, block)) // chunk_blocks
        tail = blocks_before(jnp.maximum(end, block + 1)) - full * chunk_blocks
        dq_sum[...] = in_ref[place] if carried else jnp.zeros_like(dq_sum)

        def visit(chunk, size, masked):
            queries = q_all[place]
            grads = g_all[place]
            at = pl.multiple_of(chunk * CHUNK, CHUNK)
            keys = k_sort[pl.ds(at, size), :]
            values = v_sort[pl.ds(at, size), :]
            scores = lax.dot_general(
                keys, queries, (((1,), (1,)), ((), ())), preferred_element_type=jnp.float32
            )
            raised = scores * (SCORE_SCALE * LOG2E) - l_all[place]
            if masked:
                positions = jnp.concatenate(
                    [
                        key_row + ordered[chunk * chunk_blocks + i] * block_len
                        for i in range(size // block_len)
                    ],
                    axis=0,
                )
                raised = jnp.where(positions < limit, raised, -jnp.inf)
            probs = jnp.exp2(raised)
            grad_p = lax.dot_general(
                values, grads, (((1,), (1,)), ((), ())), preferred_element_type=jnp.float32
            )
            grad_s = (probs * (grad_p - d_all[place])).astype(jnp.bfloat16)
            dv_sum[pl.ds(at, size), :] += jnp.dot(
                probs.astype(jnp.bfloat16), grads, preferred_element_type=jnp.float32
            )
            dk_sum[pl.ds(at, size), :] += jnp.dot(
                grad_s, queries, preferred_element_type=jnp.float32
            )
            if size < CHUNK:
                turned = [k_turn[chunk, :, :size]]
            else:
                turned = [k_turn[chunk + i] for i in range(size // CHUNK)]
            dq_sum[...] += jnp.dot(
                jnp.concatenate(turned, axis=1), grad_s, preferred_element_type=jnp.float32
            )

        pairs = full // 2
        pl.loop(0, pairs)(lambda pair: visit(2 * pair, WIDE, False))
        pl.loop(2 * pairs, full)(lambda chunk: visit(chunk, CHUNK, False))
        short = chunk_blocks // 2
        pl.when(tail > short)(lambda: visit(full, CHUNK, True))
        pl.when((tail > 0) & (tail <= short))(lambda: visit(full, CHUNK // 2, True))

        if carries:
            dq_refs[0][place] = dq_sum[...]
        else:
            dq_all[place] = (dq_sum[...].T * SCORE_SCALE).astype(jnp.bfloat16)

    if not carries:
        for flip in range(members):
            for step in range(BLOCKS_DEV):
                dq_refs[flip][step] = dq_all[flip * BLOCKS_DEV + step]

    def unsort(place, unit, here, at):
        kind = part_refs[place].dtype
        part_refs[place][unit, 0, here, :] = (dk_sum[at, :] * SCORE_SCALE).astype(kind)
        part_refs[place][unit, 1, here, :] = dv_sum[at, :].astype(kind)

    each_block(unsort)


def turned_back(field, cosine, signed):
    return field * cosine - pltpu.roll(field, HEAD_SIZE // 2, 1) * signed


def last_kernel(members, group, where_ref, cos_ref, sin_ref, *refs):
    dq_refs, sum_refs = refs[:members], refs[members : 2 * members]
    grad_ref, dk_ref, dv_ref = refs[2 * members :]
    member = where_ref[0]
    block_len = cos_ref.shape[0] // BLOCKS_DEV
    for step in range(BLOCKS_DEV):
        here = slice(step * block_len, (step + 1) * block_len)
        cosine = cos_ref[here, :]
        signed = sin_ref[here, :] * half_sign()
        for flip in range(members):
            lanes = head_lanes(member, flip, 1, 0)
            field = sum_refs[flip][0, here, :].astype(jnp.float32)
            dk_ref[here, lanes] = turned_back(field, cosine, signed).astype(jnp.bfloat16)
            dv_ref[here, lanes] = sum_refs[flip][1, here, :].astype(jnp.bfloat16)
            for head in range(group):
                field = dq_refs[flip][step, stacked(head, block_len), :].astype(jnp.float32)
                grad_ref[here, head_lanes(member, flip, group, head)] = turned_back(
                    field, cosine, signed
                ).astype(jnp.bfloat16)


def whole(shape):
    return pl.BlockSpec(shape, lambda *_: (0,) * len(shape))


def call(kernel, name, scalars, inputs, outputs, in_specs=None, out_specs=None, scratch=(), cost=None):
    return pl.pallas_call(
        kernel,
        grid_spec=pltpu.PrefetchScalarGridSpec(
            num_scalar_prefetch=len(scalars),
            grid=(1,),
            in_specs=in_specs or [whole(a.shape) for a in inputs],
            out_specs=out_specs or [whole(shape) for shape, _ in outputs],
            scratch_shapes=list(scratch),
        ),
        out_shape=[jax.ShapeDtypeStruct(shape, kind) for shape, kind in outputs],
        compiler_params=pltpu.CompilerParams(vmem_limit_bytes=MEMORY),
        cost_estimate=cost,
        name=name,
    )(*scalars, *inputs)


def shards(
    queries, keys, values, attn_out, out_grad, logsumexp, position_ids, block_map, span_blocks
):
    rows = queries.shape[0]
    kv_heads = keys.shape[1] // HEAD_SIZE
    group = queries.shape[1] // keys.shape[1]
    block_len = rows // BLOCKS_DEV
    layers = lax.axis_size("z")
    members = 4 if kv_heads == 4 and lax.axis_size("tp") == 2 else 1
    tp_index = lax.axis_index("tp")
    layer = lax.axis_index("z")
    in_slab = lax.axis_index("y") * 2 + lax.axis_index("core")
    device = layer * 4 + in_slab
    member = in_slab if members > 1 else jnp.zeros_like(in_slab)
    place = jnp.stack([member, tp_index, layer, jnp.full_like(layer, layers), device])
    place = place.astype(jnp.int32)
    width = group * HEAD_SIZE
    bf16, f32 = jnp.bfloat16, jnp.float32

    def flipped(array, flip):
        if flip == 0:
            return array
        return lax.ppermute(array, ("y", "core"), [(i, i ^ flip) for i in range(4)])

    def climbed(array, steps):
        route = [(i, (i + steps) % layers) for i in range(layers)]
        return lax.ppermute(array, "z", route)

    every = range(members)
    table = ((rows, HEAD_SIZE), f32)
    pair = (2, rows, HEAD_SIZE)

    inputs = [position_ids, keys, values]
    outputs = [table, table] + [(pair, bf16)] * members
    in_specs = [whole(a.shape) for a in inputs]
    if members > 1:
        other = (out_grad.shape[0], members * width)
        inputs.append(out_grad)
        in_specs.append(pl.BlockSpec(other, lambda i, where: (0, 1 - where[1])))
        outputs.append((other, bf16))
    results = call(
        functools.partial(first_kernel, members, members > 1),
        "first", [place], inputs, outputs, in_specs,
    )
    cosine, sine = results[:2]
    kv_pieces = results[2 : 2 + members]
    columns = group * block_len
    stack = (BLOCKS_DEV, columns, HEAD_SIZE)
    cosine_now = cosine
    if members > 1:
        slab = jnp.stack([flipped(kv_pieces[f], f) for f in every])
        grads_other = lax.ppermute(results[-1], "tp", [(0, 1), (1, 0)])
        far = sorted(range(1, layers), key=lambda k: abs(2 * k - layers))
        rounds = [far[: layers // 2], far[layers // 2 :] + [0]]
        slab, cosine_now = lax.optimization_barrier((slab, cosine))
        kv = {0: slab}
        for k in far:
            kv[k] = climbed(slab, k)
        kv[far[1]], grads_other = lax.optimization_barrier((kv[far[1]], grads_other))
    else:
        kv = {0: lax.all_gather(kv_pieces[0], ("z", "y", "core"), axis=0, tiled=False)}
        rounds = [[0]]
        grads_own = lax.all_to_all(out_grad, "tp", split_axis=1, concat_axis=0, tiled=True)
    q_pieces = call(
        functools.partial(query_kernel, members, group),
        "rotate", [place], [cosine_now, sine, queries], [(stack, bf16)] * members,
    )
    q_in = [flipped(q_pieces[f], f) for f in every]

    g_in = []
    for number in range(BLOCKS_DEV):

        def half_rows(i, where, number=number):
            return (block_half(members, number, where), 0)

        own_rows = pl.BlockSpec((block_len, members * width), half_rows)
        if members == 1:
            source, spec = grads_own, own_rows
        elif number == 0:
            source = out_grad
            spec = pl.BlockSpec(grads_other.shape, lambda i, where: (0, where[1]))
        else:
            source, spec = grads_other, whole(grads_other.shape)
        pieces = call(
            functools.partial(delta_kernel, members, group, number),
            "delta", [place], [attn_out, logsumexp, source],
            [((columns + STAT_ROWS, HEAD_SIZE), bf16)] * members,
            [own_rows, whole(logsumexp.shape), spec],
        )
        g_in += [flipped(pieces[f], f) for f in every]

    units = kv[0].shape[0]
    blocks = members * BLOCKS_DEV
    part = (units, 2, rows, HEAD_SIZE)
    sums = (blocks, HEAD_SIZE, columns)
    parts = {}
    carry = []
    for number, slabs in enumerate(rounds):
        tokens = len(slabs) * units * rows
        carries = number < len(rounds) - 1
        results = call(
            functools.partial(
                attend_kernel, members, group, block_len, slabs, number > 0, carries
            ),
            "attend", [place, block_map, span_blocks.reshape(-1)],
            [*[kv[k] for k in slabs], *q_in, *g_in, *carry],
            ([(sums, f32)] if carries else [(stack, bf16)] * members)
            + [(part, f32 if k == 0 and members > 1 else bf16) for k in slabs],
            scratch=[
                pltpu.VMEM((tokens, HEAD_SIZE), bf16),
                pltpu.VMEM((tokens, HEAD_SIZE), bf16),
                pltpu.VMEM((tokens // CHUNK, HEAD_SIZE, CHUNK), bf16),
                pltpu.VMEM((blocks, columns, HEAD_SIZE), bf16),
                pltpu.VMEM((blocks, columns, HEAD_SIZE), bf16),
                pltpu.VMEM((blocks, 1, columns), f32),
                pltpu.VMEM((blocks, 1, columns), f32),
                pltpu.VMEM((tokens, HEAD_SIZE), f32),
                pltpu.VMEM((tokens, HEAD_SIZE), f32),
                pltpu.VMEM((HEAD_SIZE, columns), f32),
                pltpu.VMEM((blocks, columns, HEAD_SIZE), bf16),
                pltpu.SMEM((tokens // block_len,), jnp.int32),
                pltpu.SMEM((tokens // block_len,), jnp.int32),
            ],
            cost=pl.CostEstimate(
                flops=6 * group * members * rows * tokens * HEAD_SIZE,
                bytes_accessed=6 * 1024 * 1024,
                transcendentals=group * members * rows * tokens // 2,
            ),
        )
        outs = 1 if carries else members
        carry = results[:outs]
        parts.update(zip(slabs, results[outs:]))
        if carries:
            home = {k: climbed(parts[k], layers - k) for k in slabs}
    dq_pieces = carry
    if members > 1:
        carry, home, late = lax.optimization_barrier(
            (carry, home, {k: parts[k] for k in rounds[-1]})
        )
        dq_pieces, total = carry, late.pop(0)
        home.update({k: climbed(late[k], layers - k) for k in late})
        for k in far:
            total = total + home[k].astype(f32)
        sums = [flipped(total[f].astype(bf16), f) for f in every]
    else:
        sums = [
            lax.psum_scatter(parts[0], ("z", "y", "core"), scatter_dimension=0, tiled=True)[0]
        ]
    return tuple(
        call(
            functools.partial(last_kernel, members, group),
            "last", [place],
            [cosine, sine, *[flipped(dq_pieces[f], f) for f in every], *sums],
            [(queries.shape, bf16), (keys.shape, bf16), (values.shape, bf16)],
        )
    )


def solution(mesh):
    ctx, tp = mesh.shape["ctx"], mesh.shape["tp"]
    fine = Mesh(mesh.devices.reshape(ctx // 4, 2, 2, tp), ("z", "y", "core", "tp"))
    ctx_axes = ("z", "y", "core")
    return jax.shard_map(
        shards,
        mesh=fine,
        in_specs=(
            P(ctx_axes, "tp"),
            P(ctx_axes, "tp"),
            P(ctx_axes, "tp"),
            P(ctx_axes, "tp"),
            P((*ctx_axes, "tp"), None),
            P("tp", ctx_axes),
            P(None, ctx_axes),
            P(),
            P(),
        ),
        out_specs=(P(ctx_axes, "tp"), P(ctx_axes, "tp"), P(ctx_axes, "tp")),
        check_vma=False,
    )
```
